128 devices in a mesh: blk: 4 (over z), wide: 32 (over y, x, core).
Axes of the slice: x: 4, y: 4, z: 4, core: 2. Of those that a mesh axis runs over, the one named last changes fastest.
Arguments:
- feature_table: bfloat16 [262144, 1024], P('wide', 'blk'), may hold values from -6 to 6
- owner_ids: int32 [131072, 1], P('wide'), may hold values from 0 to 31; in each aligned block of 4096 rows (0 to 4095, 4096 to 8191, ...) at most 256 rows name the same one
- row_ids: int32 [131072], P('wide'), may hold values from 0 to 8191
- near_first: int32 [65536, 15], P('wide'), may hold values from 0 to 4095
- near_second: int32 [16384, 10], P('wide'), may hold values from 0 to 2047
- w_self: bfloat16 [1024, 512], P('blk'), may hold values from -0.1875 to 0.1875
- w_near: bfloat16 [1024, 512], P('blk'), may hold values from -0.1875 to 0.1875
- bias_hidden: bfloat16 [512], P('blk'), may hold values from -3 to 3
- v_self: bfloat16 [512, 512], P('blk'), may hold values from -0.25 to 0.25
- v_near: bfloat16 [512, 512], P('blk'), may hold values from -0.25 to 0.25
- cotangent: bfloat16 [16384, 512], P('wide'), may hold values from -0.046875 to 0.046875
Outputs:
- seed_out: bfloat16 [16384, 512], P('wide', 'blk')
- grad_w_self: float32 [1024, 512], P('blk')
- grad_w_near: float32 [1024, 512], P('blk')
- grad_v_self: float32 [512, 512], P('blk')
- grad_v_near: float32 [512, 512], P('blk')
The draws below stay inside these ranges and needn't reach their ends.
Inputs may be any that keep to these rules, and one draw needn't show every extreme that they name: `owner_ids`: among the 4096 frontier nodes of one index of wide, no owner is named by more than 256, a bound that some block reaches.
All inputs are finite; a program needn't handle non-finite values.
Results may differ from the reference program's by a relative error of at most 0.025.
Values may be sent and summed in bfloat16 or wider, within the bound.
No kernel may reach another device: no remote copies, remote signals or barrier semaphores. Data moves between devices by JAX's collectives and lax.ppermute only.
A program may use at most 64 MiB of HBM per device.

```python
import math
import jax
import jax.numpy as jnp
import numpy as np
from jax import lax

F = 1024
H = 512
K1 = 15
K2 = 10
B_DEV = 512
OWN_ROWS = 8192
M_DEV = 2048
R_DEV = 4096
CAP = 256
SEEDS = 16384
TARGETS = 65536
ROWS_ALL = 131072
NODES = 262144
N_BLK = 4
N_WIDE = 32


def with_ends(values, stream_key, smallest, top_value):
    longest = values.shape.index(max(values.shape))
    spots = []
    for shift in (0, 1):
        where = [jax.random.randint(jax.random.fold_in(stream_key, axis), (), 0, length) for axis, length in enumerate(values.shape)]
        where[longest] = (where[longest] + shift) % values.shape[longest]
        spots.append(tuple(where))
    return values.at[spots[0]].set(smallest).at[spots[1]].set(top_value)


def block_levels(rng, extent, cuts, smallest, high):
    loudness = 1.0
    for dim, shards_of in cuts:
        heights = jax.random.uniform(jax.random.fold_in(jax.random.fold_in(rng, 6), dim), (shards_of,), jnp.float32, smallest / len(cuts), high / len(cuts))
        loudness = loudness * jnp.repeat(jnp.exp(heights), extent[dim] // shards_of).reshape((-1,) + (1,) * (len(extent) - 1 - dim))
    return loudness


def routed_block(rng, own, number, rows, number_of, top, most, lean):
    ranking = jax.random.permutation(rng, number_of)
    crowded, common = load_shares(number_of, rows * top, most, lean, True), load_shares(number_of, rows * top, most, lean, False)
    places = jnp.arange(number_of)

    def named(lengths, turn):
        used = int((lengths > 0).sum())
        fixed = max(1, used // 4)
        shifted = fixed + (places - fixed + turn * (used - fixed)) % max(1, number_of - fixed)
        return jnp.zeros((number_of,), jnp.int32).at[ranking[jnp.where(places < fixed, places, shifted)]].set(jnp.asarray(lengths, jnp.int32))

    lengths = jnp.where(number % 4 == 0, named(crowded, number // 4), named(common, number - number // 4 - 1))
    mixed = jax.random.permutation(jax.random.fold_in(own, 3), number_of)
    donor, taker = mixed[0:number_of // 2 * 2:2], mixed[1:number_of // 2 * 2:2]
    room = jnp.minimum(lengths[donor] - 1, most - lengths[taker]) // 2
    room = jnp.where((donor == ranking[0]) | (taker == ranking[0]) | (lengths[taker] == 0), 0, jnp.maximum(room, 0))
    shifted = jax.random.randint(jax.random.fold_in(own, 4), (number_of // 2,), 0, 1 << 20) % (room + 1)
    lengths = lengths.at[donor].add(-shifted).at[taker].add(shifted)
    items = jnp.searchsorted(jnp.cumsum(lengths), jnp.arange(rows * top), side="right").astype(jnp.int32)
    table = items.reshape(top, rows).T
    table = table[jax.random.permutation(jax.random.fold_in(own, 1), rows)]
    turn = jax.random.randint(jax.random.fold_in(own, 2), (rows, 1), 0, top)
    return jnp.take_along_axis(table, (jnp.arange(top)[None, :] + turn) % top, axis=1)


def load_shares(number_of, total, most, skew, full):
    portions = [(1 << 20) // math.isqrt(rank ** skew) + 1 for rank in range(1, number_of + 1)]
    largest = most if full else min(most, max(-(-total // number_of), total * portions[0] // sum(portions)))
    least = 1 if total - largest >= number_of - 1 else 0
    holding, surplus = [largest] + [least] * (number_of - 1), total - largest - least * (number_of - 1)
    while surplus > 0:
        movable = [i for i in range(1, number_of) if holding[i] < largest] or [i for i in range(1, number_of) if holding[i] < most]
        mass, remaining = sum([portions[i] for i in movable]), surplus
        for i in movable:
            more = min(most - holding[i], max(1, remaining * portions[i] // mass), surplus)
            holding[i] = holding[i] + more
            surplus = surplus - more
    return np.array(holding)


def scatter_about(own_key, shape, scale, limit, cuts=(), kind=jnp.bfloat16):
    gain = block_levels(own_key, shape, cuts, -0.22, 0.18) if cuts else 1.0
    drawn = jax.random.normal(own_key, shape, jnp.float32) * scale * gain
    return jnp.minimum(jnp.maximum(drawn, -limit), limit).astype(kind)


def setup_inputs(seed: int = 0) -> dict:
    keys = jax.random.split(jax.random.key(seed), 12)
    feature_table = scatter_about(keys[0], (NODES, F), 1.0, 6.0, ((0, 32), (1, 4)))
    owner_ids_keys = jax.random.split(jax.random.fold_in(keys[1], 1), ROWS_ALL // R_DEV)
    owner_ids_turns = jax.random.permutation(jax.random.fold_in(keys[1], 3), ROWS_ALL // R_DEV)
    owner_ids = jax.vmap(lambda own, number: routed_block(jax.random.fold_in(keys[1], 2), own, number, R_DEV, N_WIDE, 1, CAP, 2))(owner_ids_keys, owner_ids_turns).reshape((ROWS_ALL, 1))
    row_ids = with_ends(jax.random.randint(keys[2], (ROWS_ALL,), 0, OWN_ROWS), jax.random.fold_in(keys[2], 1), 0, OWN_ROWS - 1).astype(jnp.int32)
    near_first = with_ends(jax.random.randint(keys[3], (TARGETS, K1), 0, R_DEV), jax.random.fold_in(keys[3], 1), 0, R_DEV - 1).astype(jnp.int32)
    near_second = with_ends(jax.random.randint(keys[4], (SEEDS, K2), 0, M_DEV), jax.random.fold_in(keys[4], 1), 0, M_DEV - 1).astype(jnp.int32)
    w_self = scatter_about(keys[5], (F, H), F ** -0.5, 0.1875, ((0, 4),))
    w_near = scatter_about(keys[6], (F, H), F ** -0.5, 0.1875, ((0, 4),))
    bias_hidden = scatter_about(keys[7], (H,), 0.5, 3.0, ((0, 4),))
    v_self = scatter_about(keys[8], (H, H), H ** -0.5, 0.25, ((0, 4),))
    v_near = scatter_about(keys[9], (H, H), H ** -0.5, 0.25, ((0, 4),))
    cotangent = scatter_about(keys[10], (SEEDS, H), (1.0 / SEEDS ** 0.5), 0.046875, ((0, 32),))
    return dict(feature_table=feature_table, owner_ids=owner_ids, row_ids=row_ids, near_first=near_first, near_second=near_second, w_self=w_self, w_near=w_near, bias_hidden=bias_hidden, v_self=v_self, v_near=v_near, cotangent=cotangent)


def neighbour_mean(source, lists, list_width):
    running_sum = jnp.zeros((lists.shape[0], source.shape[1]), jnp.float32)
    for step in range(list_width):
        running_sum = running_sum + jnp.take(source, lists[:, step], axis=0).astype(jnp.float32)
    return (running_sum / list_width).astype(jnp.bfloat16)


def silu_slope(active):
    sigmoid_value = 1.0 / (1.0 + jnp.exp(-active))
    return sigmoid_value * (1.0 + active * (1.0 - sigmoid_value))


def reference(feature_table, owner_ids, row_ids, near_first, near_second, w_self, w_near, bias_hidden, v_self, v_near, cotangent):
    quarter = F // N_BLK
    owner_groups = owner_ids.reshape(N_WIDE, R_DEV)
    row_groups = row_ids.reshape(N_WIDE, R_DEV)
    first_groups = near_first.reshape(N_WIDE, M_DEV, K1)
    second_groups = near_second.reshape(N_WIDE, B_DEV, K2)
    grad_groups = cotangent.reshape(N_WIDE, B_DEV, H)

    def one_group(per_group):
        owners, local_rows, first_lists, second_lists, grad_out = per_group
        global_row = (owners * OWN_ROWS + local_rows).astype(jnp.int32)
        frontier = jnp.take(feature_table, global_row, axis=0)
        self_rows = frontier[:M_DEV]
        near_mean = neighbour_mean(frontier, first_lists, K1)
        pre_act = jnp.zeros((M_DEV, H), jnp.float32)
        for part_index in range(N_BLK):
            low = part_index * quarter
            high = low + quarter
            part_sum = jnp.dot(self_rows[:, low:high], w_self[low:high], preferred_element_type=jnp.float32)
            part_sum = part_sum + jnp.dot(near_mean[:, low:high], w_near[low:high], preferred_element_type=jnp.float32)
            rounded = lax.optimization_barrier(part_sum.astype(jnp.bfloat16))
            pre_act = pre_act + rounded.astype(jnp.float32)
        active = pre_act + bias_hidden.astype(jnp.float32)
        hidden = jax.nn.silu(active).astype(jnp.bfloat16)
        second_mean = neighbour_mean(hidden, second_lists, K2)
        seed_hidden = hidden[:B_DEV]
        seed_out = (jnp.dot(seed_hidden, v_self, preferred_element_type=jnp.float32)
                    + jnp.dot(second_mean, v_near, preferred_element_type=jnp.float32)).astype(jnp.bfloat16)
        grad_vs = jnp.dot(seed_hidden.T, grad_out, preferred_element_type=jnp.float32)
        grad_vn = jnp.dot(second_mean.T, grad_out, preferred_element_type=jnp.float32)
        d_self = jnp.dot(grad_out, v_self.T, preferred_element_type=jnp.float32)
        d_mean = jnp.dot(grad_out, v_near.T, preferred_element_type=jnp.float32) / K2
        d_hidden = jnp.zeros((M_DEV, H), jnp.float32).at[:B_DEV].add(d_self)
        for step in range(K2):
            d_hidden = d_hidden.at[second_lists[:, step]].add(d_mean)
        slope = (d_hidden * silu_slope(active)).astype(jnp.bfloat16)
        grad_ws = jnp.dot(self_rows.T, slope, preferred_element_type=jnp.float32)
        grad_wn = jnp.dot(near_mean.T, slope, preferred_element_type=jnp.float32)
        return seed_out, grad_ws, grad_wn, grad_vs, grad_vn

    outs_all = lax.map(one_group, (owner_groups, row_groups, first_groups, second_groups, grad_groups))
    seed_out = outs_all[0].reshape(SEEDS, H)
    return (seed_out, jnp.sum(outs_all[1], axis=0), jnp.sum(outs_all[2], axis=0),
            jnp.sum(outs_all[3], axis=0), jnp.sum(outs_all[4], axis=0))
```

```python
import functools

import jax
import jax.numpy as jnp
from jax import lax
from jax.experimental import pallas as pl
from jax.experimental.pallas import tpu as pltpu
from jax.sharding import PartitionSpec as P

BF = jnp.bfloat16
F32 = jnp.float32
NT = (((1,), (1,)), ((), ()))
TN = (((0,), (0,)), ((), ()))


def iota(shape, axis):
    return lax.broadcasted_iota(jnp.int32, shape, axis)


def one_hot(hit):
    return jnp.where(hit, 1.0, 0.0).astype(BF)


def chunk(index, size):
    return pl.ds(pl.multiple_of(index * size, size), size)


def request_kernel(own_ref, row_ref, req_ref, flat_ref, hot, picked, spots):
    peers, cap = req_ref.shape
    lines, width = own_ref.shape
    names = iota((peers, width), 0)
    for r in range(lines):
        hot[r * peers:(r + 1) * peers, :] = one_hot(own_ref[r:r + 1, :] == names)
    before = one_hot(iota((width, 2 * width), 0) <= iota((width, 2 * width), 1))
    counted = jnp.dot(hot[...], before, preferred_element_type=F32)
    base = jnp.full((peers, width), -1.0, F32)
    slots = iota((cap, width), 0)
    for r in range(lines):
        here = counted[r * peers:(r + 1) * peers]
        hit = own_ref[r:r + 1, :] == names
        slot = jnp.sum(jnp.where(hit, here[:, :width] + base, 0.0), axis=0, keepdims=True)
        slot = slot.astype(jnp.int32)
        base = base + here[:, width:]
        flat_ref[r:r + 1, :] = own_ref[r:r + 1, :] * cap + slot
        cols = slice(r * width, (r + 1) * width)
        row = row_ref[r:r + 1, :]
        upper = jnp.broadcast_to((row >> 6).astype(F32), (peers, width))
        lower = jnp.broadcast_to((row & 63).astype(F32), (peers, width))
        picked[:peers, cols] = jnp.where(hit, upper, 0.0).astype(BF)
        picked[peers:, cols] = jnp.where(hit, lower, 0.0).astype(BF)
        spots[:, cols] = one_hot(slots == slot)
    found = lax.dot_general(picked[...], spots[...], NT, preferred_element_type=F32)
    req_ref[...] = (found[:peers] * 64.0 + found[peers:]).astype(jnp.int32)


def request_table(owners, rows, peers, cap):
    lines, width = owners.shape
    return pl.pallas_call(
        request_kernel,
        out_shape=(
            jax.ShapeDtypeStruct((peers, cap), jnp.int32),
            jax.ShapeDtypeStruct(owners.shape, jnp.int32),
        ),
        scratch_shapes=[
            pltpu.VMEM((lines * peers, width), BF),
            pltpu.VMEM((2 * peers, lines * width), BF),
            pltpu.VMEM((cap, lines * width), BF),
        ],
        compiler_params=pltpu.CompilerParams(vmem_limit_bytes=40 << 20),
        name="request_table",
    )(owners, rows)


def count_kernel(idx_ref, out_ref):
    groups = idx_ref.shape[0]
    uppers = out_ref.shape[0]
    target = iota((1, 256), 1) >> 4
    rows_upper = iota((uppers * 16, 256), 0)
    rows_lower = iota((256, 256), 0)

    def group(g, carry):
        value = idx_ref[pl.ds(g, 1), :]
        code = jnp.where(value >= 0, (value >> 8) * 16 + target, -1)
        found = lax.dot_general(
            one_hot(rows_upper == code),
            one_hot(rows_lower == (value & 255)),
            NT,
            preferred_element_type=F32,
        ).astype(BF)
        for u in range(uppers):
            out_ref[u, chunk(g, 16), :] = found[u * 16:(u + 1) * 16, :]
        return carry

    lax.fori_loop(0, groups, group, 0, unroll=4)


def neighbour_counts(lists, sources, block_groups=16):
    targets, places = lists.shape
    uppers = sources // 256
    padded = jnp.pad(lists, ((0, 0), (0, 16 - places)), constant_values=-1)
    return pl.pallas_call(
        count_kernel,
        grid=(targets // 16 // block_groups,),
        in_specs=[pl.BlockSpec((block_groups, 256), lambda i: (i, 0))],
        out_specs=pl.BlockSpec((uppers, block_groups * 16, 256), lambda i: (0, i, 0)),
        out_shape=jax.ShapeDtypeStruct((uppers, targets, 256), BF),
        compiler_params=pltpu.CompilerParams(vmem_limit_bytes=40 << 20),
        cost_estimate=pl.CostEstimate(
            flops=512 * targets * sources,
            bytes_accessed=2 * targets * sources,
            transcendentals=0,
        ),
        name="neighbour_counts",
    )(padded.reshape(targets // 16, 256))


def widen(source_ref, low, high):
    half = low.shape[1]

    def some(i, carry):
        part = chunk(i, 256)
        low[part, :] = source_ref[part, :half].astype(F32)
        high[part, :] = source_ref[part, half:].astype(F32)
        return carry

    lax.fori_loop(0, source_ref.shape[0] // 256, some, 0)


def pick_rows(idx_ref, first, count, low, high, out_ref):
    half = low.shape[1]
    line = iota((8, half), 0)

    def some(i, carry):
        begin = pl.multiple_of(i * 16, 16)
        lows, highs = [], []
        for h in range(2):
            for j in range(8):
                row = idx_ref[first + begin + h * 8 + j]
                new_low = jnp.broadcast_to(low[pl.ds(row, 1), :], (8, half))
                new_high = jnp.broadcast_to(high[pl.ds(row, 1), :], (8, half))
                if j == 0:
                    got_low, got_high = new_low, new_high
                else:
                    got_low = jnp.where(line == j, new_low, got_low)
                    got_high = jnp.where(line == j, new_high, got_high)
            lows.append(got_low)
            highs.append(got_high)
        out_ref[pl.ds(begin, 16), :half] = jnp.concatenate(lows, axis=0).astype(BF)
        out_ref[pl.ds(begin, 16), half:] = jnp.concatenate(highs, axis=0).astype(BF)
        return carry

    lax.fori_loop(0, count // 16, some, 0, unroll=4)


def gather_kernel(idx_ref, table_ref, out_ref, low, high):
    step = pl.program_id(0)
    rows = out_ref.shape[0]

    @pl.when(step == 0)
    def _():
        widen(table_ref, low, high)

    pick_rows(idx_ref, step * rows, rows, low, high, out_ref)


def gather_rows(table, idx, rows=1024):
    total = idx.shape[0]
    own_rows, width = table.shape
    return pl.pallas_call(
        gather_kernel,
        grid_spec=pltpu.PrefetchScalarGridSpec(
            num_scalar_prefetch=1,
            grid=(total // rows,),
            in_specs=[pl.BlockSpec(table.shape, lambda i, s: (0, 0))],
            out_specs=pl.BlockSpec((rows, width), lambda i, s: (i, 0)),
            scratch_shapes=[pltpu.VMEM((own_rows, width // 2), F32)] * 2,
        ),
        out_shape=jax.ShapeDtypeStruct((total, width), BF),
        compiler_params=pltpu.CompilerParams(vmem_limit_bytes=40 << 20),
        name="gather_rows",
    )(idx, table)


def layer_kernel(list_width, idx_ref, spot_ref, arrived_ref, counts_ref, ws_ref, wn_ref,
                 parts_ref, both_ref, low, high, frontier):
    step = pl.program_id(0)
    block = counts_ref.shape[1]
    uppers = counts_ref.shape[0]
    width = arrived_ref.shape[1]

    @pl.when(step == 0)
    def _():
        widen(arrived_ref, low, high)
        pick_rows(idx_ref, 0, frontier.shape[0], low, high, frontier)

    total = jnp.zeros((block, width), F32)
    for u in range(uppers):
        total = total + jnp.dot(
            counts_ref[u], frontier[u * 256:(u + 1) * 256, :], preferred_element_type=F32
        )
    mean = (total / list_width).astype(BF)
    here = chunk(step, block)
    own = frontier[here, :]
    both_ref[here, :width] = own
    both_ref[here, width:] = mean
    quarters, _, share = parts_ref.shape
    for d in range(quarters):
        cols = chunk(lax.rem(spot_ref[0] + d, quarters), share)
        part = jnp.dot(own, ws_ref[:, cols], preferred_element_type=F32)
        part = part + jnp.dot(mean, wn_ref[:, cols], preferred_element_type=F32)
        parts_ref[d, here, :] = part.astype(BF)


def first_layer(idx, spot, arrived, counts, w_self, w_near, list_width, quarters, block=256):
    uppers, targets, lower = counts.shape
    slots, width = arrived.shape
    hidden = w_self.shape[1]

    def full(shape):
        return pl.BlockSpec(shape, lambda i, *s: (0,) * len(shape))

    return pl.pallas_call(
        functools.partial(layer_kernel, list_width),
        grid_spec=pltpu.PrefetchScalarGridSpec(
            num_scalar_prefetch=2,
            grid=(targets // block,),
            in_specs=[
                full(arrived.shape),
                pl.BlockSpec((uppers, block, lower), lambda i, *s: (0, i, 0)),
                full(w_self.shape),
                full(w_near.shape),
            ],
            out_specs=[
                full((quarters, targets, hidden // quarters)),
                full((targets, 2 * width)),
            ],
            scratch_shapes=[pltpu.VMEM((slots, width // 2), F32)] * 2
            + [pltpu.VMEM((idx.shape[0], width), BF)],
        ),
        out_shape=[
            jax.ShapeDtypeStruct((quarters, targets, hidden // quarters), BF),
            jax.ShapeDtypeStruct((targets, 2 * width), BF),
        ],
        compiler_params=pltpu.CompilerParams(vmem_limit_bytes=56 << 20),
        name="first_layer",
    )(idx, spot, arrived, counts, w_self, w_near)


def finish_kernel(spot_ref, sums_ref, ws_ref, wn_ref, vs_ref, vn_ref):
    quarters = sums_ref.shape[0] // 2
    feats, share = ws_ref.shape[0], vs_ref.shape[0]
    for d in range(quarters):
        cols = chunk(lax.rem(spot_ref[0] + d, quarters), share)
        ws_ref[:, cols] = sums_ref[d, :feats, :].astype(F32)
        wn_ref[:, cols] = sums_ref[d, feats:, :].astype(F32)
    for c in range(quarters):
        cols = slice(c * share, (c + 1) * share)
        vs_ref[:, cols] = sums_ref[quarters + c, :share, :].astype(F32)
        vn_ref[:, cols] = sums_ref[quarters + c, share:2 * share, :].astype(F32)


def body(
    feature_table,
    owner_ids,
    row_ids,
    near_first,
    near_second,
    w_self,
    w_near,
    bias_hidden,
    v_self,
    v_near,
    cotangent,
):
    peers = lax.axis_size("wide")
    quarters = lax.axis_size("blk")
    z = lax.axis_index("blk")
    spot = jnp.full((1,), z, jnp.int32)
    frontier_count = row_ids.shape[0]
    cap = 2 * frontier_count // peers
    targets, first_width = near_first.shape
    seeds, second_width = near_second.shape
    feats, hidden_units = w_self.shape
    share = hidden_units // quarters
    half = targets // 2

    def shift(value, by):
        return lax.ppermute(value, "blk", [(i, (i + by) % quarters) for i in range(quarters)])

    with jax.named_scope("requests"):
        requests, flat = request_table(
            owner_ids.reshape(frontier_count // 128, 128),
            row_ids.reshape(frontier_count // 128, 128),
            peers,
            cap,
        )
        wanted = lax.all_to_all(requests, "wide", split_axis=0, concat_axis=0, tiled=True)
    with jax.named_scope("rows"):
        found = gather_rows(feature_table, wanted.reshape(-1))
        arrived = lax.all_to_all(
            found.reshape(peers, cap, feats), "wide", split_axis=0, concat_axis=0, tiled=True
        ).reshape(peers * cap, feats)
    with jax.named_scope("beside_rows"):
        counts_first = neighbour_counts(near_first, frontier_count)
        counts_second = neighbour_counts(near_second, targets)
        d_self = lax.dot_general(cotangent, v_self, NT, preferred_element_type=F32)
        d_mean = lax.dot_general(cotangent, v_near, NT, preferred_element_type=F32) / second_width
        d_upper = d_mean.astype(BF)
        d_lower = (d_mean - d_upper.astype(F32)).astype(BF)
        spread = lax.dot_general(
            counts_second,
            jnp.concatenate([d_upper, d_lower], axis=1),
            (((1,), (0,)), ((), ())),
            preferred_element_type=F32,
        ).reshape(targets, 2 * share)
        d_hidden = spread[:, :share] + spread[:, share:]
        d_hidden = d_hidden + jnp.pad(d_self, ((0, targets - seeds), (0, 0)))
    with jax.named_scope("first_layer"):
        parts, both = first_layer(
            flat.reshape(-1), spot, arrived, counts_first, w_self, w_near, first_width, quarters
        )
    with jax.named_scope("pre_act_exchange"):
        far_up = shift(parts[2, :half], 1)
        far_down = shift(parts[2, half:], -1)
        up_own = shift(parts[1, half:], 1)
        down_own = shift(parts[3, :half], -1)
        up_sum = shift((parts[1, :half].astype(F32) + far_up.astype(F32)).astype(BF), 1)
        down_sum = shift((parts[3, half:].astype(F32) + far_down.astype(F32)).astype(BF), -1)
        first_half = parts[0, :half].astype(F32) + down_own.astype(F32) + up_sum.astype(F32)
        last_half = parts[0, half:].astype(F32) + up_own.astype(F32) + down_sum.astype(F32)
        active = jnp.concatenate([first_half, last_half]) + bias_hidden.astype(F32)
    with jax.named_scope("slope"):
        sigmoid = 1.0 / (1.0 + jnp.exp(-active))
        hidden = (active / (1.0 + jnp.exp(-active))).astype(BF)
        slope = (d_hidden * (sigmoid * (1.0 + active * (1.0 - sigmoid)))).astype(BF)
    with jax.named_scope("slope_exchange"):
        from_down = (shift(slope[:half], 1), shift(slope[half:], 1))
        from_up = (shift(slope[:half], -1), shift(slope[half:], -1))
        from_far = (shift(from_down[0], 1), shift(from_up[1], -1))

    with jax.named_scope("second_layer"):
        seed_hidden = hidden[:seeds]
        second_mean = (
            lax.dot_general(
                counts_second,
                hidden.reshape(counts_second.shape[0], 256, share),
                (((0, 2), (0, 1)), ((), ())),
                preferred_element_type=F32,
            )
            / second_width
        ).astype(BF)
        grad_v = jnp.concatenate(
            [
                lax.dot_general(seed_hidden, cotangent, TN, preferred_element_type=F32),
                lax.dot_general(second_mean, cotangent, TN, preferred_element_type=F32),
            ]
        ).astype(BF)
        partial_out = jnp.dot(seed_hidden, v_self, preferred_element_type=F32) + jnp.dot(
            second_mean, v_near, preferred_element_type=F32
        )

        def out_part(d):
            return lax.dynamic_slice_in_dim(partial_out, (z + d) % quarters * share, share, 1)

        seed_out = out_part(0)
        for d in range(1, quarters):
            seed_out = seed_out + shift(out_part(d).astype(BF), d).astype(F32)
        seed_out = seed_out.astype(BF)

    def grad_w(slope_part):
        return lax.dot_general(both, slope_part, TN, preferred_element_type=F32).astype(BF)

    def scatter_sum(values):
        rows = values.shape[0] // peers
        got = lax.all_to_all(
            values.reshape(peers, rows, share), "wide", split_axis=0, concat_axis=0, tiled=True
        )
        return jnp.sum(got.astype(F32), axis=0).astype(BF)

    with jax.named_scope("gradients"):
        grad_v_cols = [grad_v[:, c * share:(c + 1) * share] for c in range(quarters)]
        early = scatter_sum(jnp.concatenate(grad_v_cols + [grad_w(slope)]))
        late = scatter_sum(
            jnp.concatenate(
                [
                    grad_w(jnp.concatenate(from_up)),
                    grad_w(jnp.concatenate(from_far)),
                    grad_w(jnp.concatenate(from_down)),
                ]
            )
        )
        sums = lax.all_gather(jnp.concatenate([early, late]), "wide", axis=0)
        early_rows = early.shape[0]
        sums_early = sums[:, :early_rows].reshape(-1, share)
        sums_late = sums[:, early_rows:].reshape(-1, share)
        v_rows = 2 * share * quarters
        tall = 2 * feats
        sums_v = sums_early[:v_rows].reshape(quarters, 2 * share, share)
        sums_v = jnp.pad(sums_v, ((0, 0), (0, tall - 2 * share), (0, 0)))
        sums_all = jnp.concatenate(
            [
                sums_early[v_rows:].reshape(1, tall, share),
                sums_late.reshape(quarters - 1, tall, share),
                sums_v,
            ]
        )
        grads = pl.pallas_call(
            finish_kernel,
            in_specs=[
                pl.BlockSpec(memory_space=pltpu.SMEM),
                pl.BlockSpec(memory_space=pltpu.VMEM),
            ],
            out_specs=[pl.BlockSpec(memory_space=pltpu.VMEM)] * 4,
            out_shape=[jax.ShapeDtypeStruct((feats, hidden_units), F32)] * 2
            + [jax.ShapeDtypeStruct((share, hidden_units), F32)] * 2,
            compiler_params=pltpu.CompilerParams(vmem_limit_bytes=16 << 20),
            name="finish",
        )(spot, sums_all)
    return (seed_out, *grads)


def solution(mesh):
    placed = (
        P("wide", "blk"),
        P("wide", None),
        P("wide"),
        P("wide", None),
        P("wide", None),
        P("blk", None),
        P("blk", None),
        P("blk"),
        P("blk", None),
        P("blk", None),
        P("wide", None),
    )
    return jax.shard_map(
        body,
        mesh=mesh,
        in_specs=placed,
        out_specs=(
            P("wide", "blk"),
            P("blk", None),
            P("blk", None),
            P("blk", None),
            P("blk", None),
        ),
        check_vma=False,
    )
```

```python
import functools

import jax
import jax.numpy as jnp
from jax import lax
from jax.experimental import pallas as pl
from jax.experimental.pallas import tpu as pltpu
from jax.sharding import PartitionSpec as P

BF = jnp.bfloat16
F32 = jnp.float32
NT = (((1,), (1,)), ((), ()))
TN = (((0,), (0,)), ((), ()))


def iota(shape, axis):
    return lax.broadcasted_iota(jnp.int32, shape, axis)


def one_hot(hit):
    return jnp.where(hit, 1.0, 0.0).astype(BF)


def chunk(index, size):
    return pl.ds(pl.multiple_of(index * size, size), size)


def request_kernel(own_hbm, row_hbm, req_ref, flat_ref, own_ref, row_ref, hot, picked, spots, sems):
    peers, _, cap = req_ref.shape
    lines, width = own_ref.shape
    copies = [
        pltpu.make_async_copy(own_hbm, own_ref, sems.at[0]),
        pltpu.make_async_copy(row_hbm, row_ref, sems.at[1]),
    ]
    for copy in copies:
        copy.start()
    for copy in copies:
        copy.wait()
    names = iota((peers, width), 0)
    for r in range(lines):
        hot[r * peers:(r + 1) * peers, :] = one_hot(own_ref[r:r + 1, :] == names)
    before = one_hot(iota((width, 2 * width), 0) <= iota((width, 2 * width), 1))
    counted = jnp.dot(hot[...], before, preferred_element_type=F32)
    base = jnp.full((peers, width), -1.0, F32)
    slots = iota((cap, width), 0)
    for r in range(lines):
        here = counted[r * peers:(r + 1) * peers]
        hit = own_ref[r:r + 1, :] == names
        slot = jnp.sum(jnp.where(hit, here[:, :width] + base, 0.0), axis=0, keepdims=True)
        slot = slot.astype(jnp.int32)
        base = base + here[:, width:]
        flat_ref[r:r + 1, :] = own_ref[r:r + 1, :] * cap + slot
        cols = slice(r * width, (r + 1) * width)
        row = row_ref[r:r + 1, :]
        upper = jnp.broadcast_to((row >> 6).astype(F32), (peers, width))
        lower = jnp.broadcast_to((row & 63).astype(F32), (peers, width))
        picked[:peers, cols] = jnp.where(hit, upper, 0.0).astype(BF)
        picked[peers:, cols] = jnp.where(hit, lower, 0.0).astype(BF)
        spots[:, cols] = one_hot(slots == slot)
    found = lax.dot_general(picked[...], spots[...], NT, preferred_element_type=F32)
    req_ref[:, 0, :] = (found[:peers] * 64.0 + found[peers:]).astype(jnp.int32)


def request_table(owners, rows, peers, cap):
    lines, width = owners.shape
    return pl.pallas_call(
        request_kernel,
        out_shape=(
            jax.ShapeDtypeStruct((peers, 1, cap), jnp.int32),
            jax.ShapeDtypeStruct(owners.shape, jnp.int32),
        ),
        in_specs=[pl.BlockSpec(memory_space=pltpu.HBM)] * 2,
        scratch_shapes=[
            pltpu.VMEM(owners.shape, jnp.int32),
            pltpu.VMEM(owners.shape, jnp.int32),
            pltpu.VMEM((lines * peers, width), BF),
            pltpu.VMEM((2 * peers, lines * width), BF),
            pltpu.VMEM((cap, lines * width), BF),
            pltpu.SemaphoreType.DMA((2,)),
        ],
        compiler_params=pltpu.CompilerParams(vmem_limit_bytes=62 << 20),
        name="request_table",
    )(owners, rows)


def count_kernel(idx_ref, out_ref):
    groups = idx_ref.shape[0]
    uppers = out_ref.shape[1] // 256
    target = iota((1, 256), 1) >> 4
    rows_upper = iota((uppers * 16, 256), 0)
    rows_lower = iota((256, 256), 0)

    def group(g, carry):
        value = idx_ref[pl.ds(g, 1), :]
        code = jnp.where(value >= 0, (value >> 8) * 16 + target, -1)
        found = lax.dot_general(
            one_hot(rows_upper == code),
            one_hot(rows_lower == (value & 255)),
            NT,
            preferred_element_type=F32,
        ).astype(BF)
        for u in range(uppers):
            out_ref[chunk(g, 16), u * 256:(u + 1) * 256] = found[u * 16:(u + 1) * 16, :]
        return carry

    lax.fori_loop(0, groups, group, 0, unroll=4)


def neighbour_counts(lists, sources, block_groups=16):
    targets, places = lists.shape
    padded = jnp.pad(lists, ((0, 0), (0, 16 - places)), constant_values=-1)
    return pl.pallas_call(
        count_kernel,
        grid=(targets // 16 // block_groups,),
        in_specs=[pl.BlockSpec((block_groups, 256), lambda i: (i, 0))],
        out_specs=pl.BlockSpec((block_groups * 16, sources), lambda i: (i, 0)),
        out_shape=jax.ShapeDtypeStruct((targets, sources), BF),
        compiler_params=pltpu.CompilerParams(vmem_limit_bytes=40 << 20),
        cost_estimate=pl.CostEstimate(
            flops=512 * targets * sources,
            bytes_accessed=2 * targets * sources,
            transcendentals=0,
        ),
        name="neighbour_counts",
    )(padded.reshape(targets // 16, 256))


def pick_rows(idx_ref, first, count, low, high, out_ref):
    half = low.shape[1]
    line = iota((8, half), 0)

    def some(i, carry):
        begin = pl.multiple_of(i * 16, 16)
        lows, highs = [], []
        for h in range(2):
            for j in range(8):
                row = idx_ref[first + begin + h * 8 + j]
                new_low = jnp.broadcast_to(low[pl.ds(row, 1), :], (8, half))
                new_high = jnp.broadcast_to(high[pl.ds(row, 1), :], (8, half))
                if j == 0:
                    got_low, got_high = new_low, new_high
                else:
                    got_low = jnp.where(line == j, new_low, got_low)
                    got_high = jnp.where(line == j, new_high, got_high)
            lows.append(got_low)
            highs.append(got_high)
        out_ref[pl.ds(begin, 16), :half] = jnp.concatenate(lows, axis=0).astype(BF)
        out_ref[pl.ds(begin, 16), half:] = jnp.concatenate(highs, axis=0).astype(BF)
        return carry

    lax.fori_loop(0, count // 16, some, 0, unroll=4)


def piece_copies(source_ref, held, sems):
    rows = held.shape[0] // sems.shape[0]
    return [
        pltpu.make_async_copy(
            source_ref.at[pl.ds(p * rows, rows), :], held.at[pl.ds(p * rows, rows), :], sems.at[p]
        )
        for p in range(sems.shape[0])
    ]


def widen(held, low, high, copies):
    rows = held.shape[0] // len(copies)
    half = low.shape[1]
    for p, copy in enumerate(copies):
        copy.wait()

        def some(i, carry):
            part = pl.ds(pl.multiple_of(p * rows + i * 128, 128), 128)
            low[part, :] = held[part, :half].astype(F32)
            high[part, :] = held[part, half:].astype(F32)
            return carry

        lax.fori_loop(0, rows // 128, some, 0, unroll=2)


def gather_kernel(idx_ref, table_ref, out_ref, held, low, high, sems):
    step = pl.program_id(0)
    rows = out_ref.shape[0]

    @pl.when(step == 0)
    def _():
        copies = piece_copies(table_ref, held, sems)
        for copy in copies:
            copy.start()
        widen(held, low, high, copies)

    pick_rows(idx_ref, step * rows, rows, low, high, out_ref)


def gather_rows(table, idx, rows=1024):
    total = idx.shape[0]
    own_rows, width = table.shape
    return pl.pallas_call(
        gather_kernel,
        grid_spec=pltpu.PrefetchScalarGridSpec(
            num_scalar_prefetch=1,
            grid=(total // rows,),
            in_specs=[pl.BlockSpec(memory_space=pltpu.HBM)],
            out_specs=pl.BlockSpec((rows, width), lambda i, s: (i, 0)),
            scratch_shapes=[
                pltpu.VMEM((own_rows, width), BF),
                pltpu.VMEM((own_rows, width // 2), F32),
                pltpu.VMEM((own_rows, width // 2), F32),
                pltpu.SemaphoreType.DMA((8,)),
            ],
        ),
        out_shape=pltpu.HBM((total, width), BF),
        compiler_params=pltpu.CompilerParams(vmem_limit_bytes=62 << 20),
        name="gather_rows",
    )(idx, table)


def layer_kernel(list_width, idx_ref, spot_ref, arrived_ref, counts_ref, ws_ref, wn_ref,
                 *refs):
    part_refs, (both_ref, held, low, high, frontier, counts, sems, count_sems) = refs[:-8], refs[-8:]
    step = pl.program_id(0)
    block = both_ref.shape[0]
    width = held.shape[1]

    def count_copy(b):
        return pltpu.make_async_copy(
            counts_ref.at[pl.ds(b * block, block), :],
            counts.at[pl.ds(b * block, block), :],
            count_sems.at[b],
        )

    @pl.when(step == 0)
    def _():
        copies = piece_copies(arrived_ref, held, sems)
        for copy in copies:
            copy.start()
        for b in range(counts.shape[0] // block):
            count_copy(b).start()
        widen(held, low, high, copies)
        pick_rows(idx_ref, 0, frontier.shape[0], low, high, frontier)

    count_copy(step).wait()
    here = chunk(step, block)
    total = jnp.dot(counts[here, :], frontier[...], preferred_element_type=F32)
    own = frontier[here, :]
    mean = (total / list_width).astype(BF)
    both_ref[:, :width] = own
    both_ref[:, width:] = mean
    share = part_refs[0].shape[1]
    quarters = ws_ref.shape[1] // share
    made = jnp.dot(own, ws_ref[...], preferred_element_type=F32)
    made = (made + jnp.dot(mean, wn_ref[...], preferred_element_type=F32)).astype(BF)
    for q in range(quarters):
        d = lax.rem(q + quarters - spot_ref[0], quarters)
        for e in range(quarters):
            for half in range(2):
                @pl.when((d == e) & (step // (pl.num_programs(0) // 2) == half))
                def _():
                    part_refs[2 * e + half][...] = made[:, q * share:(q + 1) * share]


def first_layer(idx, spot, arrived, counts, w_self, w_near, list_width, quarters, block=1024):
    targets, positions = counts.shape
    slots, width = arrived.shape
    share = w_self.shape[1] // quarters
    steps = targets // block
    middle = steps // 2

    def full(shape):
        return pl.BlockSpec(shape, lambda i, *s: (0, 0))

    halves = [
        pl.BlockSpec((block, share), lambda i, *s: (jnp.minimum(i, middle - 1), 0)),
        pl.BlockSpec((block, share), lambda i, *s: (jnp.maximum(i - middle, 0), 0)),
    ]
    return pl.pallas_call(
        functools.partial(layer_kernel, list_width),
        grid_spec=pltpu.PrefetchScalarGridSpec(
            num_scalar_prefetch=2,
            grid=(steps,),
            in_specs=[
                pl.BlockSpec(memory_space=pltpu.HBM),
                pl.BlockSpec(memory_space=pltpu.HBM),
                full(w_self.shape),
                full(w_near.shape),
            ],
            out_specs=halves * quarters + [pl.BlockSpec((block, 2 * width), lambda i, *s: (i, 0))],
            scratch_shapes=[
                pltpu.VMEM((slots, width), BF),
                pltpu.VMEM((slots, width // 2), F32),
                pltpu.VMEM((slots, width // 2), F32),
                pltpu.VMEM((positions, width), BF),
                pltpu.VMEM((targets, positions), BF),
                pltpu.SemaphoreType.DMA((8,)),
                pltpu.SemaphoreType.DMA((steps,)),
            ],
        ),
        out_shape=[jax.ShapeDtypeStruct((targets // 2, share), BF)] * (2 * quarters)
        + [jax.ShapeDtypeStruct((targets, 2 * width), BF)],
        compiler_params=pltpu.CompilerParams(vmem_limit_bytes=62 << 20),
        name="first_layer",
    )(idx, spot, arrived, counts, w_self, w_near)


def slope_kernel(part0, up, down, far, bias_ref, d_ref, hidden_ref, slope_ref):
    active = part0[...].astype(F32) + up[...].astype(F32) + down[...].astype(F32) + far[...].astype(F32)
    active = active + bias_ref[...].astype(F32)
    below = 1.0 + jnp.exp(-active)
    sigmoid = 1.0 / below
    hidden_ref[...] = (active / below).astype(BF)
    slope_ref[...] = (d_ref[...] * (sigmoid * (1.0 + active * (1.0 - sigmoid)))).astype(BF)


def hidden_and_slope(part0, up, down, far, bias, d_hidden, first, block=512):
    rows, share = part0.shape
    place = pl.BlockSpec((block, share), lambda i: (i, 0))
    return pl.pallas_call(
        slope_kernel,
        grid=(rows // block,),
        in_specs=[place] * 4
        + [
            pl.BlockSpec((1, share), lambda i: (0, 0)),
            pl.BlockSpec((block, share), lambda i: (i + first // block, 0)),
        ],
        out_specs=[place, place],
        out_shape=[jax.ShapeDtypeStruct((rows, share), BF)] * 2,
        compiler_params=pltpu.CompilerParams(vmem_limit_bytes=16 << 20),
        name="hidden_and_slope",
    )(part0, up, down, far, bias, d_hidden)


def finish_kernel(spot_ref, mine_ref, other_ref, ws_ref, wn_ref, vs_ref, vn_ref):
    peers, shard, share = mine_ref.shape
    feats = ws_ref.shape[0]
    some = feats // peers
    order = (0, 1, 3, 2)
    v_rows = shard - some * len(order)
    front = spot_ref[1] == 0

    def halves(first, count):
        part = slice(first, first + count)
        mine = mine_ref[:, part, :].astype(F32).reshape(peers * count, share)
        other = other_ref[:, part, :].astype(F32).reshape(peers * count, share)
        return jnp.where(front, mine, other), jnp.where(front, other, mine)

    for place, d in enumerate(order):
        cols = chunk(lax.rem(spot_ref[0] + d, len(order)), share)
        ws_ref[:, cols], wn_ref[:, cols] = halves(v_rows + place * some, some)
    for half, block in enumerate(halves(0, v_rows)):
        for e in range(len(order) // 2):
            cols = slice((2 * half + e) * share, (2 * half + e + 1) * share)
            vs_ref[:, cols] = block[2 * e * share:(2 * e + 1) * share]
            vn_ref[:, cols] = block[(2 * e + 1) * share:(2 * e + 2) * share]


def body(
    feature_table,
    owner_ids,
    row_ids,
    near_first,
    near_second,
    w_self,
    w_near,
    bias_hidden,
    v_self,
    v_near,
    cotangent,
):
    peers = lax.axis_size("wide")
    quarters = lax.axis_size("blk")
    z = lax.axis_index("blk")
    core = lax.axis_index("wide") % 2
    frontier_count = row_ids.shape[0]
    cap = 2 * frontier_count // peers
    targets, first_width = near_first.shape
    seeds, second_width = near_second.shape
    feats, hidden_units = w_self.shape
    share = hidden_units // quarters

    def shift(value, by):
        return lax.ppermute(value, "blk", [(i, (i + by) % quarters) for i in range(quarters)])

    def exchange(value):
        return lax.all_to_all(value, "wide", split_axis=0, concat_axis=0, tiled=True)

    with jax.named_scope("requests"):
        requests, flat = request_table(
            owner_ids.reshape(frontier_count // 128, 128),
            row_ids.reshape(frontier_count // 128, 128),
            peers,
            cap,
        )
        wanted = exchange(requests).reshape(-1)
        flat = flat.reshape(-1)
    with jax.named_scope("rows"):
        found = gather_rows(feature_table, wanted)
        arrived = exchange(found.reshape(peers, cap, feats)).reshape(peers * cap, feats)
    with jax.named_scope("beside_rows"):
        counts_first = neighbour_counts(near_first, frontier_count)
        counts_second = neighbour_counts(near_second, targets)
        d_self = lax.dot_general(cotangent, v_self, NT, preferred_element_type=F32)
        d_mean = lax.dot_general(cotangent, v_near, NT, preferred_element_type=F32) / second_width
        d_upper = d_mean.astype(BF)
        d_lower = (d_mean - d_upper.astype(F32)).astype(BF)
        spread = lax.dot_general(
            counts_second,
            jnp.concatenate([d_upper, d_lower], axis=1),
            TN,
            preferred_element_type=F32,
        )
        d_hidden = spread[:, :share] + spread[:, share:]
        d_hidden = d_hidden + jnp.pad(d_self, ((0, targets - seeds), (0, 0)))
        arrived, counts_first, counts_second, d_hidden = lax.optimization_barrier(
            (arrived, counts_first, counts_second, d_hidden)
        )
    with jax.named_scope("first_layer"):
        *parts, both = first_layer(
            flat,
            jnp.full((1,), z, jnp.int32),
            arrived,
            counts_first,
            w_self,
            w_near,
            first_width,
            quarters,
        )
    with jax.named_scope("pre_act_exchange"):
        hiddens, slopes = [], []
        for half in range(2):
            far = shift(parts[2 * 2 + half], 2)
            up = shift(parts[2 * 1 + half], 1)
            down = shift(parts[2 * 3 + half], -1)
            hidden, slope = hidden_and_slope(
                parts[half], up, down, far, bias_hidden.reshape(1, share), d_hidden, half * targets // 2
            )
            hiddens.append(hidden)
            slopes.append(slope)
    with jax.named_scope("slope_exchange"):
        from_far = jnp.concatenate([shift(slope, 2) for slope in slopes])
        from_down = jnp.concatenate([shift(slope, 1) for slope in slopes])
        from_up = jnp.concatenate([shift(slope, -1) for slope in slopes])

    def grad_w(slope_part):
        return lax.dot_general(both, slope_part, TN, preferred_element_type=F32).astype(BF)

    def shards(values):
        rows = values.shape[0] // peers
        split = values.reshape(2, peers // 2, rows, share)
        return split.transpose(1, 0, 2, 3).reshape(peers, rows, share)

    def scatter_sum(values):
        return jnp.sum(exchange(values).astype(F32), axis=0).astype(BF)

    with jax.named_scope("second_layer"):
        hidden = jnp.concatenate(hiddens)
        seed_hidden = hidden[:seeds]
        second_mean = (
            jnp.dot(counts_second, hidden, preferred_element_type=F32) / second_width
        ).astype(BF)
        grad_v = jnp.concatenate(
            [
                lax.dot_general(seed_hidden, cotangent, TN, preferred_element_type=F32),
                lax.dot_general(second_mean, cotangent, TN, preferred_element_type=F32),
            ]
        ).astype(BF)
        grad_v = jnp.concatenate([grad_v[:, c * share:(c + 1) * share] for c in range(quarters)])
        partial_out = jnp.dot(seed_hidden, v_self, preferred_element_type=F32) + jnp.dot(
            second_mean, v_near, preferred_element_type=F32
        )

        def out_part(d):
            return lax.dynamic_slice_in_dim(partial_out, (z + d) % quarters * share, share, 1)

        outs = [shift(out_part(d).astype(BF), d) for d in range(1, quarters)]
    with jax.named_scope("gradients"):
        early = scatter_sum(
            jnp.concatenate([shards(grad_v), shards(grad_w(jnp.concatenate(slopes)))], axis=1)
        )
        near_two = grad_w(jnp.concatenate([from_up, from_down], axis=1))
        late = scatter_sum(
            jnp.concatenate(
                [shards(near_two[:, :share]), shards(near_two[:, share:]), shards(grad_w(from_far))], axis=1
            )
        )
        sums, *outs = lax.optimization_barrier((jnp.concatenate([early, late]), *outs))
        seed_out = out_part(0)
        for part in outs:
            seed_out = seed_out + part.astype(F32)
        seed_out = seed_out.astype(BF)
        chips = peers // 2
        mine = lax.all_to_all(
            jnp.broadcast_to(sums, (chips, *sums.shape)),
            "wide",
            split_axis=0,
            concat_axis=0,
            axis_index_groups=[list(range(c, peers, 2)) for c in range(2)],
            tiled=True,
        )
        other = lax.ppermute(mine, "wide", [(i, i ^ 1) for i in range(peers)])
        grads = pl.pallas_call(
            finish_kernel,
            in_specs=[pl.BlockSpec(memory_space=pltpu.SMEM)] + [pl.BlockSpec(memory_space=pltpu.VMEM)] * 2,
            out_specs=[pl.BlockSpec(memory_space=pltpu.VMEM)] * 4,
            out_shape=[jax.ShapeDtypeStruct((feats, hidden_units), F32)] * 2
            + [jax.ShapeDtypeStruct((share, hidden_units), F32)] * 2,
            compiler_params=pltpu.CompilerParams(vmem_limit_bytes=16 << 20),
            name="finish",
        )(jnp.stack([z, core]).astype(jnp.int32), mine, other)
    return (seed_out, *grads)


def solution(mesh):
    placed = (
        P("wide", "blk"),
        P("wide", None),
        P("wide"),
        P("wide", None),
        P("wide", None),
        P("blk", None),
        P("blk", None),
        P("blk"),
        P("blk", None),
        P("blk", None),
        P("wide", None),
    )
    return jax.shard_map(
        body,
        mesh=mesh,
        in_specs=placed,
        out_specs=(
            P("wide", "blk"),
            P("blk", None),
            P("blk", None),
            P("blk", None),
            P("blk", None),
        ),
        check_vma=False,
    )
```

```python
import functools

import jax
import jax.numpy as jnp
from jax import lax
from jax.experimental import pallas as pl
from jax.experimental.pallas import tpu as pltpu
from jax.sharding import PartitionSpec as P

BF = jnp.bfloat16
F32 = jnp.float32
NT = (((1,), (1,)), ((), ()))
TN = (((0,), (0,)), ((), ()))


def iota(shape, axis):
    return lax.broadcasted_iota(jnp.int32, shape, axis)


def one_hot(hit):
    return jnp.where(hit, 1.0, 0.0).astype(BF)


def chunk(index, size):
    return pl.ds(pl.multiple_of(index * size, size), size)


def request_kernel(own_hbm, row_hbm, req_ref, flat_ref, own_ref, row_ref, hot, picked, spots, sems):
    peers, _, cap = req_ref.shape
    lines, width = own_ref.shape
    copies = [
        pltpu.make_async_copy(own_hbm, own_ref, sems.at[0]),
        pltpu.make_async_copy(row_hbm, row_ref, sems.at[1]),
    ]
    for copy in copies:
        copy.start()
    for copy in copies:
        copy.wait()
    names = iota((peers, width), 0)
    for r in range(lines):
        hot[r * peers:(r + 1) * peers, :] = one_hot(own_ref[r:r + 1, :] == names)
    before = one_hot(iota((width, 2 * width), 0) <= iota((width, 2 * width), 1))
    counted = jnp.dot(hot[...], before, preferred_element_type=F32)
    base = jnp.full((peers, width), -1.0, F32)
    slots = iota((cap, width), 0)
    for r in range(lines):
        here = counted[r * peers:(r + 1) * peers]
        hit = own_ref[r:r + 1, :] == names
        slot = jnp.sum(jnp.where(hit, here[:, :width] + base, 0.0), axis=0, keepdims=True)
        slot = slot.astype(jnp.int32)
        base = base + here[:, width:]
        flat_ref[r:r + 1, :] = own_ref[r:r + 1, :] * cap + slot
        cols = slice(r * width, (r + 1) * width)
        row = row_ref[r:r + 1, :]
        upper = jnp.broadcast_to((row >> 6).astype(F32), (peers, width))
        lower = jnp.broadcast_to((row & 63).astype(F32), (peers, width))
        picked[:peers, cols] = jnp.where(hit, upper, 0.0).astype(BF)
        picked[peers:, cols] = jnp.where(hit, lower, 0.0).astype(BF)
        spots[:, cols] = one_hot(slots == slot)
    found = lax.dot_general(picked[...], spots[...], NT, preferred_element_type=F32)
    req_ref[:, 0, :] = (found[:peers] * 64.0 + found[peers:]).astype(jnp.int32)


def request_table(owners, rows, peers, cap):
    lines, width = owners.shape
    return pl.pallas_call(
        request_kernel,
        out_shape=(
            jax.ShapeDtypeStruct((peers, 1, cap), jnp.int32),
            jax.ShapeDtypeStruct(owners.shape, jnp.int32),
        ),
        in_specs=[pl.BlockSpec(memory_space=pltpu.HBM)] * 2,
        scratch_shapes=[
            pltpu.VMEM(owners.shape, jnp.int32),
            pltpu.VMEM(owners.shape, jnp.int32),
            pltpu.VMEM((lines * peers, width), BF),
            pltpu.VMEM((2 * peers, lines * width), BF),
            pltpu.VMEM((cap, lines * width), BF),
            pltpu.SemaphoreType.DMA((2,)),
        ],
        compiler_params=pltpu.CompilerParams(vmem_limit_bytes=62 << 20),
        name="request_table",
    )(owners, rows)


def count_kernel(idx_ref, out_ref):
    groups = idx_ref.shape[0]
    uppers = out_ref.shape[1] // 256
    target = iota((1, 256), 1) >> 4
    rows_upper = iota((uppers * 16, 256), 0)
    rows_lower = iota((256, 256), 0)

    def group(g, carry):
        value = idx_ref[pl.ds(g, 1), :]
        code = jnp.where(value >= 0, (value >> 8) * 16 + target, -1)
        found = lax.dot_general(
            one_hot(rows_upper == code),
            one_hot(rows_lower == (value & 255)),
            NT,
            preferred_element_type=F32,
        ).astype(BF)
        for u in range(uppers):
            out_ref[chunk(g, 16), u * 256:(u + 1) * 256] = found[u * 16:(u + 1) * 16, :]
        return carry

    lax.fori_loop(0, groups, group, 0, unroll=4)


def neighbour_counts(lists, sources, block_groups=16):
    targets, places = lists.shape
    padded = jnp.pad(lists, ((0, 0), (0, 16 - places)), constant_values=-1)
    return pl.pallas_call(
        count_kernel,
        grid=(targets // 16 // block_groups,),
        in_specs=[pl.BlockSpec((block_groups, 256), lambda i: (i, 0))],
        out_specs=pl.BlockSpec((block_groups * 16, sources), lambda i: (i, 0)),
        out_shape=jax.ShapeDtypeStruct((targets, sources), BF),
        compiler_params=pltpu.CompilerParams(vmem_limit_bytes=40 << 20),
        cost_estimate=pl.CostEstimate(
            flops=512 * targets * sources,
            bytes_accessed=2 * targets * sources,
            transcendentals=0,
        ),
        name="neighbour_counts",
    )(padded.reshape(targets // 16, 256))


def pick_rows(idx_ref, first, count, low, high, out_ref):
    half = low.shape[1]
    line = iota((8, half), 0)

    def some(i, carry):
        begin = pl.multiple_of(i * 16, 16)
        lows, highs = [], []
        for h in range(2):
            for j in range(8):
                row = idx_ref[first + begin + h * 8 + j]
                new_low = jnp.broadcast_to(low[pl.ds(row, 1), :], (8, half))
                new_high = jnp.broadcast_to(high[pl.ds(row, 1), :], (8, half))
                if j == 0:
                    got_low, got_high = new_low, new_high
                else:
                    got_low = jnp.where(line == j, new_low, got_low)
                    got_high = jnp.where(line == j, new_high, got_high)
            lows.append(got_low)
            highs.append(got_high)
        out_ref[pl.ds(begin, 16), :half] = jnp.concatenate(lows, axis=0).astype(BF)
        out_ref[pl.ds(begin, 16), half:] = jnp.concatenate(highs, axis=0).astype(BF)
        return carry

    lax.fori_loop(0, count // 16, some, 0, unroll=4)


def piece_copies(source_ref, held, sems):
    rows = held.shape[0] // sems.shape[0]
    return [
        pltpu.make_async_copy(
            source_ref.at[pl.ds(p * rows, rows), :], held.at[pl.ds(p * rows, rows), :], sems.at[p]
        )
        for p in range(sems.shape[0])
    ]


def widen(held, low, high, copies):
    rows = held.shape[0] // len(copies)
    half = low.shape[1]
    for p, copy in enumerate(copies):
        copy.wait()

        def some(i, carry):
            part = pl.ds(pl.multiple_of(p * rows + i * 128, 128), 128)
            low[part, :] = held[part, :half].astype(F32)
            high[part, :] = held[part, half:].astype(F32)
            return carry

        lax.fori_loop(0, rows // 128, some, 0, unroll=2)


def gather_kernel(idx_ref, table_ref, out_ref, held, low, high, sems):
    step = pl.program_id(0)
    rows = out_ref.shape[0]

    @pl.when(step == 0)
    def _():
        copies = piece_copies(table_ref, held, sems)
        for copy in copies:
            copy.start()
        widen(held, low, high, copies)

    pick_rows(idx_ref, step * rows, rows, low, high, out_ref)


def gather_rows(table, idx, rows=1024):
    total = idx.shape[0]
    own_rows, width = table.shape
    return pl.pallas_call(
        gather_kernel,
        grid_spec=pltpu.PrefetchScalarGridSpec(
            num_scalar_prefetch=1,
            grid=(total // rows,),
            in_specs=[pl.BlockSpec(memory_space=pltpu.HBM)],
            out_specs=pl.BlockSpec((rows, width), lambda i, s: (i, 0)),
            scratch_shapes=[
                pltpu.VMEM((own_rows, width), BF),
                pltpu.VMEM((own_rows, width // 2), F32),
                pltpu.VMEM((own_rows, width // 2), F32),
                pltpu.SemaphoreType.DMA((8,)),
            ],
        ),
        out_shape=pltpu.HBM((total, width), BF),
        compiler_params=pltpu.CompilerParams(vmem_limit_bytes=62 << 20),
        name="gather_rows",
    )(idx, table)


def layer_kernel(list_width, idx_ref, spot_ref, arrived_ref, counts_ref, ws_ref, wn_ref,
                 *refs):
    part_refs, (both_ref, held, low, high, frontier, counts, sems, count_sems) = refs[:-8], refs[-8:]
    step = pl.program_id(0)
    block = both_ref.shape[0]
    width = held.shape[1]

    def count_copy(b):
        return pltpu.make_async_copy(
            counts_ref.at[pl.ds(b * block, block), :],
            counts.at[pl.ds(b * block, block), :],
            count_sems.at[b],
        )

    @pl.when(step == 0)
    def _():
        copies = piece_copies(arrived_ref, held, sems)
        for copy in copies:
            copy.start()
        for b in range(counts.shape[0] // block):
            count_copy(b).start()
        widen(held, low, high, copies)
        pick_rows(idx_ref, 0, frontier.shape[0], low, high, frontier)

    count_copy(step).wait()
    here = chunk(step, block)
    total = jnp.dot(counts[here, :], frontier[...], preferred_element_type=F32)
    own = frontier[here, :]
    mean = (total / list_width).astype(BF)
    both_ref[:, :width] = own
    both_ref[:, width:] = mean
    share = part_refs[0].shape[1]
    quarters = ws_ref.shape[1] // share
    made = jnp.dot(own, ws_ref[...], preferred_element_type=F32)
    made = (made + jnp.dot(mean, wn_ref[...], preferred_element_type=F32)).astype(BF)
    for q in range(quarters):
        d = lax.rem(q + quarters - spot_ref[0], quarters)
        for e in range(quarters):
            for half in range(2):
                @pl.when((d == e) & (step // (pl.num_programs(0) // 2) == half))
                def _():
                    part_refs[2 * e + half][...] = made[:, q * share:(q + 1) * share]


def first_layer(idx, spot, arrived, counts, w_self, w_near, list_width, quarters, block=1024):
    targets, positions = counts.shape
    slots, width = arrived.shape
    share = w_self.shape[1] // quarters
    steps = targets // block
    middle = steps // 2

    def full(shape):
        return pl.BlockSpec(shape, lambda i, *s: (0, 0))

    halves = [
        pl.BlockSpec((block, share), lambda i, *s: (jnp.minimum(i, middle - 1), 0)),
        pl.BlockSpec((block, share), lambda i, *s: (jnp.maximum(i - middle, 0), 0)),
    ]
    return pl.pallas_call(
        functools.partial(layer_kernel, list_width),
        grid_spec=pltpu.PrefetchScalarGridSpec(
            num_scalar_prefetch=2,
            grid=(steps,),
            in_specs=[
                pl.BlockSpec(memory_space=pltpu.HBM),
                pl.BlockSpec(memory_space=pltpu.HBM),
                full(w_self.shape),
                full(w_near.shape),
            ],
            out_specs=halves * quarters + [pl.BlockSpec((block, 2 * width), lambda i, *s: (i, 0))],
            scratch_shapes=[
                pltpu.VMEM((slots, width), BF),
                pltpu.VMEM((slots, width // 2), F32),
                pltpu.VMEM((slots, width // 2), F32),
                pltpu.VMEM((positions, width), BF),
                pltpu.VMEM((targets, positions), BF),
                pltpu.SemaphoreType.DMA((8,)),
                pltpu.SemaphoreType.DMA((steps,)),
            ],
        ),
        out_shape=[jax.ShapeDtypeStruct((targets // 2, share), BF)] * (2 * quarters)
        + [jax.ShapeDtypeStruct((targets, 2 * width), BF)],
        compiler_params=pltpu.CompilerParams(vmem_limit_bytes=62 << 20),
        name="first_layer",
    )(idx, spot, arrived, counts, w_self, w_near)


def slope_kernel(part0, up, down, bias_ref, d_ref, hidden_ref, slope_ref):
    active = part0[...].astype(F32) + up[...].astype(F32) + down[...].astype(F32)
    active = active + bias_ref[...].astype(F32)
    below = 1.0 + jnp.exp(-active)
    sigmoid = 1.0 / below
    hidden_ref[...] = (active / below).astype(BF)
    slope_ref[...] = (d_ref[...] * (sigmoid * (1.0 + active * (1.0 - sigmoid)))).astype(BF)


def hidden_and_slope(part0, up, down, bias, d_hidden, first, block=512):
    rows, share = part0.shape
    place = pl.BlockSpec((block, share), lambda i: (i, 0))
    return pl.pallas_call(
        slope_kernel,
        grid=(rows // block,),
        in_specs=[place] * 3
        + [
            pl.BlockSpec((1, share), lambda i: (0, 0)),
            pl.BlockSpec((block, share), lambda i: (i + first // block, 0)),
        ],
        out_specs=[place, place],
        out_shape=[jax.ShapeDtypeStruct((rows, share), BF)] * 2,
        compiler_params=pltpu.CompilerParams(vmem_limit_bytes=16 << 20),
        name="hidden_and_slope",
    )(part0, up, down, bias, d_hidden)


def pack_kernel(*refs):
    *value_refs, out_ref = refs
    peers, _, share = out_ref.shape
    chips = peers // 2
    first = 0
    for ref in value_refs:
        rows = ref.shape[0] // peers
        for c in range(ref.shape[1] // share):
            for peer in range(peers):
                shard = peer % 2 * chips + peer // 2
                out_ref[peer, first:first + rows, :] = ref[shard * rows:(shard + 1) * rows, c * share:(c + 1) * share]
            first += rows


def pack_shards(values, peers, share):
    rows = sum(v.size for v in values) // (peers * share)
    return pl.pallas_call(
        pack_kernel,
        in_specs=[pl.BlockSpec(memory_space=pltpu.VMEM)] * len(values),
        out_specs=pl.BlockSpec(memory_space=pltpu.VMEM),
        out_shape=jax.ShapeDtypeStruct((peers, rows, share), BF),
        compiler_params=pltpu.CompilerParams(vmem_limit_bytes=16 << 20),
        name="pack_shards",
    )(*values)


def finish_kernel(spot_ref, mine_ref, other_ref, ws_ref, wn_ref, vs_ref, vn_ref):
    peers, shard, share = mine_ref.shape
    feats = ws_ref.shape[0]
    some = feats // peers
    order = (0, 1, 3, 2)
    v_rows = shard - some * len(order)
    front = spot_ref[1] == 0

    def halves(first, count):
        part = slice(first, first + count)
        mine = mine_ref[:, part, :].astype(F32).reshape(peers * count, share)
        other = other_ref[:, part, :].astype(F32).reshape(peers * count, share)
        return jnp.where(front, mine, other), jnp.where(front, other, mine)

    for place, d in enumerate(order):
        cols = chunk(lax.rem(spot_ref[0] + d, len(order)), share)
        ws_ref[:, cols], wn_ref[:, cols] = halves(v_rows + place * some, some)
    for half, block in enumerate(halves(0, v_rows)):
        for e in range(len(order) // 2):
            cols = slice((2 * half + e) * share, (2 * half + e + 1) * share)
            vs_ref[:, cols] = block[2 * e * share:(2 * e + 1) * share]
            vn_ref[:, cols] = block[(2 * e + 1) * share:(2 * e + 2) * share]


def body(
    feature_table,
    owner_ids,
    row_ids,
    near_first,
    near_second,
    w_self,
    w_near,
    bias_hidden,
    v_self,
    v_near,
    cotangent,
):
    peers = lax.axis_size("wide")
    quarters = lax.axis_size("blk")
    z = lax.axis_index("blk")
    core = lax.axis_index("wide") % 2
    frontier_count = row_ids.shape[0]
    cap = 2 * frontier_count // peers
    targets, first_width = near_first.shape
    seeds, second_width = near_second.shape
    feats, hidden_units = w_self.shape
    share = hidden_units // quarters

    def shift(value, by):
        return lax.ppermute(value, "blk", [(i, (i + by) % quarters) for i in range(quarters)])

    def exchange(value):
        return lax.all_to_all(value, "wide", split_axis=0, concat_axis=0, tiled=True)

    with jax.named_scope("requests"):
        requests, flat = request_table(
            owner_ids.reshape(frontier_count // 128, 128),
            row_ids.reshape(frontier_count // 128, 128),
            peers,
            cap,
        )
        wanted = exchange(requests).reshape(-1)
        flat = flat.reshape(-1)
    with jax.named_scope("rows"):
        found = gather_rows(feature_table, wanted)
        arrived = exchange(found.reshape(peers, cap, feats)).reshape(peers * cap, feats)
    with jax.named_scope("beside_rows"):
        counts_first = neighbour_counts(near_first, frontier_count)
        counts_second = neighbour_counts(near_second, targets)
        d_self = lax.dot_general(cotangent, v_self, NT, preferred_element_type=F32)
        d_mean = lax.dot_general(cotangent, v_near, NT, preferred_element_type=F32) / second_width
        d_upper = d_mean.astype(BF)
        d_lower = (d_mean - d_upper.astype(F32)).astype(BF)
        spread = lax.dot_general(
            counts_second,
            jnp.concatenate([d_upper, d_lower], axis=1),
            TN,
            preferred_element_type=F32,
        )
        d_hidden = spread[:, :share] + spread[:, share:]
        d_hidden = d_hidden + jnp.pad(d_self, ((0, targets - seeds), (0, 0)))
        arrived, counts_first, counts_second, d_hidden = lax.optimization_barrier(
            (arrived, counts_first, counts_second, d_hidden)
        )
    with jax.named_scope("first_layer"):
        *parts, both = first_layer(
            flat,
            jnp.full((1,), z, jnp.int32),
            arrived,
            counts_first,
            w_self,
            w_near,
            first_width,
            quarters,
        )
    def added(left, right):
        return (left.astype(F32) + right.astype(F32)).astype(BF)

    with jax.named_scope("pre_act_exchange"):
        own, above, far, below = [parts[2 * d:2 * d + 2] for d in range(quarters)]
        passing_up = shift(far[0], 1)
        passing_down = shift(far[1], -1)
        down_0 = shift(below[0], -1)
        up_1 = shift(above[1], 1)
        up_0 = shift(added(above[0], passing_up), 1)
        down_1 = shift(added(below[1], passing_down), -1)
        hiddens, slopes = [], []
        for half, (up, down) in enumerate([(up_0, down_0), (up_1, down_1)]):
            hidden, slope = hidden_and_slope(
                own[half], up, down, bias_hidden.reshape(1, share), d_hidden, half * targets // 2
            )
            hiddens.append(hidden)
            slopes.append(slope)
    with jax.named_scope("slope_exchange"):
        from_down = [shift(slope, 1) for slope in slopes]
        from_up = [shift(slope, -1) for slope in slopes]
        from_far = [shift(from_down[0], 1), shift(from_up[1], -1)]
        from_down, from_up, from_far = [jnp.concatenate(v) for v in (from_down, from_up, from_far)]

    def grad_w(slope_part):
        return lax.dot_general(both, slope_part, TN, preferred_element_type=F32).astype(BF)

    def scatter_sum(values):
        return jnp.sum(exchange(values).astype(F32), axis=0).astype(BF)

    with jax.named_scope("second_layer"):
        hidden = jnp.concatenate(hiddens)
        seed_hidden = hidden[:seeds]
        second_mean = (
            jnp.dot(counts_second, hidden, preferred_element_type=F32) / second_width
        ).astype(BF)
        grad_v = jnp.concatenate(
            [
                lax.dot_general(seed_hidden, cotangent, TN, preferred_element_type=F32),
                lax.dot_general(second_mean, cotangent, TN, preferred_element_type=F32),
            ]
        ).astype(BF)
        grad_v = jnp.concatenate([grad_v[:, c * share:(c + 1) * share] for c in range(quarters)])
        partial_out = jnp.dot(seed_hidden, v_self, preferred_element_type=F32) + jnp.dot(
            second_mean, v_near, preferred_element_type=F32
        )

        def out_part(d):
            return lax.dynamic_slice_in_dim(partial_out, (z + d) % quarters * share, share, 1)

        outs = [shift(out_part(d).astype(BF), d) for d in range(1, quarters)]
    with jax.named_scope("gradients"):
        near_two = grad_w(jnp.concatenate([from_up, from_down], axis=1))
        packed = pack_shards(
            [grad_v, grad_w(jnp.concatenate(slopes)), near_two, grad_w(from_far)], peers, share
        )
        sums = scatter_sum(packed)
        sums, *outs = lax.optimization_barrier((sums, *outs))
        seed_out = out_part(0)
        for part in outs:
            seed_out = seed_out + part.astype(F32)
        seed_out = seed_out.astype(BF)
        sums, seed_out = lax.optimization_barrier((sums, seed_out))
        chips = peers // 2
        mine = lax.all_to_all(
            jnp.broadcast_to(sums, (chips, *sums.shape)),
            "wide",
            split_axis=0,
            concat_axis=0,
            axis_index_groups=[list(range(c, peers, 2)) for c in range(2)],
            tiled=True,
        )
        other = lax.ppermute(mine, "wide", [(i, i ^ 1) for i in range(peers)])
        grads = pl.pallas_call(
            finish_kernel,
            in_specs=[pl.BlockSpec(memory_space=pltpu.SMEM)] + [pl.BlockSpec(memory_space=pltpu.VMEM)] * 2,
            out_specs=[pl.BlockSpec(memory_space=pltpu.VMEM)] * 4,
            out_shape=[jax.ShapeDtypeStruct((feats, hidden_units), F32)] * 2
            + [jax.ShapeDtypeStruct((share, hidden_units), F32)] * 2,
            compiler_params=pltpu.CompilerParams(vmem_limit_bytes=16 << 20),
            name="finish",
        )(jnp.stack([z, core]).astype(jnp.int32), mine, other)
    return (seed_out, *grads)


def solution(mesh):
    placed = (
        P("wide", "blk"),
        P("wide", None),
        P("wide"),
        P("wide", None),
        P("wide", None),
        P("blk", None),
        P("blk", None),
        P("blk"),
        P("blk", None),
        P("blk", None),
        P("wide", None),
    )
    return jax.shard_map(
        body,
        mesh=mesh,
        in_specs=placed,
        out_specs=(
            P("wide", "blk"),
            P("blk", None),
            P("blk", None),
            P("blk", None),
            P("blk", None),
        ),
        check_vma=False,
    )
```

```python
import functools

import jax
import jax.numpy as jnp
from jax import lax
from jax.experimental import pallas as pl
from jax.experimental.pallas import tpu as pltpu
from jax.sharding import PartitionSpec as P

BF = jnp.bfloat16
F32 = jnp.float32
NT = (((1,), (1,)), ((), ()))
TN = (((0,), (0,)), ((), ()))


def iota(shape, axis):
    return lax.broadcasted_iota(jnp.int32, shape, axis)


def one_hot(hit):
    return jnp.where(hit, 1.0, 0.0).astype(BF)


def chunk(index, size):
    return pl.ds(pl.multiple_of(index * size, size), size)


def request_kernel(own_hbm, row_hbm, req_ref, flat_ref, own_ref, row_ref, hot, picked, spots, sems):
    peers, _, cap = req_ref.shape
    lines, width = own_ref.shape
    copies = [
        pltpu.make_async_copy(own_hbm, own_ref, sems.at[0]),
        pltpu.make_async_copy(row_hbm, row_ref, sems.at[1]),
    ]
    for copy in copies:
        copy.start()
    for copy in copies:
        copy.wait()
    names = iota((peers, width), 0)
    for r in range(lines):
        hot[r * peers:(r + 1) * peers, :] = one_hot(own_ref[r:r + 1, :] == names)
    before = one_hot(iota((width, 2 * width), 0) <= iota((width, 2 * width), 1))
    counted = jnp.dot(hot[...], before, preferred_element_type=F32)
    base = jnp.full((peers, width), -1.0, F32)
    slots = iota((cap, width), 0)
    for r in range(lines):
        here = counted[r * peers:(r + 1) * peers]
        hit = own_ref[r:r + 1, :] == names
        slot = jnp.sum(jnp.where(hit, here[:, :width] + base, 0.0), axis=0, keepdims=True)
        slot = slot.astype(jnp.int32)
        base = base + here[:, width:]
        flat_ref[r:r + 1, :] = own_ref[r:r + 1, :] * cap + slot
        cols = slice(r * width, (r + 1) * width)
        row = row_ref[r:r + 1, :]
        upper = jnp.broadcast_to((row >> 6).astype(F32), (peers, width))
        lower = jnp.broadcast_to((row & 63).astype(F32), (peers, width))
        picked[:peers, cols] = jnp.where(hit, upper, 0.0).astype(BF)
        picked[peers:, cols] = jnp.where(hit, lower, 0.0).astype(BF)
        spots[:, cols] = one_hot(slots == slot)
    found = lax.dot_general(picked[...], spots[...], NT, preferred_element_type=F32)
    req_ref[:, 0, :] = (found[:peers] * 64.0 + found[peers:]).astype(jnp.int32)


def request_table(owners, rows, peers, cap):
    lines, width = owners.shape
    return pl.pallas_call(
        request_kernel,
        out_shape=(
            jax.ShapeDtypeStruct((peers, 1, cap), jnp.int32),
            jax.ShapeDtypeStruct(owners.shape, jnp.int32),
        ),
        in_specs=[pl.BlockSpec(memory_space=pltpu.HBM)] * 2,
        scratch_shapes=[
            pltpu.VMEM(owners.shape, jnp.int32),
            pltpu.VMEM(owners.shape, jnp.int32),
            pltpu.VMEM((lines * peers, width), BF),
            pltpu.VMEM((2 * peers, lines * width), BF),
            pltpu.VMEM((cap, lines * width), BF),
            pltpu.SemaphoreType.DMA((2,)),
        ],
        compiler_params=pltpu.CompilerParams(vmem_limit_bytes=62 << 20),
        name="request_table",
    )(owners, rows)


def count_kernel(idx_ref, out_ref):
    groups = idx_ref.shape[0]
    uppers = out_ref.shape[1] // 256
    target = iota((1, 256), 1) >> 4
    rows_upper = iota((uppers * 16, 256), 0)
    rows_lower = iota((256, 256), 0)

    def group(g, carry):
        value = idx_ref[pl.ds(g, 1), :]
        code = jnp.where(value >= 0, (value >> 8) * 16 + target, -1)
        found = lax.dot_general(
            one_hot(rows_upper == code),
            one_hot(rows_lower == (value & 255)),
            NT,
            preferred_element_type=F32,
        ).astype(BF)
        for u in range(uppers):
            out_ref[chunk(g, 16), u * 256:(u + 1) * 256] = found[u * 16:(u + 1) * 16, :]
        return carry

    lax.fori_loop(0, groups, group, 0, unroll=4)


def neighbour_counts(lists, sources, block_groups=16):
    targets, places = lists.shape
    padded = jnp.pad(lists, ((0, 0), (0, 16 - places)), constant_values=-1)
    return pl.pallas_call(
        count_kernel,
        grid=(targets // 16 // block_groups,),
        in_specs=[pl.BlockSpec((block_groups, 256), lambda i: (i, 0))],
        out_specs=pl.BlockSpec((block_groups * 16, sources), lambda i: (i, 0)),
        out_shape=jax.ShapeDtypeStruct((targets, sources), BF),
        compiler_params=pltpu.CompilerParams(vmem_limit_bytes=40 << 20),
        cost_estimate=pl.CostEstimate(
            flops=512 * targets * sources,
            bytes_accessed=2 * targets * sources,
            transcendentals=0,
        ),
        name="neighbour_counts",
    )(padded.reshape(targets // 16, 256))


def pick_rows(idx_ref, first, count, low, high, out_ref):
    half = low.shape[1]
    line = iota((8, half), 0)

    def some(i, carry):
        begin = pl.multiple_of(i * 16, 16)
        lows, highs = [], []
        for h in range(2):
            for j in range(8):
                row = idx_ref[first + begin + h * 8 + j]
                new_low = jnp.broadcast_to(low[pl.ds(row, 1), :], (8, half))
                new_high = jnp.broadcast_to(high[pl.ds(row, 1), :], (8, half))
                if j == 0:
                    got_low, got_high = new_low, new_high
                else:
                    got_low = jnp.where(line == j, new_low, got_low)
                    got_high = jnp.where(line == j, new_high, got_high)
            lows.append(got_low)
            highs.append(got_high)
        out_ref[pl.ds(begin, 16), :half] = jnp.concatenate(lows, axis=0).astype(BF)
        out_ref[pl.ds(begin, 16), half:] = jnp.concatenate(highs, axis=0).astype(BF)
        return carry

    lax.fori_loop(0, count // 16, some, 0, unroll=8)


def piece_copies(source_ref, held, sems):
    rows = held.shape[0] // sems.shape[0]
    return [
        pltpu.make_async_copy(
            source_ref.at[pl.ds(p * rows, rows), :], held.at[pl.ds(p * rows, rows), :], sems.at[p]
        )
        for p in range(sems.shape[0])
    ]


def widen(held, low, high, copies):
    rows = held.shape[0] // len(copies)
    half = low.shape[1]
    for p, copy in enumerate(copies):
        copy.wait()

        def some(i, carry):
            part = pl.ds(pl.multiple_of(p * rows + i * 128, 128), 128)
            low[part, :] = held[part, :half].astype(F32)
            high[part, :] = held[part, half:].astype(F32)
            return carry

        lax.fori_loop(0, rows // 128, some, 0, unroll=2)


def gather_kernel(idx_ref, table_ref, out_ref, held, low, high, sems):
    step = pl.program_id(0)
    rows = out_ref.shape[0]

    @pl.when(step == 0)
    def _():
        copies = piece_copies(table_ref, held, sems)
        for copy in copies:
            copy.start()
        widen(held, low, high, copies)

    pick_rows(idx_ref, step * rows, rows, low, high, out_ref)


def gather_rows(table, idx, rows=1024):
    total = idx.shape[0]
    own_rows, width = table.shape
    return pl.pallas_call(
        gather_kernel,
        grid_spec=pltpu.PrefetchScalarGridSpec(
            num_scalar_prefetch=1,
            grid=(total // rows,),
            in_specs=[pl.BlockSpec(memory_space=pltpu.HBM)],
            out_specs=pl.BlockSpec((rows, width), lambda i, s: (i, 0)),
            scratch_shapes=[
                pltpu.VMEM((own_rows, width), BF),
                pltpu.VMEM((own_rows, width // 2), F32),
                pltpu.VMEM((own_rows, width // 2), F32),
                pltpu.SemaphoreType.DMA((8,)),
            ],
        ),
        out_shape=pltpu.HBM((total, width), BF),
        compiler_params=pltpu.CompilerParams(vmem_limit_bytes=62 << 20),
        name="gather_rows",
    )(idx, table)


def layer_kernel(list_width, idx_ref, spot_ref, arrived_ref, counts_ref, ws_ref, wn_ref,
                 *refs):
    part_refs, (both_ref, held, low, high, frontier, counts, sems, count_sems) = refs[:-8], refs[-8:]
    step = pl.program_id(0)
    block = both_ref.shape[0]
    width = held.shape[1]

    def count_copy(b):
        return pltpu.make_async_copy(
            counts_ref.at[pl.ds(b * block, block), :],
            counts.at[pl.ds(b * block, block), :],
            count_sems.at[b],
        )

    @pl.when(step == 0)
    def _():
        copies = piece_copies(arrived_ref, held, sems)
        for copy in copies:
            copy.start()
        for b in range(counts.shape[0] // block):
            count_copy(b).start()
        widen(held, low, high, copies)
        pick_rows(idx_ref, 0, frontier.shape[0], low, high, frontier)

    count_copy(step).wait()
    here = chunk(step, block)
    total = jnp.dot(counts[here, :], frontier[...], preferred_element_type=F32)
    own = frontier[here, :]
    mean = (total / list_width).astype(BF)
    both_ref[:, :width] = own
    both_ref[:, width:] = mean
    share = part_refs[0].shape[1]
    quarters = ws_ref.shape[1] // share
    made = jnp.dot(own, ws_ref[...], preferred_element_type=F32)
    made = (made + jnp.dot(mean, wn_ref[...], preferred_element_type=F32)).astype(BF)
    for q in range(quarters):
        d = lax.rem(q + quarters - spot_ref[0], quarters)
        for e in range(quarters):
            for half in range(2):
                @pl.when((d == e) & (step // (pl.num_programs(0) // 2) == half))
                def _():
                    part_refs[2 * e + half][...] = made[:, q * share:(q + 1) * share]


def first_layer(idx, spot, arrived, counts, w_self, w_near, list_width, quarters, block=1024):
    targets, positions = counts.shape
    slots, width = arrived.shape
    share = w_self.shape[1] // quarters
    steps = targets // block
    middle = steps // 2

    def full(shape):
        return pl.BlockSpec(shape, lambda i, *s: (0, 0))

    halves = [
        pl.BlockSpec((block, share), lambda i, *s: (jnp.minimum(i, middle - 1), 0)),
        pl.BlockSpec((block, share), lambda i, *s: (jnp.maximum(i - middle, 0), 0)),
    ]
    return pl.pallas_call(
        functools.partial(layer_kernel, list_width),
        grid_spec=pltpu.PrefetchScalarGridSpec(
            num_scalar_prefetch=2,
            grid=(steps,),
            in_specs=[
                pl.BlockSpec(memory_space=pltpu.HBM),
                pl.BlockSpec(memory_space=pltpu.HBM),
                full(w_self.shape),
                full(w_near.shape),
            ],
            out_specs=halves * quarters + [pl.BlockSpec((block, 2 * width), lambda i, *s: (i, 0))],
            scratch_shapes=[
                pltpu.VMEM((slots, width), BF),
                pltpu.VMEM((slots, width // 2), F32),
                pltpu.VMEM((slots, width // 2), F32),
                pltpu.VMEM((positions, width), BF),
                pltpu.VMEM((targets, positions), BF),
                pltpu.SemaphoreType.DMA((8,)),
                pltpu.SemaphoreType.DMA((steps,)),
            ],
        ),
        out_shape=[jax.ShapeDtypeStruct((targets // 2, share), BF)] * 2
        + [pltpu.VMEM((targets // 2, share), BF)] * (2 * quarters - 2)
        + [jax.ShapeDtypeStruct((targets, 2 * width), BF)],
        compiler_params=pltpu.CompilerParams(vmem_limit_bytes=60 << 20),
        name="first_layer",
    )(idx, spot, arrived, counts, w_self, w_near)


def slope_kernel(part0, up, down, bias_ref, d_ref, hidden_ref, slope_ref):
    active = part0[...].astype(F32) + up[...].astype(F32) + down[...].astype(F32)
    active = active + bias_ref[...].astype(F32)
    below = 1.0 + jnp.exp(-active)
    sigmoid = 1.0 / below
    hidden_ref[...] = (active / below).astype(BF)
    slope_ref[...] = (d_ref[...] * (sigmoid * (1.0 + active * (1.0 - sigmoid)))).astype(BF)


def hidden_and_slope(part0, up, down, bias, d_hidden, first, block=512):
    rows, share = part0.shape
    place = pl.BlockSpec((block, share), lambda i: (i, 0))
    return pl.pallas_call(
        slope_kernel,
        grid=(rows // block,),
        in_specs=[place] * 3
        + [
            pl.BlockSpec((1, share), lambda i: (0, 0)),
            pl.BlockSpec((block, share), lambda i: (i + first // block, 0)),
        ],
        out_specs=[place, place],
        out_shape=[jax.ShapeDtypeStruct((rows, share), BF)] * 2,
        compiler_params=pltpu.CompilerParams(vmem_limit_bytes=16 << 20),
        name="hidden_and_slope",
    )(part0, up, down, bias, d_hidden)


def pack_kernel(core_ref, *refs):
    *value_refs, keep_ref, give_ref = refs
    chips, _, share = keep_ref.shape
    first = 0
    for ref in value_refs:
        rows = ref.shape[0] // (2 * chips)
        for c in range(ref.shape[1] // share):
            cols = slice(c * share, (c + 1) * share)
            for out_ref, core in ((keep_ref, core_ref[0]), (give_ref, 1 - core_ref[0])):
                block = ref[chunk(core, chips * rows), cols]
                out_ref[:, first:first + rows, :] = block.reshape(chips, rows, share)
            first += rows


def pack_shards(core, values, chips, share):
    rows = sum(v.size for v in values) // (2 * chips * share)
    return pl.pallas_call(
        pack_kernel,
        in_specs=[pl.BlockSpec(memory_space=pltpu.SMEM)]
        + [pl.BlockSpec(memory_space=pltpu.VMEM)] * len(values),
        out_specs=[pl.BlockSpec(memory_space=pltpu.VMEM)] * 2,
        out_shape=[jax.ShapeDtypeStruct((chips, rows, share), BF)] * 2,
        compiler_params=pltpu.CompilerParams(vmem_limit_bytes=16 << 20),
        name="pack_shards",
    )(core, *values)


def finish_kernel(spot_ref, mine_ref, other_ref, ws_ref, wn_ref, vs_ref, vn_ref):
    peers, shard, share = mine_ref.shape
    feats = ws_ref.shape[0]
    some = feats // peers
    order = (0, 1, 3, 2)
    v_rows = shard - some * len(order)
    front = spot_ref[1] == 0

    def halves(first, count):
        part = slice(first, first + count)
        mine = mine_ref[:, part, :].astype(F32).reshape(peers * count, share)
        other = other_ref[:, part, :].astype(F32).reshape(peers * count, share)
        return jnp.where(front, mine, other), jnp.where(front, other, mine)

    for place, d in enumerate(order):
        cols = chunk(lax.rem(spot_ref[0] + d, len(order)), share)
        ws_ref[:, cols], wn_ref[:, cols] = halves(v_rows + place * some, some)
    for half, block in enumerate(halves(0, v_rows)):
        for e in range(len(order) // 2):
            cols = slice((2 * half + e) * share, (2 * half + e + 1) * share)
            vs_ref[:, cols] = block[2 * e * share:(2 * e + 1) * share]
            vn_ref[:, cols] = block[(2 * e + 1) * share:(2 * e + 2) * share]


def body(
    feature_table,
    owner_ids,
    row_ids,
    near_first,
    near_second,
    w_self,
    w_near,
    bias_hidden,
    v_self,
    v_near,
    cotangent,
):
    peers = lax.axis_size("wide")
    quarters = lax.axis_size("blk")
    z = lax.axis_index("blk")
    core = lax.axis_index("wide") % 2
    frontier_count = row_ids.shape[0]
    cap = 2 * frontier_count // peers
    targets, first_width = near_first.shape
    seeds, second_width = near_second.shape
    feats, hidden_units = w_self.shape
    share = hidden_units // quarters

    def shift(value, by):
        return lax.ppermute(value, "blk", [(i, (i + by) % quarters) for i in range(quarters)])

    def exchange(value):
        return lax.all_to_all(value, "wide", split_axis=0, concat_axis=0, tiled=True)

    with jax.named_scope("requests"):
        requests, flat = request_table(
            owner_ids.reshape(frontier_count // 128, 128),
            row_ids.reshape(frontier_count // 128, 128),
            peers,
            cap,
        )
        wanted = exchange(requests).reshape(-1)
        flat = flat.reshape(-1)
    with jax.named_scope("rows"):
        found = gather_rows(feature_table, wanted)
        arrived = exchange(found.reshape(peers, cap, feats)).reshape(peers * cap, feats)
    with jax.named_scope("beside_rows"):
        counts_first = neighbour_counts(near_first, frontier_count)
        counts_second = neighbour_counts(near_second, targets)
        d_self = lax.dot_general(cotangent, v_self, NT, preferred_element_type=F32)
        d_mean = lax.dot_general(cotangent, v_near, NT, preferred_element_type=F32) / second_width
        d_upper = d_mean.astype(BF)
        d_lower = (d_mean - d_upper.astype(F32)).astype(BF)
        spread = lax.dot_general(
            counts_second,
            jnp.concatenate([d_upper, d_lower], axis=1),
            TN,
            preferred_element_type=F32,
        )
        d_hidden = spread[:, :share] + spread[:, share:]
        d_hidden = d_hidden + jnp.pad(d_self, ((0, targets - seeds), (0, 0)))
        arrived, counts_first, counts_second, d_hidden = lax.optimization_barrier(
            (arrived, counts_first, counts_second, d_hidden)
        )
    with jax.named_scope("first_layer"):
        *parts, both = first_layer(
            flat,
            jnp.full((1,), z, jnp.int32),
            arrived,
            counts_first,
            w_self,
            w_near,
            first_width,
            quarters,
        )
    def added(left, right):
        return (left.astype(F32) + right.astype(F32)).astype(BF)

    with jax.named_scope("pre_act_exchange"):
        own, above, far, below = [parts[2 * d:2 * d + 2] for d in range(quarters)]
        passing_up = shift(far[0], 1)
        passing_down = shift(far[1], -1)
        down_0 = shift(below[0], -1)
        up_1 = shift(above[1], 1)
        up_0 = shift(added(above[0], passing_up), 1)
        down_1 = shift(added(below[1], passing_down), -1)
        hiddens, slopes = [], []
        for half, (up, down) in enumerate([(up_0, down_0), (up_1, down_1)]):
            hidden, slope = hidden_and_slope(
                own[half], up, down, bias_hidden.reshape(1, share), d_hidden, half * targets // 2
            )
            hiddens.append(hidden)
            slopes.append(slope)
    with jax.named_scope("slope_exchange"):
        from_down = [shift(slope, 1) for slope in slopes]
        from_up = [shift(slope, -1) for slope in slopes]
        from_far = [shift(from_down[0], 1), shift(from_up[1], -1)]
        from_down, from_up, from_far = [jnp.concatenate(v) for v in (from_down, from_up, from_far)]

    def grad_w(slope_part):
        return lax.dot_general(both, slope_part, TN, preferred_element_type=F32).astype(BF)

    def swap(value):
        return lax.ppermute(value, "wide", [(i, i ^ 1) for i in range(peers)])

    def between_chips(value):
        return lax.all_to_all(
            value,
            "wide",
            split_axis=0,
            concat_axis=0,
            axis_index_groups=[list(range(c, peers, 2)) for c in range(2)],
            tiled=True,
        )

    with jax.named_scope("second_layer"):
        hidden = jnp.concatenate(hiddens)
        seed_hidden = hidden[:seeds]
        second_mean = (
            jnp.dot(counts_second, hidden, preferred_element_type=F32) / second_width
        ).astype(BF)
        grad_v = jnp.concatenate(
            [
                lax.dot_general(seed_hidden, cotangent, TN, preferred_element_type=F32),
                lax.dot_general(second_mean, cotangent, TN, preferred_element_type=F32),
            ]
        ).astype(BF)
        grad_v = jnp.concatenate([grad_v[:, c * share:(c + 1) * share] for c in range(quarters)])
        partial_out = jnp.dot(seed_hidden, v_self, preferred_element_type=F32) + jnp.dot(
            second_mean, v_near, preferred_element_type=F32
        )

        def out_part(d):
            return lax.dynamic_slice_in_dim(partial_out, (z + d) % quarters * share, share, 1)

        outs = [shift(out_part(d).astype(BF), d) for d in range(1, quarters)]
    with jax.named_scope("gradients"):
        near_two = grad_w(jnp.concatenate([from_up, from_down], axis=1))
        chips = peers // 2
        keep, give = pack_shards(
            core.reshape(1), [grad_v, grad_w(jnp.concatenate(slopes)), near_two, grad_w(from_far)], chips, share
        )
        sums = between_chips(added(keep, swap(give)))
        sums = jnp.sum(sums.astype(F32), axis=0).astype(BF)
        mine = between_chips(jnp.broadcast_to(sums, (chips, *sums.shape)))
        mine, *outs = lax.optimization_barrier((mine, *outs))
        other = swap(mine)
        seed_out = out_part(0)
        for part in outs:
            seed_out = seed_out + part.astype(F32)
        seed_out = seed_out.astype(BF)
        grads = pl.pallas_call(
            finish_kernel,
            in_specs=[pl.BlockSpec(memory_space=pltpu.SMEM)] + [pl.BlockSpec(memory_space=pltpu.VMEM)] * 2,
            out_specs=[pl.BlockSpec(memory_space=pltpu.VMEM)] * 4,
            out_shape=[jax.ShapeDtypeStruct((feats, hidden_units), F32)] * 2
            + [jax.ShapeDtypeStruct((share, hidden_units), F32)] * 2,
            compiler_params=pltpu.CompilerParams(vmem_limit_bytes=16 << 20),
            name="finish",
        )(jnp.stack([z, core]).astype(jnp.int32), mine, other)
    return (seed_out, *grads)


def solution(mesh):
    placed = (
        P("wide", "blk"),
        P("wide", None),
        P("wide"),
        P("wide", None),
        P("wide", None),
        P("blk", None),
        P("blk", None),
        P("blk"),
        P("blk", None),
        P("blk", None),
        P("wide", None),
    )
    return jax.shard_map(
        body,
        mesh=mesh,
        in_specs=placed,
        out_specs=(
            P("wide", "blk"),
            P("blk", None),
            P("blk", None),
            P("blk", None),
            P("blk", None),
        ),
        check_vma=False,
    )
```

```python
import functools

import jax
import jax.numpy as jnp
from jax import lax
from jax.experimental import pallas as pl
from jax.experimental.pallas import tpu as pltpu
from jax.sharding import PartitionSpec as P

BF = jnp.bfloat16
F32 = jnp.float32
NT = (((1,), (1,)), ((), ()))
TN = (((0,), (0,)), ((), ()))


def iota(shape, axis):
    return lax.broadcasted_iota(jnp.int32, shape, axis)


def one_hot(hit):
    return jnp.where(hit, 1.0, 0.0).astype(BF)


def chunk(index, size):
    return pl.ds(pl.multiple_of(index * size, size), size)


def request_kernel(own_hbm, row_hbm, req_ref, flat_ref, own_ref, row_ref, hot, picked, spots, sems):
    peers, _, cap = req_ref.shape
    lines, width = own_ref.shape
    copies = [
        pltpu.make_async_copy(own_hbm, own_ref, sems.at[0]),
        pltpu.make_async_copy(row_hbm, row_ref, sems.at[1]),
    ]
    for copy in copies:
        copy.start()
    for copy in copies:
        copy.wait()
    names = iota((peers, width), 0)
    for r in range(lines):
        hot[r * peers:(r + 1) * peers, :] = one_hot(own_ref[r:r + 1, :] == names)
    before = one_hot(iota((width, 2 * width), 0) <= iota((width, 2 * width), 1))
    counted = jnp.dot(hot[...], before, preferred_element_type=F32)
    base = jnp.full((peers, width), -1.0, F32)
    slots = iota((cap, width), 0)
    for r in range(lines):
        here = counted[r * peers:(r + 1) * peers]
        hit = own_ref[r:r + 1, :] == names
        slot = jnp.sum(jnp.where(hit, here[:, :width] + base, 0.0), axis=0, keepdims=True)
        slot = slot.astype(jnp.int32)
        base = base + here[:, width:]
        flat_ref[r:r + 1, :] = own_ref[r:r + 1, :] * cap + slot
        cols = slice(r * width, (r + 1) * width)
        row = row_ref[r:r + 1, :]
        upper = jnp.broadcast_to((row >> 6).astype(F32), (peers, width))
        lower = jnp.broadcast_to((row & 63).astype(F32), (peers, width))
        picked[:peers, cols] = jnp.where(hit, upper, 0.0).astype(BF)
        picked[peers:, cols] = jnp.where(hit, lower, 0.0).astype(BF)
        spots[:, cols] = one_hot(slots == slot)
    found = lax.dot_general(picked[...], spots[...], NT, preferred_element_type=F32)
    req_ref[:, 0, :] = (found[:peers] * 64.0 + found[peers:]).astype(jnp.int32)


def request_table(owners, rows, peers, cap):
    lines, width = owners.shape
    return pl.pallas_call(
        request_kernel,
        out_shape=(
            jax.ShapeDtypeStruct((peers, 1, cap), jnp.int32),
            jax.ShapeDtypeStruct(owners.shape, jnp.int32),
        ),
        in_specs=[pl.BlockSpec(memory_space=pltpu.HBM)] * 2,
        scratch_shapes=[
            pltpu.VMEM(owners.shape, jnp.int32),
            pltpu.VMEM(owners.shape, jnp.int32),
            pltpu.VMEM((lines * peers, width), BF),
            pltpu.VMEM((2 * peers, lines * width), BF),
            pltpu.VMEM((cap, lines * width), BF),
            pltpu.SemaphoreType.DMA((2,)),
        ],
        compiler_params=pltpu.CompilerParams(vmem_limit_bytes=62 << 20),
        name="request_table",
    )(owners, rows)


def count_kernel(idx_ref, out_ref):
    groups = idx_ref.shape[0]
    uppers = out_ref.shape[1] // 256
    target = iota((1, 256), 1) >> 4
    rows_upper = iota((uppers * 16, 256), 0)
    rows_lower = iota((256, 256), 0)

    def group(g, carry):
        value = idx_ref[pl.ds(g, 1), :]
        code = jnp.where(value >= 0, (value >> 8) * 16 + target, -1)
        found = lax.dot_general(
            one_hot(rows_upper == code),
            one_hot(rows_lower == (value & 255)),
            NT,
            preferred_element_type=F32,
        ).astype(BF)
        for u in range(uppers):
            out_ref[chunk(g, 16), u * 256:(u + 1) * 256] = found[u * 16:(u + 1) * 16, :]
        return carry

    lax.fori_loop(0, groups, group, 0, unroll=4)


def neighbour_counts(lists, sources, block_groups=16):
    targets, places = lists.shape
    padded = jnp.pad(lists, ((0, 0), (0, 16 - places)), constant_values=-1)
    return pl.pallas_call(
        count_kernel,
        grid=(targets // 16 // block_groups,),
        in_specs=[pl.BlockSpec((block_groups, 256), lambda i: (i, 0))],
        out_specs=pl.BlockSpec((block_groups * 16, sources), lambda i: (i, 0)),
        out_shape=jax.ShapeDtypeStruct((targets, sources), BF),
        compiler_params=pltpu.CompilerParams(vmem_limit_bytes=40 << 20),
        cost_estimate=pl.CostEstimate(
            flops=512 * targets * sources,
            bytes_accessed=2 * targets * sources,
            transcendentals=0,
        ),
        name="neighbour_counts",
    )(padded.reshape(targets // 16, 256))


def pick_rows(idx_ref, first, count, low, high, out_ref):
    half = low.shape[1]
    line = iota((8, half), 0)

    def some(i, carry):
        begin = pl.multiple_of(i * 16, 16)
        lows, highs = [], []
        for h in range(2):
            for j in range(8):
                row = idx_ref[first + begin + h * 8 + j]
                new_low = jnp.broadcast_to(low[pl.ds(row, 1), :], (8, half))
                new_high = jnp.broadcast_to(high[pl.ds(row, 1), :], (8, half))
                if j == 0:
                    got_low, got_high = new_low, new_high
                else:
                    got_low = jnp.where(line == j, new_low, got_low)
                    got_high = jnp.where(line == j, new_high, got_high)
            lows.append(got_low)
            highs.append(got_high)
        out_ref[pl.ds(begin, 16), :half] = jnp.concatenate(lows, axis=0).astype(BF)
        out_ref[pl.ds(begin, 16), half:] = jnp.concatenate(highs, axis=0).astype(BF)
        return carry

    lax.fori_loop(0, count // 16, some, 0, unroll=8)


def piece_copies(source_ref, held, sems):
    rows = held.shape[0] // sems.shape[0]
    return [
        pltpu.make_async_copy(
            source_ref.at[pl.ds(p * rows, rows), :], held.at[pl.ds(p * rows, rows), :], sems.at[p]
        )
        for p in range(sems.shape[0])
    ]


def widen(held, low, high, copies):
    pieces = max(1, len(copies))
    rows = held.shape[0] // pieces
    half = low.shape[1]
    for p in range(pieces):
        if copies:
            copies[p].wait()

        def some(i, carry):
            part = pl.ds(pl.multiple_of(p * rows + i * 128, 128), 128)
            low[part, :] = held[part, :half].astype(F32)
            high[part, :] = held[part, half:].astype(F32)
            return carry

        lax.fori_loop(0, rows // 128, some, 0, unroll=2)


def gather_kernel(idx_hbm, table_ref, out_ref, idx_ref, held, low, high, sems, idx_sem):
    step = pl.program_id(0)
    rows = out_ref.shape[0]

    @pl.when(step == 0)
    def _():
        copies = piece_copies(table_ref, held, sems)
        idx_copy = pltpu.make_async_copy(idx_hbm, idx_ref, idx_sem)
        for copy in [idx_copy] + copies:
            copy.start()
        widen(held, low, high, copies)
        idx_copy.wait()

    pick_rows(idx_ref, step * rows, rows, low, high, out_ref)


def gather_rows(table, idx, rows=1024):
    total = idx.shape[0]
    own_rows, width = table.shape
    return pl.pallas_call(
        gather_kernel,
        grid=(total // rows,),
        in_specs=[pl.BlockSpec(memory_space=pltpu.HBM)] * 2,
        out_specs=pl.BlockSpec((rows, width), lambda i: (i, 0)),
        scratch_shapes=[
            pltpu.SMEM((total,), jnp.int32),
            pltpu.VMEM((own_rows, width), BF),
            pltpu.VMEM((own_rows, width // 2), F32),
            pltpu.VMEM((own_rows, width // 2), F32),
            pltpu.SemaphoreType.DMA((8,)),
            pltpu.SemaphoreType.DMA,
        ],
        out_shape=pltpu.HBM((total, width), BF),
        compiler_params=pltpu.CompilerParams(vmem_limit_bytes=62 << 20),
        name="gather_rows",
    )(idx, table)


def layer_kernel(list_width, idx_ref, spot_ref, arrived_ref, counts_ref, ws_ref, wn_ref,
                 *refs):
    part_refs, (both_ref, low, high, frontier, counts, count_sems) = refs[:-6], refs[-6:]
    step = pl.program_id(0)
    block = both_ref.shape[0]
    width = arrived_ref.shape[1]

    def count_copy(b):
        return pltpu.make_async_copy(
            counts_ref.at[pl.ds(b * block, block), :],
            counts.at[pl.ds(b * block, block), :],
            count_sems.at[b],
        )

    @pl.when(step == 0)
    def _():
        for b in range(counts.shape[0] // block):
            count_copy(b).start()
        widen(arrived_ref, low, high, [])
        pick_rows(idx_ref, 0, frontier.shape[0], low, high, frontier)

    count_copy(step).wait()
    here = chunk(step, block)
    total = jnp.dot(counts[here, :], frontier[...], preferred_element_type=F32)
    own = frontier[here, :]
    mean = (total / list_width).astype(BF)
    both_ref[:, :width] = own
    both_ref[:, width:] = mean
    share = part_refs[0].shape[1]
    quarters = ws_ref.shape[1] // share
    made = jnp.dot(own, ws_ref[...], preferred_element_type=F32)
    made = (made + jnp.dot(mean, wn_ref[...], preferred_element_type=F32)).astype(BF)
    for q in range(quarters):
        d = lax.rem(q + quarters - spot_ref[0], quarters)
        for e in range(quarters):
            for half in range(2):
                @pl.when((d == e) & (step // (pl.num_programs(0) // 2) == half))
                def _():
                    part_refs[2 * e + half][...] = made[:, q * share:(q + 1) * share]


def first_layer(idx, spot, arrived, counts, w_self, w_near, list_width, quarters, block=1024):
    targets, positions = counts.shape
    slots, width = arrived.shape
    share = w_self.shape[1] // quarters
    steps = targets // block
    middle = steps // 2

    def full(shape):
        return pl.BlockSpec(shape, lambda i, *s: (0, 0))

    halves = [
        pl.BlockSpec((block, share), lambda i, *s: (jnp.minimum(i, middle - 1), 0)),
        pl.BlockSpec((block, share), lambda i, *s: (jnp.maximum(i - middle, 0), 0)),
    ]
    return pl.pallas_call(
        functools.partial(layer_kernel, list_width),
        grid_spec=pltpu.PrefetchScalarGridSpec(
            num_scalar_prefetch=2,
            grid=(steps,),
            in_specs=[
                pl.BlockSpec(memory_space=pltpu.VMEM),
                pl.BlockSpec(memory_space=pltpu.HBM),
                full(w_self.shape),
                full(w_near.shape),
            ],
            out_specs=halves * quarters + [pl.BlockSpec((block, 2 * width), lambda i, *s: (i, 0))],
            scratch_shapes=[
                pltpu.VMEM((slots, width // 2), F32),
                pltpu.VMEM((slots, width // 2), F32),
                pltpu.VMEM((positions, width), BF),
                pltpu.VMEM((targets, positions), BF),
                pltpu.SemaphoreType.DMA((steps,)),
            ],
        ),
        out_shape=[jax.ShapeDtypeStruct((targets // 2, share), BF)] * 2
        + [pltpu.VMEM((targets // 2, share), BF)] * (2 * quarters - 2)
        + [jax.ShapeDtypeStruct((targets, 2 * width), BF)],
        compiler_params=pltpu.CompilerParams(vmem_limit_bytes=54 << 20),
        name="first_layer",
    )(idx, spot, arrived, counts, w_self, w_near)


def add_kernel(left, right, out_ref):
    out_ref[...] = (left[...].astype(F32) + right[...].astype(F32)).astype(BF)


def added(left, right):
    return pl.pallas_call(
        add_kernel,
        in_specs=[pl.BlockSpec(memory_space=pltpu.VMEM)] * 2,
        out_specs=pl.BlockSpec(memory_space=pltpu.VMEM),
        out_shape=jax.ShapeDtypeStruct(left.shape, BF),
        compiler_params=pltpu.CompilerParams(vmem_limit_bytes=16 << 20),
        name="added",
    )(left, right)


def slope_kernel(base, up, down, d_ref, hidden_ref, slope_ref):
    active = base[...] + up[...].astype(F32) + down[...].astype(F32)
    below = 1.0 + jnp.exp(-active)
    sigmoid = 1.0 / below
    hidden_ref[...] = (active / below).astype(BF)
    slope_ref[...] = (d_ref[...] * (sigmoid * (1.0 + active * (1.0 - sigmoid)))).astype(BF)


def hidden_and_slope(base, up, down, d_hidden, first, block=512):
    rows, share = base.shape
    place = pl.BlockSpec((block, share), lambda i: (i, 0))
    return pl.pallas_call(
        slope_kernel,
        grid=(rows // block,),
        in_specs=[place] * 3
        + [
            pl.BlockSpec((block, share), lambda i: (i + first // block, 0)),
        ],
        out_specs=[place, place],
        out_shape=[jax.ShapeDtypeStruct((rows, share), BF)] * 2,
        compiler_params=pltpu.CompilerParams(vmem_limit_bytes=16 << 20),
        name="hidden_and_slope",
    )(base, up, down, d_hidden)


def pack_kernel(core_ref, *refs):
    *value_refs, keep_ref, give_ref = refs
    chips, _, share = keep_ref.shape
    first = 0
    for ref in value_refs:
        rows = ref.shape[0] // (2 * chips)
        for c in range(ref.shape[1] // share):
            cols = slice(c * share, (c + 1) * share)
            for out_ref, core in ((keep_ref, core_ref[0]), (give_ref, 1 - core_ref[0])):
                block = ref[chunk(core, chips * rows), cols]
                out_ref[:, first:first + rows, :] = block.reshape(chips, rows, share)
            first += rows


def pack_shards(core, values, chips, share):
    rows = sum(v.size for v in values) // (2 * chips * share)
    return pl.pallas_call(
        pack_kernel,
        in_specs=[pl.BlockSpec(memory_space=pltpu.SMEM)]
        + [pl.BlockSpec(memory_space=pltpu.VMEM)] * len(values),
        out_specs=[pl.BlockSpec(memory_space=pltpu.VMEM)] * 2,
        out_shape=[jax.ShapeDtypeStruct((chips, rows, share), BF)] * 2,
        compiler_params=pltpu.CompilerParams(vmem_limit_bytes=16 << 20),
        name="pack_shards",
    )(core, *values)


def finish_kernel(spot_ref, mine_ref, other_ref, ws_ref, wn_ref, vs_ref, vn_ref):
    peers, shard, share = mine_ref.shape
    feats = ws_ref.shape[0]
    some = feats // peers
    order = (0, 1, 3, 2)
    v_rows = shard - some * len(order)
    front = spot_ref[1] == 0

    def halves(first, count):
        part = slice(first, first + count)
        mine = mine_ref[:, part, :].astype(F32).reshape(peers * count, share)
        other = other_ref[:, part, :].astype(F32).reshape(peers * count, share)
        return jnp.where(front, mine, other), jnp.where(front, other, mine)

    for place, d in enumerate(order):
        cols = chunk(lax.rem(spot_ref[0] + d, len(order)), share)
        ws_ref[:, cols], wn_ref[:, cols] = halves(v_rows + place * some, some)
    for half, block in enumerate(halves(0, v_rows)):
        for e in range(len(order) // 2):
            cols = slice((2 * half + e) * share, (2 * half + e + 1) * share)
            vs_ref[:, cols] = block[2 * e * share:(2 * e + 1) * share]
            vn_ref[:, cols] = block[(2 * e + 1) * share:(2 * e + 2) * share]


def join_kernel(keep, got, keep_far, got_far, out_ref):
    rows = keep.shape[1]
    out_ref[:, :rows, :] = (keep[...].astype(F32) + got[...].astype(F32)).astype(BF)
    out_ref[:, rows:, :] = (keep_far[...].astype(F32) + got_far[...].astype(F32)).astype(BF)


def joined(keep, got, keep_far, got_far):
    chips, rows, share = keep.shape
    return pl.pallas_call(
        join_kernel,
        in_specs=[pl.BlockSpec(memory_space=pltpu.VMEM)] * 4,
        out_specs=pl.BlockSpec(memory_space=pltpu.VMEM),
        out_shape=jax.ShapeDtypeStruct((chips, rows + keep_far.shape[1], share), BF),
        compiler_params=pltpu.CompilerParams(vmem_limit_bytes=16 << 20),
        name="joined",
    )(keep, got, keep_far, got_far)


def spread_kernel(got_ref, out_ref):
    total = jnp.sum(got_ref[...].astype(F32), axis=0).astype(BF)
    for chip in range(out_ref.shape[0]):
        out_ref[chip] = total


def sum_and_spread(got):
    return pl.pallas_call(
        spread_kernel,
        in_specs=[pl.BlockSpec(memory_space=pltpu.VMEM)],
        out_specs=pl.BlockSpec(memory_space=pltpu.VMEM),
        out_shape=jax.ShapeDtypeStruct(got.shape, BF),
        compiler_params=pltpu.CompilerParams(vmem_limit_bytes=16 << 20),
        name="sum_and_spread",
    )(got)


def body(
    feature_table,
    owner_ids,
    row_ids,
    near_first,
    near_second,
    w_self,
    w_near,
    bias_hidden,
    v_self,
    v_near,
    cotangent,
):
    peers = lax.axis_size("wide")
    quarters = lax.axis_size("blk")
    z = lax.axis_index("blk")
    core = lax.axis_index("wide") % 2
    frontier_count = row_ids.shape[0]
    cap = 2 * frontier_count // peers
    targets, first_width = near_first.shape
    seeds, second_width = near_second.shape
    feats, hidden_units = w_self.shape
    share = hidden_units // quarters

    def shift(value, by):
        return lax.ppermute(value, "blk", [(i, (i + by) % quarters) for i in range(quarters)])

    def exchange(value):
        return lax.all_to_all(value, "wide", split_axis=0, concat_axis=0, tiled=True)

    with jax.named_scope("requests"):
        requests, flat = request_table(
            owner_ids.reshape(frontier_count // 128, 128),
            row_ids.reshape(frontier_count // 128, 128),
            peers,
            cap,
        )
        wanted = exchange(requests).reshape(-1)
        flat = flat.reshape(-1)
    with jax.named_scope("rows"):
        found = gather_rows(feature_table, wanted)
        arrived = exchange(found.reshape(peers, cap, feats)).reshape(peers * cap, feats)
    with jax.named_scope("beside_rows"):
        counts_first = neighbour_counts(near_first, frontier_count)
        counts_second = neighbour_counts(near_second, targets)
        d_self = lax.dot_general(cotangent, v_self, NT, preferred_element_type=F32)
        d_mean = lax.dot_general(cotangent, v_near, NT, preferred_element_type=F32) / second_width
        d_upper = d_mean.astype(BF)
        d_lower = (d_mean - d_upper.astype(F32)).astype(BF)
        spread = lax.dot_general(
            counts_second,
            jnp.concatenate([d_upper, d_lower], axis=1),
            TN,
            preferred_element_type=F32,
        )
        d_hidden = spread[:, :share] + spread[:, share:]
        d_hidden = d_hidden + jnp.pad(d_self, ((0, targets - seeds), (0, 0)))
        arrived, counts_first, counts_second, d_hidden = lax.optimization_barrier(
            (arrived, counts_first, counts_second, d_hidden)
        )
    with jax.named_scope("first_layer"):
        *parts, both = first_layer(
            flat,
            jnp.full((1,), z, jnp.int32),
            arrived,
            counts_first,
            w_self,
            w_near,
            first_width,
            quarters,
        )
    with jax.named_scope("pre_act_exchange"):
        own, above, far, below = [parts[2 * d:2 * d + 2] for d in range(quarters)]
        passing_up = shift(far[0], 1)
        passing_down = shift(far[1], -1)
        down_0 = shift(below[0], -1)
        up_1 = shift(above[1], 1)
        up_0 = shift(added(above[0], passing_up), 1)
        down_1 = shift(added(below[1], passing_down), -1)
        hiddens, slopes = [], []
        for half, (up, down) in enumerate([(up_0, down_0), (up_1, down_1)]):
            base = own[half].astype(F32) + bias_hidden.astype(F32)
            hidden, slope = hidden_and_slope(base, up, down, d_hidden, half * targets // 2)
            hiddens.append(hidden)
            slopes.append(slope)
    with jax.named_scope("slope_exchange"):
        from_down = [shift(slope, 1) for slope in slopes]
        from_up = [shift(slope, -1) for slope in slopes]
        from_far = [shift(from_down[0], 1), shift(from_up[1], -1)]
        from_down, from_up, from_far = [jnp.concatenate(v) for v in (from_down, from_up, from_far)]

    def grad_w(slope_part):
        return lax.dot_general(both, slope_part, TN, preferred_element_type=F32).astype(BF)

    def swap(value):
        return lax.ppermute(value, "wide", [(i, i ^ 1) for i in range(peers)])

    def between_chips(value):
        return lax.all_to_all(
            value,
            "wide",
            split_axis=0,
            concat_axis=0,
            axis_index_groups=[list(range(c, peers, 2)) for c in range(2)],
            tiled=True,
        )

    with jax.named_scope("second_layer"):
        hidden = jnp.concatenate(hiddens)
        seed_hidden = hidden[:seeds]
        second_mean = (
            jnp.dot(counts_second, hidden, preferred_element_type=F32) / second_width
        ).astype(BF)
        grad_v = jnp.concatenate(
            [
                lax.dot_general(seed_hidden, cotangent, TN, preferred_element_type=F32),
                lax.dot_general(second_mean, cotangent, TN, preferred_element_type=F32),
            ]
        ).astype(BF)
        grad_v = jnp.concatenate([grad_v[:, c * share:(c + 1) * share] for c in range(quarters)])
        partial_out = jnp.dot(seed_hidden, v_self, preferred_element_type=F32) + jnp.dot(
            second_mean, v_near, preferred_element_type=F32
        )

        def out_part(d):
            return lax.dynamic_slice_in_dim(partial_out, (z + d) % quarters * share, share, 1)

        outs = [shift(out_part(d).astype(BF), d) for d in range(1, quarters)]
    with jax.named_scope("gradients"):
        near_two = grad_w(jnp.concatenate([from_up, from_down], axis=1))
        chips = peers // 2
        near_two, outs[0] = lax.optimization_barrier((near_two, outs[0]))
        keep, give = pack_shards(
            core.reshape(1), [grad_v, grad_w(jnp.concatenate(slopes)), near_two], chips, share
        )
        keep_far, give_far = pack_shards(core.reshape(1), [grad_w(from_far)], chips, share)
        sums = between_chips(joined(keep, swap(give), keep_far, swap(give_far)))
        mine = between_chips(sum_and_spread(sums))
        mine, *outs = lax.optimization_barrier((mine, *outs))
        other = swap(mine)
        seed_out = out_part(0)
        for part in outs:
            seed_out = seed_out + part.astype(F32)
        seed_out = seed_out.astype(BF)
        grads = pl.pallas_call(
            finish_kernel,
            in_specs=[pl.BlockSpec(memory_space=pltpu.SMEM)] + [pl.BlockSpec(memory_space=pltpu.VMEM)] * 2,
            out_specs=[pl.BlockSpec(memory_space=pltpu.VMEM)] * 4,
            out_shape=[jax.ShapeDtypeStruct((feats, hidden_units), F32)] * 2
            + [jax.ShapeDtypeStruct((share, hidden_units), F32)] * 2,
            compiler_params=pltpu.CompilerParams(vmem_limit_bytes=16 << 20),
            name="finish",
        )(jnp.stack([z, core]).astype(jnp.int32), mine, other)
    return (seed_out, *grads)


def solution(mesh):
    placed = (
        P("wide", "blk"),
        P("wide", None),
        P("wide"),
        P("wide", None),
        P("wide", None),
        P("blk", None),
        P("blk", None),
        P("blk"),
        P("blk", None),
        P("blk", None),
        P("wide", None),
    )
    return jax.shard_map(
        body,
        mesh=mesh,
        in_specs=placed,
        out_specs=(
            P("wide", "blk"),
            P("blk", None),
            P("blk", None),
            P("blk", None),
            P("blk", None),
        ),
        check_vma=False,
    )
```

```python
import functools

import jax
import jax.numpy as jnp
from jax import lax
from jax.experimental import pallas as pl
from jax.experimental.pallas import tpu as pltpu
from jax.sharding import PartitionSpec as P

BF = jnp.bfloat16
F32 = jnp.float32
NT = (((1,), (1,)), ((), ()))
TN = (((0,), (0,)), ((), ()))


def iota(shape, axis):
    return lax.broadcasted_iota(jnp.int32, shape, axis)


def one_hot(hit):
    return jnp.where(hit, 1.0, 0.0).astype(BF)


def chunk(index, size):
    return pl.ds(pl.multiple_of(index * size, size), size)


def request_kernel(own_hbm, row_hbm, req_ref, flat_ref, own_ref, row_ref, hot, picked, spots, sems):
    peers, _, cap = req_ref.shape
    lines, width = own_ref.shape
    copies = [
        pltpu.make_async_copy(own_hbm, own_ref, sems.at[0]),
        pltpu.make_async_copy(row_hbm, row_ref, sems.at[1]),
    ]
    for copy in copies:
        copy.start()
    for copy in copies:
        copy.wait()
    names = iota((peers, width), 0)
    for r in range(lines):
        hot[r * peers:(r + 1) * peers, :] = one_hot(own_ref[r:r + 1, :] == names)
    before = one_hot(iota((width, 2 * width), 0) <= iota((width, 2 * width), 1))
    counted = jnp.dot(hot[...], before, preferred_element_type=F32)
    base = jnp.full((peers, width), -1.0, F32)
    slots = iota((cap, width), 0)
    for r in range(lines):
        here = counted[r * peers:(r + 1) * peers]
        hit = own_ref[r:r + 1, :] == names
        slot = jnp.sum(jnp.where(hit, here[:, :width] + base, 0.0), axis=0, keepdims=True)
        slot = slot.astype(jnp.int32)
        base = base + here[:, width:]
        flat_ref[r:r + 1, :] = own_ref[r:r + 1, :] * cap + slot
        cols = slice(r * width, (r + 1) * width)
        row = row_ref[r:r + 1, :]
        upper = jnp.broadcast_to((row >> 6).astype(F32), (peers, width))
        lower = jnp.broadcast_to((row & 63).astype(F32), (peers, width))
        picked[:peers, cols] = jnp.where(hit, upper, 0.0).astype(BF)
        picked[peers:, cols] = jnp.where(hit, lower, 0.0).astype(BF)
        spots[:, cols] = one_hot(slots == slot)
    found = lax.dot_general(picked[...], spots[...], NT, preferred_element_type=F32)
    req_ref[:, 0, :] = (found[:peers] * 64.0 + found[peers:]).astype(jnp.int32)


def request_table(owners, rows, peers, cap):
    lines, width = owners.shape
    return pl.pallas_call(
        request_kernel,
        out_shape=(
            jax.ShapeDtypeStruct((peers, 1, cap), jnp.int32),
            jax.ShapeDtypeStruct(owners.shape, jnp.int32),
        ),
        in_specs=[pl.BlockSpec(memory_space=pltpu.HBM)] * 2,
        scratch_shapes=[
            pltpu.VMEM(owners.shape, jnp.int32),
            pltpu.VMEM(owners.shape, jnp.int32),
            pltpu.VMEM((lines * peers, width), BF),
            pltpu.VMEM((2 * peers, lines * width), BF),
            pltpu.VMEM((cap, lines * width), BF),
            pltpu.SemaphoreType.DMA((2,)),
        ],
        compiler_params=pltpu.CompilerParams(vmem_limit_bytes=62 << 20),
        name="request_table",
    )(owners, rows)


def count_kernel(idx_ref, out_ref):
    groups = idx_ref.shape[0]
    uppers = out_ref.shape[1] // 256
    target = iota((1, 256), 1) >> 4
    rows_upper = iota((uppers * 16, 256), 0)
    rows_lower = iota((256, 256), 0)

    def group(g, carry):
        value = idx_ref[pl.ds(g, 1), :]
        code = jnp.where(value >= 0, (value >> 8) * 16 + target, -1)
        found = lax.dot_general(
            one_hot(rows_upper == code),
            one_hot(rows_lower == (value & 255)),
            NT,
            preferred_element_type=F32,
        ).astype(BF)
        for u in range(uppers):
            out_ref[chunk(g, 16), u * 256:(u + 1) * 256] = found[u * 16:(u + 1) * 16, :]
        return carry

    lax.fori_loop(0, groups, group, 0, unroll=4)


def neighbour_counts(lists, sources, block_groups=16):
    targets, places = lists.shape
    padded = jnp.pad(lists, ((0, 0), (0, 16 - places)), constant_values=-1)
    return pl.pallas_call(
        count_kernel,
        grid=(targets // 16 // block_groups,),
        in_specs=[pl.BlockSpec((block_groups, 256), lambda i: (i, 0))],
        out_specs=pl.BlockSpec((block_groups * 16, sources), lambda i: (i, 0)),
        out_shape=jax.ShapeDtypeStruct((targets, sources), BF),
        compiler_params=pltpu.CompilerParams(vmem_limit_bytes=40 << 20),
        cost_estimate=pl.CostEstimate(
            flops=512 * targets * sources,
            bytes_accessed=2 * targets * sources,
            transcendentals=0,
        ),
        name="neighbour_counts",
    )(padded.reshape(targets // 16, 256))


def pick_rows(idx_ref, first, count, low, high, out_ref):
    half = low.shape[1]
    line = iota((8, half), 0)

    def some(i, carry):
        begin = pl.multiple_of(i * 16, 16)
        lows, highs = [], []
        for h in range(2):
            for j in range(8):
                row = idx_ref[first + begin + h * 8 + j]
                new_low = jnp.broadcast_to(low[pl.ds(row, 1), :], (8, half))
                new_high = jnp.broadcast_to(high[pl.ds(row, 1), :], (8, half))
                if j == 0:
                    got_low, got_high = new_low, new_high
                else:
                    got_low = jnp.where(line == j, new_low, got_low)
                    got_high = jnp.where(line == j, new_high, got_high)
            lows.append(got_low)
            highs.append(got_high)
        out_ref[pl.ds(begin, 16), :half] = jnp.concatenate(lows, axis=0).astype(BF)
        out_ref[pl.ds(begin, 16), half:] = jnp.concatenate(highs, axis=0).astype(BF)
        return carry

    lax.fori_loop(0, count // 16, some, 0, unroll=16)


def piece_copies(source_ref, held, sems):
    rows = held.shape[0] // sems.shape[0]
    return [
        pltpu.make_async_copy(
            source_ref.at[pl.ds(p * rows, rows), :], held.at[pl.ds(p * rows, rows), :], sems.at[p]
        )
        for p in range(sems.shape[0])
    ]


def widen(held, low, high, copies):
    pieces = max(1, len(copies))
    rows = held.shape[0] // pieces
    half = low.shape[1]
    for p in range(pieces):
        if copies:
            copies[p].wait()

        def some(i, carry):
            part = pl.ds(pl.multiple_of(p * rows + i * 128, 128), 128)
            low[part, :] = held[part, :half].astype(F32)
            high[part, :] = held[part, half:].astype(F32)
            return carry

        lax.fori_loop(0, rows // 128, some, 0, unroll=2)


def gather_kernel(idx_hbm, table_ref, out_ref, idx_ref, held, low, high, sems, idx_sem):
    step = pl.program_id(0)
    rows = out_ref.shape[0]

    @pl.when(step == 0)
    def _():
        copies = piece_copies(table_ref, held, sems)
        idx_copy = pltpu.make_async_copy(idx_hbm, idx_ref, idx_sem)
        for copy in [idx_copy] + copies:
            copy.start()
        widen(held, low, high, copies)
        idx_copy.wait()

    pick_rows(idx_ref, step * rows, rows, low, high, out_ref)


def gather_rows(table, idx, rows=1024):
    total = idx.shape[0]
    own_rows, width = table.shape
    return pl.pallas_call(
        gather_kernel,
        grid=(total // rows,),
        in_specs=[pl.BlockSpec(memory_space=pltpu.HBM)] * 2,
        out_specs=pl.BlockSpec((rows, width), lambda i: (i, 0)),
        scratch_shapes=[
            pltpu.SMEM((total,), jnp.int32),
            pltpu.VMEM((own_rows, width), BF),
            pltpu.VMEM((own_rows, width // 2), F32),
            pltpu.VMEM((own_rows, width // 2), F32),
            pltpu.SemaphoreType.DMA((8,)),
            pltpu.SemaphoreType.DMA,
        ],
        out_shape=pltpu.HBM((total, width), BF),
        compiler_params=pltpu.CompilerParams(vmem_limit_bytes=62 << 20),
        name="gather_rows",
    )(idx, table)


def layer_kernel(list_width, idx_ref, spot_ref, arrived_ref, counts_ref, ws_ref, wn_ref,
                 *refs):
    part_refs, (both_ref, low, high, frontier, counts, count_sems) = refs[:-6], refs[-6:]
    step = pl.program_id(0)
    block = both_ref.shape[0]
    width = arrived_ref.shape[1]

    def count_copy(b):
        return pltpu.make_async_copy(
            counts_ref.at[pl.ds(b * block, block), :],
            counts.at[pl.ds(b * block, block), :],
            count_sems.at[b],
        )

    @pl.when(step == 0)
    def _():
        for b in range(counts.shape[0] // block):
            count_copy(b).start()
        widen(arrived_ref, low, high, [])
        pick_rows(idx_ref, 0, frontier.shape[0], low, high, frontier)

    count_copy(step).wait()
    here = chunk(step, block)
    total = jnp.dot(counts[here, :], frontier[...], preferred_element_type=F32)
    own = frontier[here, :]
    mean = (total / list_width).astype(BF)
    both_ref[:, :width] = own
    both_ref[:, width:] = mean
    share = part_refs[0].shape[1]
    quarters = ws_ref.shape[1] // share
    made = jnp.dot(own, ws_ref[...], preferred_element_type=F32)
    made = (made + jnp.dot(mean, wn_ref[...], preferred_element_type=F32)).astype(BF)
    for q in range(quarters):
        d = lax.rem(q + quarters - spot_ref[0], quarters)
        for e in range(quarters):
            for half in range(2):
                @pl.when((d == e) & (step // (pl.num_programs(0) // 2) == half))
                def _():
                    part_refs[2 * e + half][...] = made[:, q * share:(q + 1) * share]


def first_layer(idx, spot, arrived, counts, w_self, w_near, list_width, quarters, block=1024):
    targets, positions = counts.shape
    slots, width = arrived.shape
    share = w_self.shape[1] // quarters
    steps = targets // block
    middle = steps // 2

    def full(shape):
        return pl.BlockSpec(shape, lambda i, *s: (0, 0))

    halves = [
        pl.BlockSpec((block, share), lambda i, *s: (jnp.minimum(i, middle - 1), 0)),
        pl.BlockSpec((block, share), lambda i, *s: (jnp.maximum(i - middle, 0), 0)),
    ]
    return pl.pallas_call(
        functools.partial(layer_kernel, list_width),
        grid_spec=pltpu.PrefetchScalarGridSpec(
            num_scalar_prefetch=2,
            grid=(steps,),
            in_specs=[
                pl.BlockSpec(memory_space=pltpu.VMEM),
                pl.BlockSpec(memory_space=pltpu.HBM),
                full(w_self.shape),
                full(w_near.shape),
            ],
            out_specs=halves * quarters + [pl.BlockSpec((block, 2 * width), lambda i, *s: (i, 0))],
            scratch_shapes=[
                pltpu.VMEM((slots, width // 2), F32),
                pltpu.VMEM((slots, width // 2), F32),
                pltpu.VMEM((positions, width), BF),
                pltpu.VMEM((targets, positions), BF),
                pltpu.SemaphoreType.DMA((steps,)),
            ],
        ),
        out_shape=[jax.ShapeDtypeStruct((targets // 2, share), BF)] * 2
        + [pltpu.VMEM((targets // 2, share), BF)] * (2 * quarters - 2)
        + [jax.ShapeDtypeStruct((targets, 2 * width), BF)],
        compiler_params=pltpu.CompilerParams(vmem_limit_bytes=54 << 20),
        name="first_layer",
    )(idx, spot, arrived, counts, w_self, w_near)


def add_kernel(left, right, out_ref):
    out_ref[...] = (left[...].astype(F32) + right[...].astype(F32)).astype(BF)


def added(left, right):
    return pl.pallas_call(
        add_kernel,
        in_specs=[pl.BlockSpec(memory_space=pltpu.VMEM)] * 2,
        out_specs=pl.BlockSpec(memory_space=pltpu.VMEM),
        out_shape=jax.ShapeDtypeStruct(left.shape, BF),
        compiler_params=pltpu.CompilerParams(vmem_limit_bytes=16 << 20),
        name="added",
    )(left, right)


def slope_kernel(base, up, down, d_ref, hidden_ref, slope_ref):
    active = base[...] + up[...].astype(F32) + down[...].astype(F32)
    below = 1.0 + jnp.exp(-active)
    sigmoid = 1.0 / below
    hidden_ref[...] = (active / below).astype(BF)
    slope_ref[...] = (d_ref[...] * (sigmoid * (1.0 + active * (1.0 - sigmoid)))).astype(BF)


def hidden_and_slope(base, up, down, d_hidden, first, block=512):
    rows, share = base.shape
    place = pl.BlockSpec((block, share), lambda i: (i, 0))
    return pl.pallas_call(
        slope_kernel,
        grid=(rows // block,),
        in_specs=[place] * 3
        + [
            pl.BlockSpec((block, share), lambda i: (i + first // block, 0)),
        ],
        out_specs=[place, place],
        out_shape=[jax.ShapeDtypeStruct((rows, share), BF)] * 2,
        compiler_params=pltpu.CompilerParams(vmem_limit_bytes=16 << 20),
        name="hidden_and_slope",
    )(base, up, down, d_hidden)


def pack_kernel(core_ref, *refs):
    *value_refs, keep_ref, give_ref = refs
    chips, _, share = keep_ref.shape
    first = 0
    for ref in value_refs:
        rows = ref.shape[0] // (2 * chips)
        for c in range(ref.shape[1] // share):
            cols = slice(c * share, (c + 1) * share)
            for out_ref, core in ((keep_ref, core_ref[0]), (give_ref, 1 - core_ref[0])):
                block = ref[chunk(core, chips * rows), cols]
                out_ref[:, first:first + rows, :] = block.reshape(chips, rows, share)
            first += rows


def pack_shards(core, values, chips, share):
    rows = sum(v.size for v in values) // (2 * chips * share)
    return pl.pallas_call(
        pack_kernel,
        in_specs=[pl.BlockSpec(memory_space=pltpu.SMEM)]
        + [pl.BlockSpec(memory_space=pltpu.VMEM)] * len(values),
        out_specs=[pl.BlockSpec(memory_space=pltpu.VMEM)] * 2,
        out_shape=[jax.ShapeDtypeStruct((chips, rows, share), BF)] * 2,
        compiler_params=pltpu.CompilerParams(vmem_limit_bytes=16 << 20),
        name="pack_shards",
    )(core, *values)


def finish_kernel(spot_ref, mine_ref, other_ref, ws_ref, wn_ref, vs_ref, vn_ref):
    peers, shard, share = mine_ref.shape
    feats = ws_ref.shape[0]
    some = feats // peers
    order = (0, 1, 3, 2)
    v_rows = shard - some * len(order)
    front = spot_ref[1] == 0

    def halves(first, count):
        part = slice(first, first + count)
        mine = mine_ref[:, part, :].astype(F32).reshape(peers * count, share)
        other = other_ref[:, part, :].astype(F32).reshape(peers * count, share)
        return jnp.where(front, mine, other), jnp.where(front, other, mine)

    for place, d in enumerate(order):
        cols = chunk(lax.rem(spot_ref[0] + d, len(order)), share)
        ws_ref[:, cols], wn_ref[:, cols] = halves(v_rows + place * some, some)
    for half, block in enumerate(halves(0, v_rows)):
        for e in range(len(order) // 2):
            cols = slice((2 * half + e) * share, (2 * half + e + 1) * share)
            vs_ref[:, cols] = block[2 * e * share:(2 * e + 1) * share]
            vn_ref[:, cols] = block[(2 * e + 1) * share:(2 * e + 2) * share]


def join_kernel(keep, got, keep_far, got_far, out_ref):
    rows = keep.shape[1]
    out_ref[:, :rows, :] = (keep[...].astype(F32) + got[...].astype(F32)).astype(BF)
    out_ref[:, rows:, :] = (keep_far[...].astype(F32) + got_far[...].astype(F32)).astype(BF)


def joined(keep, got, keep_far, got_far):
    chips, rows, share = keep.shape
    return pl.pallas_call(
        join_kernel,
        in_specs=[pl.BlockSpec(memory_space=pltpu.VMEM)] * 4,
        out_specs=pl.BlockSpec(memory_space=pltpu.VMEM),
        out_shape=jax.ShapeDtypeStruct((chips, rows + keep_far.shape[1], share), BF),
        compiler_params=pltpu.CompilerParams(vmem_limit_bytes=16 << 20),
        name="joined",
    )(keep, got, keep_far, got_far)


def spread_kernel(got_ref, out_ref):
    total = jnp.sum(got_ref[...].astype(F32), axis=0).astype(BF)
    for chip in range(out_ref.shape[0]):
        out_ref[chip] = total


def sum_and_spread(got):
    return pl.pallas_call(
        spread_kernel,
        in_specs=[pl.BlockSpec(memory_space=pltpu.VMEM)],
        out_specs=pl.BlockSpec(memory_space=pltpu.VMEM),
        out_shape=jax.ShapeDtypeStruct(got.shape, BF),
        compiler_params=pltpu.CompilerParams(vmem_limit_bytes=16 << 20),
        name="sum_and_spread",
    )(got)


def body(
    feature_table,
    owner_ids,
    row_ids,
    near_first,
    near_second,
    w_self,
    w_near,
    bias_hidden,
    v_self,
    v_near,
    cotangent,
):
    peers = lax.axis_size("wide")
    quarters = lax.axis_size("blk")
    z = lax.axis_index("blk")
    core = lax.axis_index("wide") % 2
    frontier_count = row_ids.shape[0]
    cap = 2 * frontier_count // peers
    targets, first_width = near_first.shape
    seeds, second_width = near_second.shape
    feats, hidden_units = w_self.shape
    share = hidden_units // quarters

    def shift(value, by):
        return lax.ppermute(value, "blk", [(i, (i + by) % quarters) for i in range(quarters)])

    def exchange(value):
        return lax.all_to_all(value, "wide", split_axis=0, concat_axis=0, tiled=True)

    with jax.named_scope("requests"):
        requests, flat = request_table(
            owner_ids.reshape(frontier_count // 128, 128),
            row_ids.reshape(frontier_count // 128, 128),
            peers,
            cap,
        )
        wanted = exchange(requests).reshape(-1)
        flat = flat.reshape(-1)
    with jax.named_scope("rows"):
        found = gather_rows(feature_table, wanted)
        arrived = exchange(found.reshape(peers, cap, feats)).reshape(peers * cap, feats)
    with jax.named_scope("beside_rows"):
        counts_first = neighbour_counts(near_first, frontier_count)
        counts_second = neighbour_counts(near_second, targets)
        d_self = lax.dot_general(cotangent, v_self, NT, preferred_element_type=F32)
        d_mean = lax.dot_general(cotangent, v_near, NT, preferred_element_type=F32) / second_width
        d_upper = d_mean.astype(BF)
        d_lower = (d_mean - d_upper.astype(F32)).astype(BF)
        spread = lax.dot_general(
            counts_second,
            jnp.concatenate([d_upper, d_lower], axis=1),
            TN,
            preferred_element_type=F32,
        )
        d_hidden = spread[:, :share] + spread[:, share:]
        d_hidden = d_hidden + jnp.pad(d_self, ((0, targets - seeds), (0, 0)))
        arrived, counts_first, counts_second, d_hidden = lax.optimization_barrier(
            (arrived, counts_first, counts_second, d_hidden)
        )
    with jax.named_scope("first_layer"):
        *parts, both = first_layer(
            flat,
            jnp.full((1,), z, jnp.int32),
            arrived,
            counts_first,
            w_self,
            w_near,
            first_width,
            quarters,
        )
    with jax.named_scope("pre_act_exchange"):
        own, above, far, below = [parts[2 * d:2 * d + 2] for d in range(quarters)]
        passing_up = shift(far[0], 1)
        passing_down = shift(far[1], -1)
        down_0 = shift(below[0], -1)
        up_1 = shift(above[1], 1)
        up_0 = shift(added(above[0], passing_up), 1)
        down_1 = shift(added(below[1], passing_down), -1)
        hiddens, slopes = [], []
        for half, (up, down) in enumerate([(up_0, down_0), (up_1, down_1)]):
            base = own[half].astype(F32) + bias_hidden.astype(F32)
            hidden, slope = hidden_and_slope(base, up, down, d_hidden, half * targets // 2)
            hiddens.append(hidden)
            slopes.append(slope)
    with jax.named_scope("slope_exchange"):
        from_down = [shift(slope, 1) for slope in slopes]
        from_up = [shift(slope, -1) for slope in slopes]
        from_far = [shift(from_down[0], 1), shift(from_up[1], -1)]
        from_down, from_up, from_far = [jnp.concatenate(v) for v in (from_down, from_up, from_far)]

    def grad_w(slope_part):
        return lax.dot_general(both, slope_part, TN, preferred_element_type=F32).astype(BF)

    def swap(value):
        return lax.ppermute(value, "wide", [(i, i ^ 1) for i in range(peers)])

    def between_chips(value):
        return lax.all_to_all(
            value,
            "wide",
            split_axis=0,
            concat_axis=0,
            axis_index_groups=[list(range(c, peers, 2)) for c in range(2)],
            tiled=True,
        )

    with jax.named_scope("second_layer"):
        hidden = jnp.concatenate(hiddens)
        seed_hidden = hidden[:seeds]
        second_mean = (
            jnp.dot(counts_second, hidden, preferred_element_type=F32) / second_width
        ).astype(BF)
        grad_v = jnp.concatenate(
            [
                lax.dot_general(seed_hidden, cotangent, TN, preferred_element_type=F32),
                lax.dot_general(second_mean, cotangent, TN, preferred_element_type=F32),
            ]
        ).astype(BF)
        grad_v = jnp.concatenate([grad_v[:, c * share:(c + 1) * share] for c in range(quarters)])
        partial_out = jnp.dot(seed_hidden, v_self, preferred_element_type=F32) + jnp.dot(
            second_mean, v_near, preferred_element_type=F32
        )

        def out_part(d):
            return lax.dynamic_slice_in_dim(partial_out, (z + d) % quarters * share, share, 1)

        outs = [shift(out_part(d).astype(BF), d) for d in range(1, quarters)]
    with jax.named_scope("gradients"):
        near_two = grad_w(jnp.concatenate([from_up, from_down], axis=1))
        chips = peers // 2
        near_two, outs[0] = lax.optimization_barrier((near_two, outs[0]))
        keep, give = pack_shards(
            core.reshape(1), [grad_v, grad_w(jnp.concatenate(slopes)), near_two], chips, share
        )
        keep_far, give_far = pack_shards(core.reshape(1), [grad_w(from_far)], chips, share)
        sums = between_chips(joined(keep, swap(give), keep_far, swap(give_far)))
        mine = between_chips(sum_and_spread(sums))
        mine, *outs = lax.optimization_barrier((mine, *outs))
        other = swap(mine)
        seed_out = out_part(0)
        for part in outs:
            seed_out = seed_out + part.astype(F32)
        seed_out = seed_out.astype(BF)
        grads = pl.pallas_call(
            finish_kernel,
            in_specs=[pl.BlockSpec(memory_space=pltpu.SMEM)] + [pl.BlockSpec(memory_space=pltpu.VMEM)] * 2,
            out_specs=[pl.BlockSpec(memory_space=pltpu.VMEM)] * 4,
            out_shape=[jax.ShapeDtypeStruct((feats, hidden_units), F32)] * 2
            + [jax.ShapeDtypeStruct((share, hidden_units), F32)] * 2,
            compiler_params=pltpu.CompilerParams(vmem_limit_bytes=16 << 20),
            name="finish",
        )(jnp.stack([z, core]).astype(jnp.int32), mine, other)
    return (seed_out, *grads)


def solution(mesh):
    placed = (
        P("wide", "blk"),
        P("wide", None),
        P("wide"),
        P("wide", None),
        P("wide", None),
        P("blk", None),
        P("blk", None),
        P("blk"),
        P("blk", None),
        P("blk", None),
        P("wide", None),
    )
    return jax.shard_map(
        body,
        mesh=mesh,
        in_specs=placed,
        out_specs=(
            P("wide", "blk"),
            P("blk", None),
            P("blk", None),
            P("blk", None),
            P("blk", None),
        ),
        check_vma=False,
    )
```

```python
import functools

import jax
import jax.numpy as jnp
from jax import lax
from jax.experimental import pallas as pl
from jax.experimental.pallas import tpu as pltpu
from jax.sharding import PartitionSpec as P

BF = jnp.bfloat16
F32 = jnp.float32
NT = (((1,), (1,)), ((), ()))
TN = (((0,), (0,)), ((), ()))


def iota(shape, axis):
    return lax.broadcasted_iota(jnp.int32, shape, axis)


def one_hot(hit):
    return jnp.where(hit, 1.0, 0.0).astype(BF)


def chunk(index, size):
    return pl.ds(pl.multiple_of(index * size, size), size)


def request_kernel(own_hbm, row_hbm, req_ref, flat_ref, own_ref, row_ref, hot, picked, spots, sems):
    peers, _, cap = req_ref.shape
    lines, width = own_ref.shape
    copies = [
        pltpu.make_async_copy(own_hbm, own_ref, sems.at[0]),
        pltpu.make_async_copy(row_hbm, row_ref, sems.at[1]),
    ]
    for copy in copies:
        copy.start()
    for copy in copies:
        copy.wait()
    names = iota((peers, width), 0)
    for r in range(lines):
        hot[r * peers:(r + 1) * peers, :] = one_hot(own_ref[r:r + 1, :] == names)
    before = one_hot(iota((width, 2 * width), 0) <= iota((width, 2 * width), 1))
    counted = jnp.dot(hot[...], before, preferred_element_type=F32)
    base = jnp.full((peers, width), -1.0, F32)
    slots = iota((cap, width), 0)
    for r in range(lines):
        here = counted[r * peers:(r + 1) * peers]
        hit = own_ref[r:r + 1, :] == names
        slot = jnp.sum(jnp.where(hit, here[:, :width] + base, 0.0), axis=0, keepdims=True)
        slot = slot.astype(jnp.int32)
        base = base + here[:, width:]
        flat_ref[r:r + 1, :] = own_ref[r:r + 1, :] * cap + slot
        cols = slice(r * width, (r + 1) * width)
        row = row_ref[r:r + 1, :]
        upper = jnp.broadcast_to((row >> 6).astype(F32), (peers, width))
        lower = jnp.broadcast_to((row & 63).astype(F32), (peers, width))
        picked[:peers, cols] = jnp.where(hit, upper, 0.0).astype(BF)
        picked[peers:, cols] = jnp.where(hit, lower, 0.0).astype(BF)
        spots[:, cols] = one_hot(slots == slot)
    found = lax.dot_general(picked[...], spots[...], NT, preferred_element_type=F32)
    req_ref[:, 0, :] = (found[:peers] * 64.0 + found[peers:]).astype(jnp.int32)


def request_table(owners, rows, peers, cap):
    lines, width = owners.shape
    return pl.pallas_call(
        request_kernel,
        out_shape=(
            jax.ShapeDtypeStruct((peers, 1, cap), jnp.int32),
            jax.ShapeDtypeStruct(owners.shape, jnp.int32),
        ),
        in_specs=[pl.BlockSpec(memory_space=pltpu.HBM)] * 2,
        scratch_shapes=[
            pltpu.VMEM(owners.shape, jnp.int32),
            pltpu.VMEM(owners.shape, jnp.int32),
            pltpu.VMEM((lines * peers, width), BF),
            pltpu.VMEM((2 * peers, lines * width), BF),
            pltpu.VMEM((cap, lines * width), BF),
            pltpu.SemaphoreType.DMA((2,)),
        ],
        compiler_params=pltpu.CompilerParams(vmem_limit_bytes=62 << 20),
        name="request_table",
    )(owners, rows)


def count_kernel(idx_ref, out_ref):
    groups = idx_ref.shape[0]
    uppers = out_ref.shape[1] // 256
    target = iota((1, 256), 1) >> 4
    rows_upper = iota((uppers * 16, 256), 0)
    rows_lower = iota((256, 256), 0)

    def group(g, carry):
        value = idx_ref[pl.ds(g, 1), :]
        code = jnp.where(value >= 0, (value >> 8) * 16 + target, -1)
        found = lax.dot_general(
            one_hot(rows_upper == code),
            one_hot(rows_lower == (value & 255)),
            NT,
            preferred_element_type=F32,
        ).astype(BF)
        for u in range(uppers):
            out_ref[chunk(g, 16), u * 256:(u + 1) * 256] = found[u * 16:(u + 1) * 16, :]
        return carry

    lax.fori_loop(0, groups, group, 0, unroll=4)


def neighbour_counts(lists, sources, block_groups=16):
    targets, places = lists.shape
    padded = jnp.pad(lists, ((0, 0), (0, 16 - places)), constant_values=-1)
    return pl.pallas_call(
        count_kernel,
        grid=(targets // 16 // block_groups,),
        in_specs=[pl.BlockSpec((block_groups, 256), lambda i: (i, 0))],
        out_specs=pl.BlockSpec((block_groups * 16, sources), lambda i: (i, 0)),
        out_shape=jax.ShapeDtypeStruct((targets, sources), BF),
        compiler_params=pltpu.CompilerParams(vmem_limit_bytes=40 << 20),
        cost_estimate=pl.CostEstimate(
            flops=512 * targets * sources,
            bytes_accessed=2 * targets * sources,
            transcendentals=0,
        ),
        name="neighbour_counts",
    )(padded.reshape(targets // 16, 256))


def pick_rows(idx_ref, first, count, low, high, out_ref):
    half = low.shape[1]
    line = iota((8, half), 0)

    def some(i, carry):
        begin = pl.multiple_of(i * 16, 16)
        lows, highs = [], []
        for h in range(2):
            for j in range(8):
                row = idx_ref[first + begin + h * 8 + j]
                new_low = jnp.broadcast_to(low[pl.ds(row, 1), :], (8, half))
                new_high = jnp.broadcast_to(high[pl.ds(row, 1), :], (8, half))
                if j == 0:
                    got_low, got_high = new_low, new_high
                else:
                    got_low = jnp.where(line == j, new_low, got_low)
                    got_high = jnp.where(line == j, new_high, got_high)
            lows.append(got_low)
            highs.append(got_high)
        out_ref[pl.ds(begin, 16), :half] = jnp.concatenate(lows, axis=0).astype(BF)
        out_ref[pl.ds(begin, 16), half:] = jnp.concatenate(highs, axis=0).astype(BF)
        return carry

    lax.fori_loop(0, count // 16, some, 0, unroll=16)


def piece_copies(source_ref, held, sems):
    rows = held.shape[0] // sems.shape[0]
    return [
        pltpu.make_async_copy(
            source_ref.at[pl.ds(p * rows, rows), :], held.at[pl.ds(p * rows, rows), :], sems.at[p]
        )
        for p in range(sems.shape[0])
    ]


def widen(held, low, high, copies):
    pieces = max(1, len(copies))
    rows = held.shape[0] // pieces
    half = low.shape[1]
    for p in range(pieces):
        if copies:
            copies[p].wait()

        def some(i, carry):
            part = pl.ds(pl.multiple_of(p * rows + i * 128, 128), 128)
            low[part, :] = held[part, :half].astype(F32)
            high[part, :] = held[part, half:].astype(F32)
            return carry

        lax.fori_loop(0, rows // 128, some, 0, unroll=2)


def gather_kernel(idx_hbm, table_ref, out_ref, idx_ref, held, low, high, sems, idx_sem):
    step = pl.program_id(0)
    rows = out_ref.shape[0]

    @pl.when(step == 0)
    def _():
        copies = piece_copies(table_ref, held, sems)
        idx_copy = pltpu.make_async_copy(idx_hbm, idx_ref, idx_sem)
        for copy in [idx_copy] + copies:
            copy.start()
        widen(held, low, high, copies)
        idx_copy.wait()

    pick_rows(idx_ref, step * rows, rows, low, high, out_ref)


def gather_rows(table, idx, rows=1024):
    total = idx.shape[0]
    own_rows, width = table.shape
    return pl.pallas_call(
        gather_kernel,
        grid=(total // rows,),
        in_specs=[pl.BlockSpec(memory_space=pltpu.HBM)] * 2,
        out_specs=pl.BlockSpec((rows, width), lambda i: (i, 0)),
        scratch_shapes=[
            pltpu.SMEM((total,), jnp.int32),
            pltpu.VMEM((own_rows, width), BF),
            pltpu.VMEM((own_rows, width // 2), F32),
            pltpu.VMEM((own_rows, width // 2), F32),
            pltpu.SemaphoreType.DMA((8,)),
            pltpu.SemaphoreType.DMA,
        ],
        out_shape=pltpu.HBM((total, width), BF),
        compiler_params=pltpu.CompilerParams(vmem_limit_bytes=62 << 20),
        name="gather_rows",
    )(idx, table)


def layer_kernel(list_width, idx_ref, spot_ref, arrived_ref, counts_ref, ws_ref, wn_ref,
                 *refs):
    part_refs, (both_ref, low, high, frontier, counts, count_sems) = refs[:-6], refs[-6:]
    step = pl.program_id(0)
    block = both_ref.shape[0]
    width = arrived_ref.shape[1]

    def count_copy(b):
        return pltpu.make_async_copy(
            counts_ref.at[pl.ds(b * block, block), :],
            counts.at[pl.ds(b * block, block), :],
            count_sems.at[b],
        )

    @pl.when(step == 0)
    def _():
        for b in range(counts.shape[0] // block):
            count_copy(b).start()
        widen(arrived_ref, low, high, [])
        pick_rows(idx_ref, 0, frontier.shape[0], low, high, frontier)

    count_copy(step).wait()
    here = chunk(step, block)
    total = jnp.dot(counts[here, :], frontier[...], preferred_element_type=F32)
    own = frontier[here, :]
    mean = (total / list_width).astype(BF)
    both_ref[:, :width] = own
    both_ref[:, width:] = mean
    share = part_refs[0].shape[1]
    quarters = ws_ref.shape[1] // share
    made = jnp.dot(own, ws_ref[...], preferred_element_type=F32)
    made = (made + jnp.dot(mean, wn_ref[...], preferred_element_type=F32)).astype(BF)
    for q in range(quarters):
        d = lax.rem(q + quarters - spot_ref[0], quarters)
        for e in range(quarters):
            for half in range(2):
                @pl.when((d == e) & (step // (pl.num_programs(0) // 2) == half))
                def _():
                    part_refs[2 * e + half][...] = made[:, q * share:(q + 1) * share]


def first_layer(idx, spot, arrived, counts, w_self, w_near, list_width, quarters, block=1024):
    targets, positions = counts.shape
    slots, width = arrived.shape
    share = w_self.shape[1] // quarters
    steps = targets // block
    middle = steps // 2

    def full(shape):
        return pl.BlockSpec(shape, lambda i, *s: (0, 0))

    halves = [
        pl.BlockSpec((block, share), lambda i, *s: (jnp.minimum(i, middle - 1), 0)),
        pl.BlockSpec((block, share), lambda i, *s: (jnp.maximum(i - middle, 0), 0)),
    ]
    return pl.pallas_call(
        functools.partial(layer_kernel, list_width),
        grid_spec=pltpu.PrefetchScalarGridSpec(
            num_scalar_prefetch=2,
            grid=(steps,),
            in_specs=[
                pl.BlockSpec(memory_space=pltpu.VMEM),
                pl.BlockSpec(memory_space=pltpu.HBM),
                full(w_self.shape),
                full(w_near.shape),
            ],
            out_specs=halves * quarters + [pl.BlockSpec((block, 2 * width), lambda i, *s: (i, 0))],
            scratch_shapes=[
                pltpu.VMEM((slots, width // 2), F32),
                pltpu.VMEM((slots, width // 2), F32),
                pltpu.VMEM((positions, width), BF),
                pltpu.VMEM((targets, positions), BF),
                pltpu.SemaphoreType.DMA((steps,)),
            ],
        ),
        out_shape=[jax.ShapeDtypeStruct((targets // 2, share), BF)] * 2
        + [pltpu.VMEM((targets // 2, share), BF)] * (2 * quarters - 2)
        + [jax.ShapeDtypeStruct((targets, 2 * width), BF)],
        compiler_params=pltpu.CompilerParams(vmem_limit_bytes=54 << 20),
        name="first_layer",
    )(idx, spot, arrived, counts, w_self, w_near)


def add_kernel(left, right, out_ref):
    out_ref[...] = (left[...].astype(F32) + right[...].astype(F32)).astype(BF)


def added(left, right):
    return pl.pallas_call(
        add_kernel,
        in_specs=[pl.BlockSpec(memory_space=pltpu.VMEM)] * 2,
        out_specs=pl.BlockSpec(memory_space=pltpu.VMEM),
        out_shape=jax.ShapeDtypeStruct(left.shape, BF),
        compiler_params=pltpu.CompilerParams(vmem_limit_bytes=16 << 20),
        name="added",
    )(left, right)


def slope_kernel(base, up, down, d_ref, hidden_ref, slope_ref):
    active = base[...] + up[...].astype(F32) + down[...].astype(F32)
    below = 1.0 + jnp.exp(-active)
    sigmoid = 1.0 / below
    hidden_ref[...] = (active / below).astype(BF)
    slope_ref[...] = (d_ref[...] * (sigmoid * (1.0 + active * (1.0 - sigmoid)))).astype(BF)


def hidden_and_slope(base, up, down, d_hidden, first, block=512):
    rows, share = base.shape
    place = pl.BlockSpec((block, share), lambda i: (i, 0))
    return pl.pallas_call(
        slope_kernel,
        grid=(rows // block,),
        in_specs=[place] * 3
        + [
            pl.BlockSpec((block, share), lambda i: (i + first // block, 0)),
        ],
        out_specs=[place, place],
        out_shape=[jax.ShapeDtypeStruct((rows, share), BF)] * 2,
        compiler_params=pltpu.CompilerParams(vmem_limit_bytes=16 << 20),
        name="hidden_and_slope",
    )(base, up, down, d_hidden)


def pack_kernel(core_ref, *refs):
    *value_refs, keep_ref, give_ref = refs
    chips, _, share = keep_ref.shape
    first = 0
    for ref in value_refs:
        rows = ref.shape[0] // (2 * chips)
        for c in range(ref.shape[1] // share):
            cols = slice(c * share, (c + 1) * share)
            for out_ref, core in ((keep_ref, core_ref[0]), (give_ref, 1 - core_ref[0])):
                block = ref[chunk(core, chips * rows), cols]
                out_ref[:, first:first + rows, :] = block.reshape(chips, rows, share)
            first += rows


def pack_shards(core, values, chips, share):
    rows = sum(v.size for v in values) // (2 * chips * share)
    return pl.pallas_call(
        pack_kernel,
        in_specs=[pl.BlockSpec(memory_space=pltpu.SMEM)]
        + [pl.BlockSpec(memory_space=pltpu.VMEM)] * len(values),
        out_specs=[pl.BlockSpec(memory_space=pltpu.VMEM)] * 2,
        out_shape=[jax.ShapeDtypeStruct((chips, rows, share), BF)] * 2,
        compiler_params=pltpu.CompilerParams(vmem_limit_bytes=16 << 20),
        name="pack_shards",
    )(core, *values)


def finish_kernel(spot_ref, mine_ref, other_ref, ws_ref, wn_ref, vs_ref, vn_ref):
    peers, shard, share = mine_ref.shape
    feats = ws_ref.shape[0]
    some = feats // peers
    order = (0, 1, 3, 2)
    v_rows = shard - some * len(order)
    front = spot_ref[1] == 0

    def halves(first, count):
        part = slice(first, first + count)
        mine = mine_ref[:, part, :].astype(F32).reshape(peers * count, share)
        other = other_ref[:, part, :].astype(F32).reshape(peers * count, share)
        return jnp.where(front, mine, other), jnp.where(front, other, mine)

    for place, d in enumerate(order):
        cols = chunk(lax.rem(spot_ref[0] + d, len(order)), share)
        ws_ref[:, cols], wn_ref[:, cols] = halves(v_rows + place * some, some)
    for half, block in enumerate(halves(0, v_rows)):
        for e in range(len(order) // 2):
            cols = slice((2 * half + e) * share, (2 * half + e + 1) * share)
            vs_ref[:, cols] = block[2 * e * share:(2 * e + 1) * share]
            vn_ref[:, cols] = block[(2 * e + 1) * share:(2 * e + 2) * share]


def join_kernel(keep, got, keep_far, got_far, out_ref):
    rows = keep.shape[1]
    out_ref[:, :rows, :] = (keep[...].astype(F32) + got[...].astype(F32)).astype(BF)
    out_ref[:, rows:, :] = (keep_far[...].astype(F32) + got_far[...].astype(F32)).astype(BF)


def joined(keep, got, keep_far, got_far):
    chips, rows, share = keep.shape
    return pl.pallas_call(
        join_kernel,
        in_specs=[pl.BlockSpec(memory_space=pltpu.VMEM)] * 4,
        out_specs=pl.BlockSpec(memory_space=pltpu.VMEM),
        out_shape=jax.ShapeDtypeStruct((chips, rows + keep_far.shape[1], share), BF),
        compiler_params=pltpu.CompilerParams(vmem_limit_bytes=16 << 20),
        name="joined",
    )(keep, got, keep_far, got_far)


def spread_kernel(got_ref, out_ref):
    total = jnp.sum(got_ref[...].astype(F32), axis=0).astype(BF)
    for chip in range(out_ref.shape[0]):
        out_ref[chip] = total


def sum_and_spread(got):
    return pl.pallas_call(
        spread_kernel,
        in_specs=[pl.BlockSpec(memory_space=pltpu.VMEM)],
        out_specs=pl.BlockSpec(memory_space=pltpu.VMEM),
        out_shape=jax.ShapeDtypeStruct(got.shape, BF),
        compiler_params=pltpu.CompilerParams(vmem_limit_bytes=16 << 20),
        name="sum_and_spread",
    )(got)


def body(
    feature_table,
    owner_ids,
    row_ids,
    near_first,
    near_second,
    w_self,
    w_near,
    bias_hidden,
    v_self,
    v_near,
    cotangent,
):
    peers = lax.axis_size("wide")
    quarters = lax.axis_size("blk")
    z = lax.axis_index("blk")
    core = lax.axis_index("wide") % 2
    frontier_count = row_ids.shape[0]
    cap = 2 * frontier_count // peers
    targets, first_width = near_first.shape
    seeds, second_width = near_second.shape
    feats, hidden_units = w_self.shape
    share = hidden_units // quarters

    def shift(value, by):
        return lax.ppermute(value, "blk", [(i, (i + by) % quarters) for i in range(quarters)])

    def exchange(value):
        return lax.all_to_all(value, "wide", split_axis=0, concat_axis=0, tiled=True)

    with jax.named_scope("requests"):
        requests, flat = request_table(
            owner_ids.reshape(frontier_count // 128, 128),
            row_ids.reshape(frontier_count // 128, 128),
            peers,
            cap,
        )
        wanted = exchange(requests).reshape(-1)
        flat = flat.reshape(-1)
    with jax.named_scope("rows"):
        found = gather_rows(feature_table, wanted)
        arrived = exchange(found.reshape(peers, cap, feats)).reshape(peers * cap, feats)
    with jax.named_scope("beside_rows"):
        counts_first = neighbour_counts(near_first, frontier_count)
        counts_second = neighbour_counts(near_second, targets)
        d_self = lax.dot_general(cotangent, v_self, NT, preferred_element_type=F32)
        d_mean = lax.dot_general(cotangent, v_near, NT, preferred_element_type=F32) / second_width
        d_upper = d_mean.astype(BF)
        d_lower = (d_mean - d_upper.astype(F32)).astype(BF)
        spread = lax.dot_general(
            counts_second,
            jnp.concatenate([d_upper, d_lower], axis=1),
            TN,
            preferred_element_type=F32,
        )
        d_hidden = spread[:, :share] + spread[:, share:]
        d_hidden = d_hidden + jnp.pad(d_self, ((0, targets - seeds), (0, 0)))
        arrived, counts_first, counts_second, d_hidden = lax.optimization_barrier(
            (arrived, counts_first, counts_second, d_hidden)
        )
    with jax.named_scope("first_layer"):
        *parts, both = first_layer(
            flat,
            jnp.full((1,), z, jnp.int32),
            arrived,
            counts_first,
            w_self,
            w_near,
            first_width,
            quarters,
        )
    with jax.named_scope("pre_act_exchange"):
        own, above, far, below = [parts[2 * d:2 * d + 2] for d in range(quarters)]
        passing_up = shift(far[0], 1)
        passing_down = shift(far[1], -1)
        down_0 = shift(below[0], -1)
        up_1 = shift(above[1], 1)
        up_0 = shift(added(above[0], passing_up), 1)
        down_1 = shift(added(below[1], passing_down), -1)
        hiddens, slopes = [], []
        for half, (up, down) in enumerate([(up_0, down_0), (up_1, down_1)]):
            base = own[half].astype(F32) + bias_hidden.astype(F32)
            if half:
                base, _ = lax.optimization_barrier((base, slopes[0]))
            hidden, slope = hidden_and_slope(base, up, down, d_hidden, half * targets // 2)
            hiddens.append(hidden)
            slopes.append(slope)
    with jax.named_scope("slope_exchange"):
        from_down = [shift(slope, 1) for slope in slopes]
        from_up = [shift(slope, -1) for slope in slopes]
        from_far = [shift(from_down[0], 1), shift(from_up[1], -1)]
        from_down, from_up, from_far = [jnp.concatenate(v) for v in (from_down, from_up, from_far)]

    def grad_w(slope_part):
        return lax.dot_general(both, slope_part, TN, preferred_element_type=F32).astype(BF)

    def swap(value):
        return lax.ppermute(value, "wide", [(i, i ^ 1) for i in range(peers)])

    def between_chips(value):
        return lax.all_to_all(
            value,
            "wide",
            split_axis=0,
            concat_axis=0,
            axis_index_groups=[list(range(c, peers, 2)) for c in range(2)],
            tiled=True,
        )

    with jax.named_scope("second_layer"):
        hidden = jnp.concatenate(hiddens)
        seed_hidden = hidden[:seeds]
        second_mean = (
            jnp.dot(counts_second, hidden, preferred_element_type=F32) / second_width
        ).astype(BF)
        grad_v = jnp.concatenate(
            [
                lax.dot_general(seed_hidden, cotangent, TN, preferred_element_type=F32),
                lax.dot_general(second_mean, cotangent, TN, preferred_element_type=F32),
            ]
        ).astype(BF)
        grad_v = jnp.concatenate([grad_v[:, c * share:(c + 1) * share] for c in range(quarters)])
        partial_out = jnp.dot(seed_hidden, v_self, preferred_element_type=F32) + jnp.dot(
            second_mean, v_near, preferred_element_type=F32
        )

        def out_part(d):
            return lax.dynamic_slice_in_dim(partial_out, (z + d) % quarters * share, share, 1)

        outs = [shift(out_part(d).astype(BF), d) for d in range(1, quarters)]
    with jax.named_scope("gradients"):
        near_two = grad_w(jnp.concatenate([from_up, from_down], axis=1))
        chips = peers // 2
        near_two, outs[0] = lax.optimization_barrier((near_two, outs[0]))
        keep, give = pack_shards(
            core.reshape(1), [grad_v, grad_w(jnp.concatenate(slopes)), near_two], chips, share
        )
        keep_far, give_far = pack_shards(core.reshape(1), [grad_w(from_far)], chips, share)
        sums = between_chips(joined(keep, swap(give), keep_far, swap(give_far)))
        mine = between_chips(sum_and_spread(sums))
        mine, *outs = lax.optimization_barrier((mine, *outs))
        other = swap(mine)
        seed_out = out_part(0)
        for part in outs:
            seed_out = seed_out + part.astype(F32)
        seed_out = seed_out.astype(BF)
        grads = pl.pallas_call(
            finish_kernel,
            in_specs=[pl.BlockSpec(memory_space=pltpu.SMEM)] + [pl.BlockSpec(memory_space=pltpu.VMEM)] * 2,
            out_specs=[pl.BlockSpec(memory_space=pltpu.VMEM)] * 4,
            out_shape=[jax.ShapeDtypeStruct((feats, hidden_units), F32)] * 2
            + [jax.ShapeDtypeStruct((share, hidden_units), F32)] * 2,
            compiler_params=pltpu.CompilerParams(vmem_limit_bytes=16 << 20),
            name="finish",
        )(jnp.stack([z, core]).astype(jnp.int32), mine, other)
    return (seed_out, *grads)


def solution(mesh):
    placed = (
        P("wide", "blk"),
        P("wide", None),
        P("wide"),
        P("wide", None),
        P("wide", None),
        P("blk", None),
        P("blk", None),
        P("blk"),
        P("blk", None),
        P("blk", None),
        P("wide", None),
    )
    return jax.shard_map(
        body,
        mesh=mesh,
        in_specs=placed,
        out_specs=(
            P("wide", "blk"),
            P("blk", None),
            P("blk", None),
            P("blk", None),
            P("blk", None),
        ),
        check_vma=False,
    )
```

```python
import functools

import jax
import jax.numpy as jnp
from jax import lax
from jax.experimental import pallas as pl
from jax.experimental.pallas import tpu as pltpu
from jax.sharding import PartitionSpec as P

BF = jnp.bfloat16
F32 = jnp.float32
NT = (((1,), (1,)), ((), ()))
TN = (((0,), (0,)), ((), ()))


def iota(shape, axis):
    return lax.broadcasted_iota(jnp.int32, shape, axis)


def one_hot(hit):
    return jnp.where(hit, 1.0, 0.0).astype(BF)


def chunk(index, size):
    return pl.ds(pl.multiple_of(index * size, size), size)


def request_kernel(own_hbm, row_hbm, req_ref, flat_ref, own_ref, row_ref, hot, picked, spots, sems):
    peers, _, cap = req_ref.shape
    lines, width = own_ref.shape
    copies = [
        pltpu.make_async_copy(own_hbm, own_ref, sems.at[0]),
        pltpu.make_async_copy(row_hbm, row_ref, sems.at[1]),
    ]
    for copy in copies:
        copy.start()
    for copy in copies:
        copy.wait()
    names = iota((peers, width), 0)
    for r in range(lines):
        hot[r * peers:(r + 1) * peers, :] = one_hot(own_ref[r:r + 1, :] == names)
    before = one_hot(iota((width, 2 * width), 0) <= iota((width, 2 * width), 1))
    counted = jnp.dot(hot[...], before, preferred_element_type=F32)
    base = jnp.full((peers, width), -1.0, F32)
    slots = iota((cap, width), 0)
    for r in range(lines):
        here = counted[r * peers:(r + 1) * peers]
        hit = own_ref[r:r + 1, :] == names
        slot = jnp.sum(jnp.where(hit, here[:, :width] + base, 0.0), axis=0, keepdims=True)
        slot = slot.astype(jnp.int32)
        base = base + here[:, width:]
        flat_ref[r:r + 1, :] = own_ref[r:r + 1, :] * cap + slot
        cols = slice(r * width, (r + 1) * width)
        row = row_ref[r:r + 1, :]
        upper = jnp.broadcast_to((row >> 6).astype(F32), (peers, width))
        lower = jnp.broadcast_to((row & 63).astype(F32), (peers, width))
        picked[:peers, cols] = jnp.where(hit, upper, 0.0).astype(BF)
        picked[peers:, cols] = jnp.where(hit, lower, 0.0).astype(BF)
        spots[:, cols] = one_hot(slots == slot)
    found = lax.dot_general(picked[...], spots[...], NT, preferred_element_type=F32)
    req_ref[:, 0, :] = (found[:peers] * 64.0 + found[peers:]).astype(jnp.int32)


def request_table(owners, rows, peers, cap):
    lines, width = owners.shape
    return pl.pallas_call(
        request_kernel,
        out_shape=(
            jax.ShapeDtypeStruct((peers, 1, cap), jnp.int32),
            jax.ShapeDtypeStruct(owners.shape, jnp.int32),
        ),
        in_specs=[pl.BlockSpec(memory_space=pltpu.HBM)] * 2,
        scratch_shapes=[
            pltpu.VMEM(owners.shape, jnp.int32),
            pltpu.VMEM(owners.shape, jnp.int32),
            pltpu.VMEM((lines * peers, width), BF),
            pltpu.VMEM((2 * peers, lines * width), BF),
            pltpu.VMEM((cap, lines * width), BF),
            pltpu.SemaphoreType.DMA((2,)),
        ],
        compiler_params=pltpu.CompilerParams(vmem_limit_bytes=62 << 20),
        name="request_table",
    )(owners, rows)


def count_kernel(idx_ref, out_ref):
    groups = idx_ref.shape[0]
    uppers = out_ref.shape[1] // 256
    target = iota((1, 256), 1) >> 4
    rows_upper = iota((uppers * 16, 256), 0)
    rows_lower = iota((256, 256), 0)

    def group(g, carry):
        value = idx_ref[pl.ds(g, 1), :]
        code = jnp.where(value >= 0, (value >> 8) * 16 + target, -1)
        found = lax.dot_general(
            one_hot(rows_upper == code),
            one_hot(rows_lower == (value & 255)),
            NT,
            preferred_element_type=F32,
        ).astype(BF)
        for u in range(uppers):
            out_ref[chunk(g, 16), u * 256:(u + 1) * 256] = found[u * 16:(u + 1) * 16, :]
        return carry

    lax.fori_loop(0, groups, group, 0, unroll=4)


def neighbour_counts(lists, sources, block_groups=16):
    targets, places = lists.shape
    padded = jnp.pad(lists, ((0, 0), (0, 16 - places)), constant_values=-1)
    return pl.pallas_call(
        count_kernel,
        grid=(targets // 16 // block_groups,),
        in_specs=[pl.BlockSpec((block_groups, 256), lambda i: (i, 0))],
        out_specs=pl.BlockSpec((block_groups * 16, sources), lambda i: (i, 0)),
        out_shape=jax.ShapeDtypeStruct((targets, sources), BF),
        compiler_params=pltpu.CompilerParams(vmem_limit_bytes=40 << 20),
        cost_estimate=pl.CostEstimate(
            flops=512 * targets * sources,
            bytes_accessed=2 * targets * sources,
            transcendentals=0,
        ),
        name="neighbour_counts",
    )(padded.reshape(targets // 16, 256))


def pick_rows(idx_ref, first, count, low, high, out_ref):
    half = low.shape[1]
    line = iota((8, half), 0)

    def some(i, carry):
        begin = pl.multiple_of(i * 16, 16)
        lows, highs = [], []
        for h in range(2):
            for j in range(8):
                row = idx_ref[first + begin + h * 8 + j]
                new_low = jnp.broadcast_to(low[pl.ds(row, 1), :], (8, half))
                new_high = jnp.broadcast_to(high[pl.ds(row, 1), :], (8, half))
                if j == 0:
                    got_low, got_high = new_low, new_high
                else:
                    got_low = jnp.where(line == j, new_low, got_low)
                    got_high = jnp.where(line == j, new_high, got_high)
            lows.append(got_low)
            highs.append(got_high)
        out_ref[pl.ds(begin, 16), :half] = jnp.concatenate(lows, axis=0).astype(BF)
        out_ref[pl.ds(begin, 16), half:] = jnp.concatenate(highs, axis=0).astype(BF)
        return carry

    lax.fori_loop(0, count // 16, some, 0, unroll=16)


def piece_copies(source_ref, held, sems):
    rows = held.shape[0] // sems.shape[0]
    return [
        pltpu.make_async_copy(
            source_ref.at[pl.ds(p * rows, rows), :], held.at[pl.ds(p * rows, rows), :], sems.at[p]
        )
        for p in range(sems.shape[0])
    ]


def widen(held, low, high, copies):
    pieces = max(1, len(copies))
    rows = held.shape[0] // pieces
    half = low.shape[1]
    for p in range(pieces):
        if copies:
            copies[p].wait()

        def some(i, carry):
            part = pl.ds(pl.multiple_of(p * rows + i * 128, 128), 128)
            low[part, :] = held[part, :half].astype(F32)
            high[part, :] = held[part, half:].astype(F32)
            return carry

        lax.fori_loop(0, rows // 128, some, 0, unroll=2)


def gather_kernel(idx_hbm, table_ref, out_ref, idx_ref, held, low, high, sems, idx_sem):
    step = pl.program_id(0)
    rows = out_ref.shape[0]

    @pl.when(step == 0)
    def _():
        copies = piece_copies(table_ref, held, sems)
        idx_copy = pltpu.make_async_copy(idx_hbm, idx_ref, idx_sem)
        for copy in [idx_copy] + copies:
            copy.start()
        widen(held, low, high, copies)
        idx_copy.wait()

    pick_rows(idx_ref, step * rows, rows, low, high, out_ref)


def gather_rows(table, idx, rows=1024):
    total = idx.shape[0]
    own_rows, width = table.shape
    return pl.pallas_call(
        gather_kernel,
        grid=(total // rows,),
        in_specs=[pl.BlockSpec(memory_space=pltpu.HBM)] * 2,
        out_specs=pl.BlockSpec((rows, width), lambda i: (i, 0)),
        scratch_shapes=[
            pltpu.SMEM((total,), jnp.int32),
            pltpu.VMEM((own_rows, width), BF),
            pltpu.VMEM((own_rows, width // 2), F32),
            pltpu.VMEM((own_rows, width // 2), F32),
            pltpu.SemaphoreType.DMA((8,)),
            pltpu.SemaphoreType.DMA,
        ],
        out_shape=pltpu.HBM((total, width), BF),
        compiler_params=pltpu.CompilerParams(vmem_limit_bytes=62 << 20),
        name="gather_rows",
    )(idx, table)


def layer_kernel(list_width, idx_ref, spot_ref, arrived_ref, counts_ref, ws_ref, wn_ref,
                 *refs):
    part_refs, (both_ref, low, high, frontier, counts, count_sems) = refs[:-6], refs[-6:]
    step = pl.program_id(0)
    block = both_ref.shape[0]
    width = arrived_ref.shape[1]

    def count_copy(b):
        return pltpu.make_async_copy(
            counts_ref.at[pl.ds(b * block, block), :],
            counts.at[pl.ds(b * block, block), :],
            count_sems.at[b],
        )

    @pl.when(step == 0)
    def _():
        for b in range(counts.shape[0] // block):
            count_copy(b).start()
        widen(arrived_ref, low, high, [])
        pick_rows(idx_ref, 0, frontier.shape[0], low, high, frontier)

    count_copy(step).wait()
    here = chunk(step, block)
    total = jnp.dot(counts[here, :], frontier[...], preferred_element_type=F32)
    own = frontier[here, :]
    mean = (total / list_width).astype(BF)
    both_ref[:, :width] = own
    both_ref[:, width:] = mean
    share = part_refs[0].shape[1]
    quarters = ws_ref.shape[1] // share
    made = jnp.dot(own, ws_ref[...], preferred_element_type=F32)
    made = (made + jnp.dot(mean, wn_ref[...], preferred_element_type=F32)).astype(BF)
    for q in range(quarters):
        d = lax.rem(q + quarters - spot_ref[0], quarters)
        for e in range(quarters):
            for half in range(2):
                @pl.when((d == e) & (step // (pl.num_programs(0) // 2) == half))
                def _():
                    part_refs[2 * e + half][...] = made[:, q * share:(q + 1) * share]


def first_layer(idx, spot, arrived, counts, w_self, w_near, list_width, quarters, block=1024):
    targets, positions = counts.shape
    slots, width = arrived.shape
    share = w_self.shape[1] // quarters
    steps = targets // block
    middle = steps // 2

    def full(shape):
        return pl.BlockSpec(shape, lambda i, *s: (0, 0))

    halves = [
        pl.BlockSpec((block, share), lambda i, *s: (jnp.minimum(i, middle - 1), 0)),
        pl.BlockSpec((block, share), lambda i, *s: (jnp.maximum(i - middle, 0), 0)),
    ]
    return pl.pallas_call(
        functools.partial(layer_kernel, list_width),
        grid_spec=pltpu.PrefetchScalarGridSpec(
            num_scalar_prefetch=2,
            grid=(steps,),
            in_specs=[
                pl.BlockSpec(memory_space=pltpu.VMEM),
                pl.BlockSpec(memory_space=pltpu.HBM),
                full(w_self.shape),
                full(w_near.shape),
            ],
            out_specs=halves * quarters + [pl.BlockSpec((block, 2 * width), lambda i, *s: (i, 0))],
            scratch_shapes=[
                pltpu.VMEM((slots, width // 2), F32),
                pltpu.VMEM((slots, width // 2), F32),
                pltpu.VMEM((positions, width), BF),
                pltpu.VMEM((targets, positions), BF),
                pltpu.SemaphoreType.DMA((steps,)),
            ],
        ),
        out_shape=[jax.ShapeDtypeStruct((targets // 2, share), BF)] * 2
        + [pltpu.VMEM((targets // 2, share), BF)] * (2 * quarters - 2)
        + [jax.ShapeDtypeStruct((targets, 2 * width), BF)],
        compiler_params=pltpu.CompilerParams(vmem_limit_bytes=54 << 20),
        name="first_layer",
    )(idx, spot, arrived, counts, w_self, w_near)


def add_kernel(left, right, out_ref):
    out_ref[...] = (left[...].astype(F32) + right[...].astype(F32)).astype(BF)


def added(left, right):
    return pl.pallas_call(
        add_kernel,
        in_specs=[pl.BlockSpec(memory_space=pltpu.VMEM)] * 2,
        out_specs=pl.BlockSpec(memory_space=pltpu.VMEM),
        out_shape=jax.ShapeDtypeStruct(left.shape, BF),
        compiler_params=pltpu.CompilerParams(vmem_limit_bytes=16 << 20),
        name="added",
    )(left, right)


def slope_kernel(base, up, down, d_ref, hidden_ref, slope_ref):
    active = base[...] + up[...].astype(F32) + down[...].astype(F32)
    below = 1.0 + jnp.exp(-active)
    sigmoid = 1.0 / below
    hidden_ref[...] = (active / below).astype(BF)
    slope_ref[...] = (d_ref[...] * (sigmoid * (1.0 + active * (1.0 - sigmoid)))).astype(BF)


def hidden_and_slope(base, up, down, d_hidden, first, block=512):
    rows, share = base.shape
    place = pl.BlockSpec((block, share), lambda i: (i, 0))
    return pl.pallas_call(
        slope_kernel,
        grid=(rows // block,),
        in_specs=[place] * 3
        + [
            pl.BlockSpec((block, share), lambda i: (i + first // block, 0)),
        ],
        out_specs=[place, place],
        out_shape=[jax.ShapeDtypeStruct((rows, share), BF)] * 2,
        compiler_params=pltpu.CompilerParams(vmem_limit_bytes=16 << 20),
        name="hidden_and_slope",
    )(base, up, down, d_hidden)


def pack_kernel(core_ref, *refs):
    *value_refs, keep_ref, give_ref = refs
    chips, _, share = keep_ref.shape
    first = 0
    for ref in value_refs:
        rows = ref.shape[0] // (2 * chips)
        for c in range(ref.shape[1] // share):
            cols = slice(c * share, (c + 1) * share)
            for out_ref, core in ((keep_ref, core_ref[0]), (give_ref, 1 - core_ref[0])):
                block = ref[chunk(core, chips * rows), cols]
                out_ref[:, first:first + rows, :] = block.reshape(chips, rows, share)
            first += rows


def pack_shards(core, values, chips, share):
    rows = sum(v.size for v in values) // (2 * chips * share)
    return pl.pallas_call(
        pack_kernel,
        in_specs=[pl.BlockSpec(memory_space=pltpu.SMEM)]
        + [pl.BlockSpec(memory_space=pltpu.VMEM)] * len(values),
        out_specs=[pl.BlockSpec(memory_space=pltpu.VMEM)] * 2,
        out_shape=[jax.ShapeDtypeStruct((chips, rows, share), BF)] * 2,
        compiler_params=pltpu.CompilerParams(vmem_limit_bytes=16 << 20),
        name="pack_shards",
    )(core, *values)


def finish_kernel(spot_ref, mine_ref, other_ref, ws_ref, wn_ref, vs_ref, vn_ref):
    peers, shard, share = mine_ref.shape
    feats = ws_ref.shape[0]
    some = feats // peers
    order = (0, 1, 3, 2)
    v_rows = shard - some * len(order)
    front = spot_ref[1] == 0

    def halves(first, count):
        part = slice(first, first + count)
        mine = mine_ref[:, part, :].astype(F32).reshape(peers * count, share)
        other = other_ref[:, part, :].astype(F32).reshape(peers * count, share)
        return jnp.where(front, mine, other), jnp.where(front, other, mine)

    for place, d in enumerate(order):
        cols = chunk(lax.rem(spot_ref[0] + d, len(order)), share)
        ws_ref[:, cols], wn_ref[:, cols] = halves(v_rows + place * some, some)
    for half, block in enumerate(halves(0, v_rows)):
        for e in range(len(order) // 2):
            cols = slice((2 * half + e) * share, (2 * half + e + 1) * share)
            vs_ref[:, cols] = block[2 * e * share:(2 * e + 1) * share]
            vn_ref[:, cols] = block[(2 * e + 1) * share:(2 * e + 2) * share]


def join_kernel(keep, got, keep_far, got_far, out_ref):
    rows = keep.shape[1]
    out_ref[:, :rows, :] = (keep[...].astype(F32) + got[...].astype(F32)).astype(BF)
    out_ref[:, rows:, :] = (keep_far[...].astype(F32) + got_far[...].astype(F32)).astype(BF)


def joined(keep, got, keep_far, got_far):
    chips, rows, share = keep.shape
    return pl.pallas_call(
        join_kernel,
        in_specs=[pl.BlockSpec(memory_space=pltpu.VMEM)] * 4,
        out_specs=pl.BlockSpec(memory_space=pltpu.VMEM),
        out_shape=jax.ShapeDtypeStruct((chips, rows + keep_far.shape[1], share), BF),
        compiler_params=pltpu.CompilerParams(vmem_limit_bytes=16 << 20),
        name="joined",
    )(keep, got, keep_far, got_far)


def spread_kernel(got_ref, out_ref):
    total = jnp.sum(got_ref[...].astype(F32), axis=0).astype(BF)
    for chip in range(out_ref.shape[0]):
        out_ref[chip] = total


def sum_and_spread(got):
    return pl.pallas_call(
        spread_kernel,
        in_specs=[pl.BlockSpec(memory_space=pltpu.VMEM)],
        out_specs=pl.BlockSpec(memory_space=pltpu.VMEM),
        out_shape=jax.ShapeDtypeStruct(got.shape, BF),
        compiler_params=pltpu.CompilerParams(vmem_limit_bytes=16 << 20),
        name="sum_and_spread",
    )(got)


def body(
    feature_table,
    owner_ids,
    row_ids,
    near_first,
    near_second,
    w_self,
    w_near,
    bias_hidden,
    v_self,
    v_near,
    cotangent,
):
    peers = lax.axis_size("wide")
    quarters = lax.axis_size("blk")
    z = lax.axis_index("blk")
    core = lax.axis_index("wide") % 2
    frontier_count = row_ids.shape[0]
    cap = 2 * frontier_count // peers
    targets, first_width = near_first.shape
    seeds, second_width = near_second.shape
    feats, hidden_units = w_self.shape
    share = hidden_units // quarters

    def shift(value, by):
        return lax.ppermute(value, "blk", [(i, (i + by) % quarters) for i in range(quarters)])

    def exchange(value):
        return lax.all_to_all(value, "wide", split_axis=0, concat_axis=0, tiled=True)

    with jax.named_scope("requests"):
        requests, flat = request_table(
            owner_ids.reshape(frontier_count // 128, 128),
            row_ids.reshape(frontier_count // 128, 128),
            peers,
            cap,
        )
        wanted = exchange(requests).reshape(-1)
        flat = flat.reshape(-1)
    with jax.named_scope("rows"):
        found = gather_rows(feature_table, wanted)
        arrived = exchange(found.reshape(peers, cap, feats)).reshape(peers * cap, feats)
    with jax.named_scope("beside_rows"):
        counts_first = neighbour_counts(near_first, frontier_count)
        counts_second = neighbour_counts(near_second, targets)
        d_self = lax.dot_general(cotangent, v_self, NT, preferred_element_type=F32)
        d_mean = lax.dot_general(cotangent, v_near, NT, preferred_element_type=F32) / second_width
        d_upper = d_mean.astype(BF)
        d_lower = (d_mean - d_upper.astype(F32)).astype(BF)
        spread = lax.dot_general(
            counts_second,
            jnp.concatenate([d_upper, d_lower], axis=1),
            TN,
            preferred_element_type=F32,
        )
        d_hidden = spread[:, :share] + spread[:, share:]
        d_hidden = d_hidden + jnp.pad(d_self, ((0, targets - seeds), (0, 0)))
        arrived, counts_first, counts_second, d_hidden = lax.optimization_barrier(
            (arrived, counts_first, counts_second, d_hidden)
        )
    with jax.named_scope("first_layer"):
        *parts, both = first_layer(
            flat,
            jnp.full((1,), z, jnp.int32),
            arrived,
            counts_first,
            w_self,
            w_near,
            first_width,
            quarters,
        )
    with jax.named_scope("pre_act_exchange"):
        own, above, far, below = [parts[2 * d:2 * d + 2] for d in range(quarters)]
        passing_up = shift(far[0], 1)
        passing_down = shift(far[1], -1)
        down_0 = shift(below[0], -1)
        first = added(above[0], passing_up)
        up_0 = shift(first, 1)
        passing_down, _ = lax.optimization_barrier((passing_down, first))
        second, after = lax.optimization_barrier((added(below[1], passing_down), above[1]))
        down_1 = shift(second, -1)
        up_1 = shift(after, 1)
        hiddens, slopes = [], []
        for half, (up, down) in enumerate([(up_0, down_0), (up_1, down_1)]):
            base = own[half].astype(F32) + bias_hidden.astype(F32)
            if half:
                base, _ = lax.optimization_barrier((base, slopes[0]))
            hidden, slope = hidden_and_slope(base, up, down, d_hidden, half * targets // 2)
            hiddens.append(hidden)
            slopes.append(slope)
    with jax.named_scope("slope_exchange"):
        from_down = [shift(slope, 1) for slope in slopes]
        from_up = [shift(slope, -1) for slope in slopes]
        from_far = [shift(from_down[0], 1), shift(from_up[1], -1)]
        from_down, from_up, from_far = [jnp.concatenate(v) for v in (from_down, from_up, from_far)]

    def grad_w(slope_part):
        return lax.dot_general(both, slope_part, TN, preferred_element_type=F32).astype(BF)

    def swap(value):
        return lax.ppermute(value, "wide", [(i, i ^ 1) for i in range(peers)])

    def between_chips(value):
        return lax.all_to_all(
            value,
            "wide",
            split_axis=0,
            concat_axis=0,
            axis_index_groups=[list(range(c, peers, 2)) for c in range(2)],
            tiled=True,
        )

    with jax.named_scope("second_layer"):
        hidden = jnp.concatenate(hiddens)
        seed_hidden = hidden[:seeds]
        second_mean = (
            jnp.dot(counts_second, hidden, preferred_element_type=F32) / second_width
        ).astype(BF)
        grad_v = jnp.concatenate(
            [
                lax.dot_general(seed_hidden, cotangent, TN, preferred_element_type=F32),
                lax.dot_general(second_mean, cotangent, TN, preferred_element_type=F32),
            ]
        ).astype(BF)
        grad_v = jnp.concatenate([grad_v[:, c * share:(c + 1) * share] for c in range(quarters)])
        partial_out = jnp.dot(seed_hidden, v_self, preferred_element_type=F32) + jnp.dot(
            second_mean, v_near, preferred_element_type=F32
        )

        def out_part(d):
            return lax.dynamic_slice_in_dim(partial_out, (z + d) % quarters * share, share, 1)

        outs = [shift(out_part(d).astype(BF), d) for d in range(1, quarters)]
    with jax.named_scope("gradients"):
        near_two = grad_w(jnp.concatenate([from_up, from_down], axis=1))
        chips = peers // 2
        near_two, outs[0] = lax.optimization_barrier((near_two, outs[0]))
        keep, give = pack_shards(
            core.reshape(1), [grad_v, grad_w(jnp.concatenate(slopes)), near_two], chips, share
        )
        keep_far, give_far = pack_shards(core.reshape(1), [grad_w(from_far)], chips, share)
        sums = between_chips(joined(keep, swap(give), keep_far, swap(give_far)))
        mine = between_chips(sum_and_spread(sums))
        mine, *outs = lax.optimization_barrier((mine, *outs))
        other = swap(mine)
        seed_out = out_part(0)
        for part in outs:
            seed_out = seed_out + part.astype(F32)
        seed_out = seed_out.astype(BF)
        grads = pl.pallas_call(
            finish_kernel,
            in_specs=[pl.BlockSpec(memory_space=pltpu.SMEM)] + [pl.BlockSpec(memory_space=pltpu.VMEM)] * 2,
            out_specs=[pl.BlockSpec(memory_space=pltpu.VMEM)] * 4,
            out_shape=[jax.ShapeDtypeStruct((feats, hidden_units), F32)] * 2
            + [jax.ShapeDtypeStruct((share, hidden_units), F32)] * 2,
            compiler_params=pltpu.CompilerParams(vmem_limit_bytes=16 << 20),
            name="finish",
        )(jnp.stack([z, core]).astype(jnp.int32), mine, other)
    return (seed_out, *grads)


def solution(mesh):
    placed = (
        P("wide", "blk"),
        P("wide", None),
        P("wide"),
        P("wide", None),
        P("wide", None),
        P("blk", None),
        P("blk", None),
        P("blk"),
        P("blk", None),
        P("blk", None),
        P("wide", None),
    )
    return jax.shard_map(
        body,
        mesh=mesh,
        in_specs=placed,
        out_specs=(
            P("wide", "blk"),
            P("blk", None),
            P("blk", None),
            P("blk", None),
            P("blk", None),
        ),
        check_vma=False,
    )
```

```python
import functools

import jax
import jax.numpy as jnp
from jax import lax
from jax.experimental import pallas as pl
from jax.experimental.pallas import tpu as pltpu
from jax.sharding import PartitionSpec as P

BF = jnp.bfloat16
F32 = jnp.float32
NT = (((1,), (1,)), ((), ()))
TN = (((0,), (0,)), ((), ()))


def iota(shape, axis):
    return lax.broadcasted_iota(jnp.int32, shape, axis)


def one_hot(hit):
    return jnp.where(hit, 1.0, 0.0).astype(BF)


def chunk(index, size):
    return pl.ds(pl.multiple_of(index * size, size), size)


def request_kernel(own_hbm, row_hbm, req_ref, flat_ref, own_ref, row_ref, hot, picked, spots, sems):
    peers, _, cap = req_ref.shape
    lines, width = own_ref.shape
    copies = [
        pltpu.make_async_copy(own_hbm, own_ref, sems.at[0]),
        pltpu.make_async_copy(row_hbm, row_ref, sems.at[1]),
    ]
    for copy in copies:
        copy.start()
    for copy in copies:
        copy.wait()
    names = iota((peers, width), 0)
    for r in range(lines):
        hot[r * peers:(r + 1) * peers, :] = one_hot(own_ref[r:r + 1, :] == names)
    before = one_hot(iota((width, 2 * width), 0) <= iota((width, 2 * width), 1))
    counted = jnp.dot(hot[...], before, preferred_element_type=F32)
    base = jnp.full((peers, width), -1.0, F32)
    slots = iota((cap, width), 0)
    for r in range(lines):
        here = counted[r * peers:(r + 1) * peers]
        hit = own_ref[r:r + 1, :] == names
        slot = jnp.sum(jnp.where(hit, here[:, :width] + base, 0.0), axis=0, keepdims=True)
        slot = slot.astype(jnp.int32)
        base = base + here[:, width:]
        flat_ref[r:r + 1, :] = own_ref[r:r + 1, :] * cap + slot
        cols = slice(r * width, (r + 1) * width)
        row = row_ref[r:r + 1, :]
        upper = jnp.broadcast_to((row >> 6).astype(F32), (peers, width))
        lower = jnp.broadcast_to((row & 63).astype(F32), (peers, width))
        picked[:peers, cols] = jnp.where(hit, upper, 0.0).astype(BF)
        picked[peers:, cols] = jnp.where(hit, lower, 0.0).astype(BF)
        spots[:, cols] = one_hot(slots == slot)
    found = lax.dot_general(picked[...], spots[...], NT, preferred_element_type=F32)
    req_ref[:, 0, :] = (found[:peers] * 64.0 + found[peers:]).astype(jnp.int32)


def request_table(owners, rows, peers, cap):
    lines, width = owners.shape
    return pl.pallas_call(
        request_kernel,
        out_shape=(
            jax.ShapeDtypeStruct((peers, 1, cap), jnp.int32),
            jax.ShapeDtypeStruct(owners.shape, jnp.int32),
        ),
        in_specs=[pl.BlockSpec(memory_space=pltpu.HBM)] * 2,
        scratch_shapes=[
            pltpu.VMEM(owners.shape, jnp.int32),
            pltpu.VMEM(owners.shape, jnp.int32),
            pltpu.VMEM((lines * peers, width), BF),
            pltpu.VMEM((2 * peers, lines * width), BF),
            pltpu.VMEM((cap, lines * width), BF),
            pltpu.SemaphoreType.DMA((2,)),
        ],
        compiler_params=pltpu.CompilerParams(vmem_limit_bytes=62 << 20),
        name="request_table",
    )(owners, rows)


def count_kernel(idx_ref, out_ref):
    groups = idx_ref.shape[0]
    uppers = out_ref.shape[1] // 256
    target = iota((1, 256), 1) >> 4
    rows_upper = iota((uppers * 16, 256), 0)
    rows_lower = iota((256, 256), 0)

    def group(g, carry):
        value = idx_ref[pl.ds(g, 1), :]
        code = jnp.where(value >= 0, (value >> 8) * 16 + target, -1)
        found = lax.dot_general(
            one_hot(rows_upper == code),
            one_hot(rows_lower == (value & 255)),
            NT,
            preferred_element_type=F32,
        ).astype(BF)
        for u in range(uppers):
            out_ref[chunk(g, 16), u * 256:(u + 1) * 256] = found[u * 16:(u + 1) * 16, :]
        return carry

    lax.fori_loop(0, groups, group, 0, unroll=4)


def neighbour_counts(lists, sources, block_groups=16):
    targets, places = lists.shape
    padded = jnp.pad(lists, ((0, 0), (0, 16 - places)), constant_values=-1)
    return pl.pallas_call(
        count_kernel,
        grid=(targets // 16 // block_groups,),
        in_specs=[pl.BlockSpec((block_groups, 256), lambda i: (i, 0))],
        out_specs=pl.BlockSpec((block_groups * 16, sources), lambda i: (i, 0)),
        out_shape=jax.ShapeDtypeStruct((targets, sources), BF),
        compiler_params=pltpu.CompilerParams(vmem_limit_bytes=40 << 20),
        cost_estimate=pl.CostEstimate(
            flops=512 * targets * sources,
            bytes_accessed=2 * targets * sources,
            transcendentals=0,
        ),
        name="neighbour_counts",
    )(padded.reshape(targets // 16, 256))


def pick_rows(idx_ref, first, count, low, high, out_ref):
    half = low.shape[1]
    line = iota((8, half), 0)

    def some(i, carry):
        begin = pl.multiple_of(i * 16, 16)
        lows, highs = [], []
        for h in range(2):
            for j in range(8):
                row = idx_ref[first + begin + h * 8 + j]
                new_low = jnp.broadcast_to(low[pl.ds(row, 1), :], (8, half))
                new_high = jnp.broadcast_to(high[pl.ds(row, 1), :], (8, half))
                if j == 0:
                    got_low, got_high = new_low, new_high
                else:
                    got_low = jnp.where(line == j, new_low, got_low)
                    got_high = jnp.where(line == j, new_high, got_high)
            lows.append(got_low)
            highs.append(got_high)
        out_ref[pl.ds(begin, 16), :half] = jnp.concatenate(lows, axis=0).astype(BF)
        out_ref[pl.ds(begin, 16), half:] = jnp.concatenate(highs, axis=0).astype(BF)
        return carry

    lax.fori_loop(0, count // 16, some, 0, unroll=16)


def piece_copies(source_ref, held, sems):
    rows = held.shape[0] // sems.shape[0]
    return [
        pltpu.make_async_copy(
            source_ref.at[pl.ds(p * rows, rows), :], held.at[pl.ds(p * rows, rows), :], sems.at[p]
        )
        for p in range(sems.shape[0])
    ]


def widen(held, low, high, copies):
    pieces = max(1, len(copies))
    rows = held.shape[0] // pieces
    half = low.shape[1]
    for p in range(pieces):
        if copies:
            copies[p].wait()

        def some(i, carry):
            part = pl.ds(pl.multiple_of(p * rows + i * 128, 128), 128)
            low[part, :] = held[part, :half].astype(F32)
            high[part, :] = held[part, half:].astype(F32)
            return carry

        lax.fori_loop(0, rows // 128, some, 0, unroll=2)


def gather_kernel(idx_hbm, table_ref, out_ref, idx_ref, held, low, high, sems, idx_sem):
    step = pl.program_id(0)
    rows = out_ref.shape[0]

    @pl.when(step == 0)
    def _():
        copies = piece_copies(table_ref, held, sems)
        idx_copy = pltpu.make_async_copy(idx_hbm, idx_ref, idx_sem)
        for copy in [idx_copy] + copies:
            copy.start()
        widen(held, low, high, copies)
        idx_copy.wait()

    pick_rows(idx_ref, step * rows, rows, low, high, out_ref)


def gather_rows(table, idx, rows=2048):
    total = idx.shape[0]
    own_rows, width = table.shape
    return pl.pallas_call(
        gather_kernel,
        grid=(total // rows,),
        in_specs=[pl.BlockSpec(memory_space=pltpu.HBM)] * 2,
        out_specs=pl.BlockSpec((rows, width), lambda i: (i, 0)),
        scratch_shapes=[
            pltpu.SMEM((total,), jnp.int32),
            pltpu.VMEM((own_rows, width), BF),
            pltpu.VMEM((own_rows, width // 2), F32),
            pltpu.VMEM((own_rows, width // 2), F32),
            pltpu.SemaphoreType.DMA((8,)),
            pltpu.SemaphoreType.DMA,
        ],
        out_shape=pltpu.HBM((total, width), BF),
        compiler_params=pltpu.CompilerParams(vmem_limit_bytes=62 << 20),
        name="gather_rows",
    )(idx, table)


def layer_kernel(list_width, idx_ref, spot_ref, arrived_ref, counts_ref, ws_ref, wn_ref,
                 *refs):
    part_refs, (both_ref, low, high, frontier, counts, count_sems) = refs[:-6], refs[-6:]
    step = pl.program_id(0)
    block = both_ref.shape[0]
    width = arrived_ref.shape[1]

    def count_copy(b):
        return pltpu.make_async_copy(
            counts_ref.at[pl.ds(b * block, block), :],
            counts.at[pl.ds(b * block, block), :],
            count_sems.at[b],
        )

    @pl.when(step == 0)
    def _():
        for b in range(counts.shape[0] // block):
            count_copy(b).start()
        widen(arrived_ref, low, high, [])
        pick_rows(idx_ref, 0, frontier.shape[0], low, high, frontier)

    count_copy(step).wait()
    here = chunk(step, block)
    total = jnp.dot(counts[here, :], frontier[...], preferred_element_type=F32)
    own = frontier[here, :]
    mean = (total / list_width).astype(BF)
    both_ref[:, :width] = own
    both_ref[:, width:] = mean
    share = part_refs[0].shape[1]
    quarters = ws_ref.shape[1] // share
    made = jnp.dot(own, ws_ref[...], preferred_element_type=F32)
    made = (made + jnp.dot(mean, wn_ref[...], preferred_element_type=F32)).astype(BF)
    for q in range(quarters):
        d = lax.rem(q + quarters - spot_ref[0], quarters)
        for e in range(quarters):
            for half in range(2):
                @pl.when((d == e) & (step // (pl.num_programs(0) // 2) == half))
                def _():
                    part_refs[2 * e + half][...] = made[:, q * share:(q + 1) * share]


def first_layer(idx, spot, arrived, counts, w_self, w_near, list_width, quarters, block=1024):
    targets, positions = counts.shape
    slots, width = arrived.shape
    share = w_self.shape[1] // quarters
    steps = targets // block
    middle = steps // 2

    def full(shape):
        return pl.BlockSpec(shape, lambda i, *s: (0, 0))

    halves = [
        pl.BlockSpec((block, share), lambda i, *s: (jnp.minimum(i, middle - 1), 0)),
        pl.BlockSpec((block, share), lambda i, *s: (jnp.maximum(i - middle, 0), 0)),
    ]
    return pl.pallas_call(
        functools.partial(layer_kernel, list_width),
        grid_spec=pltpu.PrefetchScalarGridSpec(
            num_scalar_prefetch=2,
            grid=(steps,),
            in_specs=[
                pl.BlockSpec(memory_space=pltpu.VMEM),
                pl.BlockSpec(memory_space=pltpu.HBM),
                full(w_self.shape),
                full(w_near.shape),
            ],
            out_specs=halves * quarters + [pl.BlockSpec((block, 2 * width), lambda i, *s: (i, 0))],
            scratch_shapes=[
                pltpu.VMEM((slots, width // 2), F32),
                pltpu.VMEM((slots, width // 2), F32),
                pltpu.VMEM((positions, width), BF),
                pltpu.VMEM((targets, positions), BF),
                pltpu.SemaphoreType.DMA((steps,)),
            ],
        ),
        out_shape=[jax.ShapeDtypeStruct((targets // 2, share), BF)] * 2
        + [pltpu.VMEM((targets // 2, share), BF)] * (2 * quarters - 2)
        + [jax.ShapeDtypeStruct((targets, 2 * width), BF)],
        compiler_params=pltpu.CompilerParams(vmem_limit_bytes=54 << 20),
        name="first_layer",
    )(idx, spot, arrived, counts, w_self, w_near)


def add_kernel(left, right, out_ref):
    out_ref[...] = (left[...].astype(F32) + right[...].astype(F32)).astype(BF)


def added(left, right):
    return pl.pallas_call(
        add_kernel,
        in_specs=[pl.BlockSpec(memory_space=pltpu.VMEM)] * 2,
        out_specs=pl.BlockSpec(memory_space=pltpu.VMEM),
        out_shape=jax.ShapeDtypeStruct(left.shape, BF),
        compiler_params=pltpu.CompilerParams(vmem_limit_bytes=16 << 20),
        name="added",
    )(left, right)


def slope_kernel(base, up, down, d_ref, hidden_ref, slope_ref):
    active = base[...] + up[...].astype(F32) + down[...].astype(F32)
    below = 1.0 + jnp.exp(-active)
    sigmoid = 1.0 / below
    hidden_ref[...] = (active / below).astype(BF)
    slope_ref[...] = (d_ref[...] * (sigmoid * (1.0 + active * (1.0 - sigmoid)))).astype(BF)


def hidden_and_slope(base, up, down, d_hidden, first, block=512):
    rows, share = base.shape
    place = pl.BlockSpec((block, share), lambda i: (i, 0))
    return pl.pallas_call(
        slope_kernel,
        grid=(rows // block,),
        in_specs=[place] * 3
        + [
            pl.BlockSpec((block, share), lambda i: (i + first // block, 0)),
        ],
        out_specs=[place, place],
        out_shape=[jax.ShapeDtypeStruct((rows, share), BF)] * 2,
        compiler_params=pltpu.CompilerParams(vmem_limit_bytes=16 << 20),
        name="hidden_and_slope",
    )(base, up, down, d_hidden)


def pack_kernel(core_ref, *refs):
    *value_refs, keep_ref, give_ref = refs
    chips, _, share = keep_ref.shape
    first = 0
    for ref in value_refs:
        rows = ref.shape[0] // (2 * chips)
        for c in range(ref.shape[1] // share):
            cols = slice(c * share, (c + 1) * share)
            for out_ref, core in ((keep_ref, core_ref[0]), (give_ref, 1 - core_ref[0])):
                block = ref[chunk(core, chips * rows), cols]
                out_ref[:, first:first + rows, :] = block.reshape(chips, rows, share)
            first += rows


def pack_shards(core, values, chips, share):
    rows = sum(v.size for v in values) // (2 * chips * share)
    return pl.pallas_call(
        pack_kernel,
        in_specs=[pl.BlockSpec(memory_space=pltpu.SMEM)]
        + [pl.BlockSpec(memory_space=pltpu.VMEM)] * len(values),
        out_specs=[pl.BlockSpec(memory_space=pltpu.VMEM)] * 2,
        out_shape=[jax.ShapeDtypeStruct((chips, rows, share), BF)] * 2,
        compiler_params=pltpu.CompilerParams(vmem_limit_bytes=16 << 20),
        name="pack_shards",
    )(core, *values)


def finish_kernel(spot_ref, mine_ref, other_ref, ws_ref, wn_ref, vs_ref, vn_ref):
    peers, shard, share = mine_ref.shape
    feats = ws_ref.shape[0]
    some = feats // peers
    order = (0, 1, 3, 2)
    v_rows = shard - some * len(order)
    front = spot_ref[1] == 0

    def halves(first, count):
        part = slice(first, first + count)
        mine = mine_ref[:, part, :].astype(F32).reshape(peers * count, share)
        other = other_ref[:, part, :].astype(F32).reshape(peers * count, share)
        return jnp.where(front, mine, other), jnp.where(front, other, mine)

    for place, d in enumerate(order):
        cols = chunk(lax.rem(spot_ref[0] + d, len(order)), share)
        ws_ref[:, cols], wn_ref[:, cols] = halves(v_rows + place * some, some)
    for half, block in enumerate(halves(0, v_rows)):
        for e in range(len(order) // 2):
            cols = slice((2 * half + e) * share, (2 * half + e + 1) * share)
            vs_ref[:, cols] = block[2 * e * share:(2 * e + 1) * share]
            vn_ref[:, cols] = block[(2 * e + 1) * share:(2 * e + 2) * share]


def join_kernel(keep, got, keep_far, got_far, out_ref):
    rows = keep.shape[1]
    out_ref[:, :rows, :] = (keep[...].astype(F32) + got[...].astype(F32)).astype(BF)
    out_ref[:, rows:, :] = (keep_far[...].astype(F32) + got_far[...].astype(F32)).astype(BF)


def joined(keep, got, keep_far, got_far):
    chips, rows, share = keep.shape
    return pl.pallas_call(
        join_kernel,
        in_specs=[pl.BlockSpec(memory_space=pltpu.VMEM)] * 4,
        out_specs=pl.BlockSpec(memory_space=pltpu.VMEM),
        out_shape=jax.ShapeDtypeStruct((chips, rows + keep_far.shape[1], share), BF),
        compiler_params=pltpu.CompilerParams(vmem_limit_bytes=16 << 20),
        name="joined",
    )(keep, got, keep_far, got_far)


def spread_kernel(got_ref, out_ref):
    total = jnp.sum(got_ref[...].astype(F32), axis=0).astype(BF)
    for chip in range(out_ref.shape[0]):
        out_ref[chip] = total


def sum_and_spread(got):
    return pl.pallas_call(
        spread_kernel,
        in_specs=[pl.BlockSpec(memory_space=pltpu.VMEM)],
        out_specs=pl.BlockSpec(memory_space=pltpu.VMEM),
        out_shape=jax.ShapeDtypeStruct(got.shape, BF),
        compiler_params=pltpu.CompilerParams(vmem_limit_bytes=16 << 20),
        name="sum_and_spread",
    )(got)


def body(
    feature_table,
    owner_ids,
    row_ids,
    near_first,
    near_second,
    w_self,
    w_near,
    bias_hidden,
    v_self,
    v_near,
    cotangent,
):
    peers = lax.axis_size("wide")
    quarters = lax.axis_size("blk")
    z = lax.axis_index("blk")
    core = lax.axis_index("wide") % 2
    frontier_count = row_ids.shape[0]
    cap = 2 * frontier_count // peers
    targets, first_width = near_first.shape
    seeds, second_width = near_second.shape
    feats, hidden_units = w_self.shape
    share = hidden_units // quarters

    def shift(value, by):
        return lax.ppermute(value, "blk", [(i, (i + by) % quarters) for i in range(quarters)])

    def exchange(value):
        return lax.all_to_all(value, "wide", split_axis=0, concat_axis=0, tiled=True)

    with jax.named_scope("requests"):
        requests, flat = request_table(
            owner_ids.reshape(frontier_count // 128, 128),
            row_ids.reshape(frontier_count // 128, 128),
            peers,
            cap,
        )
        wanted = exchange(requests).reshape(-1)
        flat = flat.reshape(-1)
    with jax.named_scope("rows"):
        found = gather_rows(feature_table, wanted)
        arrived = exchange(found.reshape(peers, cap, feats)).reshape(peers * cap, feats)
    with jax.named_scope("beside_rows"):
        counts_first = neighbour_counts(near_first, frontier_count)
        counts_second = neighbour_counts(near_second, targets)
        d_self = lax.dot_general(cotangent, v_self, NT, preferred_element_type=F32)
        d_mean = lax.dot_general(cotangent, v_near, NT, preferred_element_type=F32) / second_width
        d_upper = d_mean.astype(BF)
        d_lower = (d_mean - d_upper.astype(F32)).astype(BF)
        spread = lax.dot_general(
            counts_second,
            jnp.concatenate([d_upper, d_lower], axis=1),
            TN,
            preferred_element_type=F32,
        )
        d_hidden = spread[:, :share] + spread[:, share:]
        d_hidden = d_hidden + jnp.pad(d_self, ((0, targets - seeds), (0, 0)))
        arrived, counts_first, counts_second, d_hidden = lax.optimization_barrier(
            (arrived, counts_first, counts_second, d_hidden)
        )
    with jax.named_scope("first_layer"):
        *parts, both = first_layer(
            flat,
            jnp.full((1,), z, jnp.int32),
            arrived,
            counts_first,
            w_self,
            w_near,
            first_width,
            quarters,
        )
    with jax.named_scope("pre_act_exchange"):
        own, above, far, below = [parts[2 * d:2 * d + 2] for d in range(quarters)]
        passing_up = shift(far[0], 1)
        passing_down = shift(far[1], -1)
        down_0 = shift(below[0], -1)
        first = added(above[0], passing_up)
        up_0 = shift(first, 1)
        passing_down, _ = lax.optimization_barrier((passing_down, first))
        second, after = lax.optimization_barrier((added(below[1], passing_down), above[1]))
        down_1 = shift(second, -1)
        up_1 = shift(after, 1)
        hiddens, slopes = [], []
        for half, (up, down) in enumerate([(up_0, down_0), (up_1, down_1)]):
            base = own[half].astype(F32) + bias_hidden.astype(F32)
            if half:
                base, _ = lax.optimization_barrier((base, slopes[0]))
            hidden, slope = hidden_and_slope(base, up, down, d_hidden, half * targets // 2)
            hiddens.append(hidden)
            slopes.append(slope)
    with jax.named_scope("slope_exchange"):
        from_down = [shift(slope, 1) for slope in slopes]
        from_up = [shift(slope, -1) for slope in slopes]
        from_far = [shift(from_down[0], 1), shift(from_up[1], -1)]
        from_down, from_up, from_far = [jnp.concatenate(v) for v in (from_down, from_up, from_far)]

    def grad_w(slope_part):
        return lax.dot_general(both, slope_part, TN, preferred_element_type=F32).astype(BF)

    def swap(value):
        return lax.ppermute(value, "wide", [(i, i ^ 1) for i in range(peers)])

    def between_chips(value):
        return lax.all_to_all(
            value,
            "wide",
            split_axis=0,
            concat_axis=0,
            axis_index_groups=[list(range(c, peers, 2)) for c in range(2)],
            tiled=True,
        )

    with jax.named_scope("second_layer"):
        hidden = jnp.concatenate(hiddens)
        seed_hidden = hidden[:seeds]
        second_mean = (
            jnp.dot(counts_second, hidden, preferred_element_type=F32) / second_width
        ).astype(BF)
        grad_v = jnp.concatenate(
            [
                lax.dot_general(seed_hidden, cotangent, TN, preferred_element_type=F32),
                lax.dot_general(second_mean, cotangent, TN, preferred_element_type=F32),
            ]
        ).astype(BF)
        grad_v = jnp.concatenate([grad_v[:, c * share:(c + 1) * share] for c in range(quarters)])
        partial_out = jnp.dot(seed_hidden, v_self, preferred_element_type=F32) + jnp.dot(
            second_mean, v_near, preferred_element_type=F32
        )

        def out_part(d):
            return lax.dynamic_slice_in_dim(partial_out, (z + d) % quarters * share, share, 1)

        outs = [shift(out_part(d).astype(BF), d) for d in range(1, quarters)]
    with jax.named_scope("gradients"):
        near_two = grad_w(jnp.concatenate([from_up, from_down], axis=1))
        chips = peers // 2
        near_two, outs[0] = lax.optimization_barrier((near_two, outs[0]))
        keep, give = pack_shards(
            core.reshape(1), [grad_v, grad_w(jnp.concatenate(slopes)), near_two], chips, share
        )
        keep_far, give_far = pack_shards(core.reshape(1), [grad_w(from_far)], chips, share)
        sums = between_chips(joined(keep, swap(give), keep_far, swap(give_far)))
        mine = between_chips(sum_and_spread(sums))
        mine, *outs = lax.optimization_barrier((mine, *outs))
        other = swap(mine)
        seed_out = out_part(0)
        for part in outs:
            seed_out = seed_out + part.astype(F32)
        seed_out = seed_out.astype(BF)
        grads = pl.pallas_call(
            finish_kernel,
            in_specs=[pl.BlockSpec(memory_space=pltpu.SMEM)] + [pl.BlockSpec(memory_space=pltpu.VMEM)] * 2,
            out_specs=[pl.BlockSpec(memory_space=pltpu.VMEM)] * 4,
            out_shape=[jax.ShapeDtypeStruct((feats, hidden_units), F32)] * 2
            + [jax.ShapeDtypeStruct((share, hidden_units), F32)] * 2,
            compiler_params=pltpu.CompilerParams(vmem_limit_bytes=16 << 20),
            name="finish",
        )(jnp.stack([z, core]).astype(jnp.int32), mine, other)
    return (seed_out, *grads)


def solution(mesh):
    placed = (
        P("wide", "blk"),
        P("wide", None),
        P("wide"),
        P("wide", None),
        P("wide", None),
        P("blk", None),
        P("blk", None),
        P("blk"),
        P("blk", None),
        P("blk", None),
        P("wide", None),
    )
    return jax.shard_map(
        body,
        mesh=mesh,
        in_specs=placed,
        out_specs=(
            P("wide", "blk"),
            P("blk", None),
            P("blk", None),
            P("blk", None),
            P("blk", None),
        ),
        check_vma=False,
    )
```
